256 devices in a mesh: patch: 128 (over x, y, z), feat: 2 (over core).
Axes of the slice: x: 4, y: 4, z: 8, core: 2. Of those that a mesh axis runs over, the one named last changes fastest.
Arguments:
- node_feats: bfloat16 [81920, 512], P('patch', 'feat'), may hold values from -6 to 6
- cotangent: bfloat16 [81920, 512], P('patch', 'feat'), may hold values from -6 to 6
- send_weight: bfloat16 [512, 512], P(None, 'feat'), may hold values from -0.25 to 0.25
- recv_weight: bfloat16 [512, 512], P(None, 'feat'), may hold values from -0.25 to 0.25
- out_weight: bfloat16 [512, 512], P('feat'), may hold values from -0.125 to 0.125
- edge_bias: float32 [512], P('feat'), may hold values from -1 to 1
- sender: int32 [1048576], P('patch'), may hold values from 0 to 2943, as said below
- receiver: int32 [1048576], P('patch'), may hold values from 0 to 640, as said below
- wanted: int32 [128, 128, 16], P('patch'), may hold values from 0 to 79
Outputs:
- updated: bfloat16 [81920, 512], P('patch', 'feat')
- grad_nodes: bfloat16 [81920, 512], P('patch', 'feat')
- grad_send: float32 [512, 512], P(None, 'feat')
- grad_recv: float32 [512, 512], P(None, 'feat')
- grad_out: float32 [512, 512], P('feat')
- grad_bias: float32 [512], P('feat')
The draws below stay inside these ranges and needn't reach their ends.
Inputs may be any that keep to these rules, and one draw needn't show every extreme that they name: `sender`: values below 896 name rows of the own and neighbouring patches, larger ones a listed coarse node; every patch has a slot with 0 and one with the largest value. `receiver`: 640 marks an empty slot; empty slots stand after the live ones; one patch has all 8192 slots live, every other patch at least three quarters of them.
All inputs are finite; a program needn't handle non-finite values.
Results may differ from the reference program's by a relative error of at most 0.006.
Values may be sent and summed in bfloat16 or wider, within the bound.
A program may use at most 128 MiB of HBM per device.

```python
import jax
import jax.numpy as jnp
from jax import lax

D = 512
NODE_DEV = 640
EDGE_DEV = 8192
HALO = 128
COARSE_DEV = 80
QUOTA = 16
NODES = 81920
FAR_SLOTS = 2048
N_PATCH = 128


def draw_sender(key, part):
    key = jax.random.fold_in(key, 11)
    first_key, second_key, third_key = jax.random.split(key, 3)
    local_span = NODE_DEV + 2 * HALO
    near_rows = jax.random.randint(first_key, (N_PATCH, EDGE_DEV), 0, local_span)
    far_rows = local_span + jax.random.randint(second_key, (N_PATCH, EDGE_DEV), 0, FAR_SLOTS)
    pick_far = jax.random.randint(third_key, (N_PATCH, EDGE_DEV), 0, 4) == 0
    result = jnp.where(pick_far, far_rows, near_rows)
    result = result.at[:, 0].set(0).at[:, EDGE_DEV - 1].set(local_span + FAR_SLOTS - 1)
    return result.reshape(-1).astype(jnp.int32)


def draw_receiver(key, part):
    key = jax.random.fold_in(key, 23)
    first_key, second_key, third_key = jax.random.split(key, 3)
    live_count = jax.random.randint(first_key, (N_PATCH,), 3 * EDGE_DEV // 4, EDGE_DEV)
    fullest = jax.random.randint(second_key, (), 0, N_PATCH)
    live_count = jnp.where(jnp.arange(N_PATCH) == fullest, EDGE_DEV, live_count)
    targets = jax.random.randint(third_key, (N_PATCH, EDGE_DEV), 0, NODE_DEV)
    slot_ids = jnp.arange(EDGE_DEV)
    result = jnp.where(slot_ids[None, :] < live_count[:, None], targets, NODE_DEV)
    result = result.at[:, 0].set(0)
    return result.reshape(-1).astype(jnp.int32)


def set_ends(array, key, least, top_value):
    longest = array.shape.index(max(array.shape))
    spots = []
    for shift in (0, 1):
        where = [jax.random.randint(jax.random.fold_in(key, axis), (), 0, length) for axis, length in enumerate(array.shape)]
        where[longest] = (where[longest] + shift) % array.shape[longest]
        spots.append(tuple(where))
    return array.at[spots[0]].set(least).at[spots[1]].set(top_value)


def level_of(own_key, extent, pieces, low, high):
    def one(axis_at, shards_of):
        steps = jax.random.uniform(jax.random.fold_in(jax.random.fold_in(own_key, 6), axis_at), (shards_of,), jnp.float32, low / len(pieces), high / len(pieces))
        return jnp.repeat(jnp.exp(steps), extent[axis_at] // shards_of).reshape((-1,) + (1,) * (len(extent) - axis_at - 1))

    loudness = one(*pieces[0])
    for cut in pieces[1:]:
        loudness = loudness * one(*cut)
    return loudness


def centred(rng, extent, spread, most, shards=(), held_as=jnp.bfloat16):
    entries = spread * jax.random.normal(rng, extent, jnp.float32)
    if shards:
        entries = entries * level_of(rng, extent, shards, -0.22, 0.18)
    return jnp.clip(entries, -most, most).astype(held_as)


def setup_inputs(seed: int = 0) -> dict:
    seeds = jax.random.split(jax.random.key(seed), 10)
    node_feats = centred(seeds[0], (NODES, D), 1.0, 6.0, ((0, 128), (1, 2)))
    cotangent = centred(seeds[1], (NODES, D), 1.0, 6.0, ((0, 128), (1, 2)))
    send_weight = centred(seeds[2], (D, D), D ** -0.5, 0.25, ((1, 2),))
    recv_weight = centred(seeds[3], (D, D), D ** -0.5, 0.25, ((1, 2),))
    out_weight = centred(seeds[4], (D, D), (4 * D) ** -0.5, 0.125, ((0, 2),))
    edge_bias = jnp.clip(jax.random.uniform(seeds[5], (D,), jnp.float32, -1.0, 1.0) * level_of(seeds[5], (D,), ((0, 2),), -0.4, 0.0), -1.0, 1.0)
    sender = draw_sender(jax.random.fold_in(seeds[9], 71), 0)
    receiver = draw_receiver(jax.random.fold_in(seeds[9], 71), 0)
    wanted = set_ends(jax.random.randint(seeds[8], (N_PATCH, N_PATCH, QUOTA), 0, COARSE_DEV), jax.random.fold_in(seeds[8], 1), 0, COARSE_DEV - 1).astype(jnp.int32)
    return {"node_feats": node_feats, "cotangent": cotangent, "send_weight": send_weight, "recv_weight": recv_weight, "out_weight": out_weight, "edge_bias": edge_bias, "sender": sender, "receiver": receiver, "wanted": wanted}


def source_nodes(sender, wanted):
    device_ids = jnp.arange(N_PATCH, dtype=jnp.int32)[:, None]
    values = sender.reshape(N_PATCH, EDGE_DEV)
    low_node = ((device_ids - 1) % N_PATCH) * NODE_DEV + NODE_DEV - HALO + values
    own_node = device_ids * NODE_DEV + values - HALO
    high_node = ((device_ids + 1) % N_PATCH) * NODE_DEV + values - NODE_DEV - HALO
    far_index = jnp.clip(values - NODE_DEV - 2 * HALO, 0, FAR_SLOTS - 1).astype(jnp.int32)
    listed = jnp.take_along_axis(wanted.reshape(N_PATCH, FAR_SLOTS), far_index, axis=1)
    far_node = (far_index // QUOTA) * NODE_DEV + listed
    result = jnp.where(values < HALO, low_node,
             jnp.where(values < HALO + NODE_DEV, own_node,
             jnp.where(values < NODE_DEV + 2 * HALO, high_node, far_node)))
    return result.astype(jnp.int32)


def reference(node_feats, cotangent, send_weight, recv_weight, out_weight, edge_bias, sender, receiver, wanted):
    proj_send = jnp.dot(node_feats, send_weight, preferred_element_type=jnp.float32).astype(jnp.bfloat16)
    proj_recv = jnp.dot(node_feats, recv_weight, preferred_element_type=jnp.float32)
    sources = source_nodes(sender, wanted)
    targets = receiver.reshape(N_PATCH, EDGE_DEV)
    recv_blocks = jnp.concatenate([proj_recv.reshape(N_PATCH, NODE_DEV, D), jnp.zeros((N_PATCH, 1, D), jnp.float32)], axis=1)

    def pre_of(device):
        return (jnp.take(proj_send, sources[device], axis=0).astype(jnp.float32)
                + jnp.take(recv_blocks[device], targets[device], axis=0) + edge_bias)

    def forward_one(device):
        hidden = jax.nn.silu(pre_of(device))
        return jax.ops.segment_sum(hidden, targets[device], num_segments=NODE_DEV + 1)[:NODE_DEV]

    edge_sum = lax.map(forward_one, jnp.arange(N_PATCH, dtype=jnp.int32)).reshape(NODES, D).astype(jnp.bfloat16)
    updated = (node_feats.astype(jnp.float32) + jnp.dot(edge_sum, out_weight, preferred_element_type=jnp.float32)).astype(jnp.bfloat16)
    grad_out = jnp.dot(edge_sum.T, cotangent, preferred_element_type=jnp.float32)
    grad_sum = jnp.dot(cotangent, out_weight.T, preferred_element_type=jnp.float32)
    grad_blocks = jnp.concatenate([grad_sum.reshape(N_PATCH, NODE_DEV, D), jnp.zeros((N_PATCH, 1, D), jnp.float32)], axis=1)

    def backward_one(carry, device):
        send_total, bias_total = carry
        pre_act = pre_of(device)
        sigmoid_act = jax.nn.sigmoid(pre_act)
        grad_pre = jnp.take(grad_blocks[device], targets[device], axis=0) * sigmoid_act * (1.0 + pre_act * (1.0 - sigmoid_act))
        recv_part = jax.ops.segment_sum(grad_pre, targets[device], num_segments=NODE_DEV + 1)[:NODE_DEV]
        send_total = send_total.at[sources[device]].add(grad_pre)
        return (send_total, bias_total + jnp.sum(grad_pre, axis=0)), recv_part

    start = (jnp.zeros((NODES, D), jnp.float32), jnp.zeros((D,), jnp.float32))
    (dsend_full, grad_bias), drecv_parts = lax.scan(backward_one, start, jnp.arange(N_PATCH, dtype=jnp.int32))
    dsend = dsend_full.astype(jnp.bfloat16)
    drecv = drecv_parts.reshape(NODES, D).astype(jnp.bfloat16)
    grad_send = jnp.dot(node_feats.T, dsend, preferred_element_type=jnp.float32)
    grad_recv = jnp.dot(node_feats.T, drecv, preferred_element_type=jnp.float32)
    back_terms = jnp.dot(dsend, send_weight.T, preferred_element_type=jnp.float32) + jnp.dot(drecv, recv_weight.T, preferred_element_type=jnp.float32)
    grad_nodes = (cotangent.astype(jnp.float32) + back_terms).astype(jnp.bfloat16)
    return (updated, grad_nodes, grad_send, grad_recv, grad_out, grad_bias)
```

```python
import functools

import jax
import jax.numpy as jnp
from jax import lax
from jax.experimental import pallas as pl
from jax.experimental.pallas import tpu as pltpu
from jax.sharding import PartitionSpec as P

HALO = 128
COARSE = 80
QUOTA = 16
ROWS = 640
HALF = 256
EDGES = 8192
NEAR = ROWS + 2 * HALO
BLOCK = 256
TILE = 256
MESH = pl.DeviceIdType.MESH
F32 = jnp.float32
BF16 = jnp.bfloat16
I32 = jnp.int32
NN = (((1,), (0,)), ((), ()))
TN = (((0,), (0,)), ((), ()))
NT = (((1,), (1,)), ((), ()))


def mm(a, b, dims=NN):
    return lax.dot_general(a, b, dims, preferred_element_type=F32)


def place(n_patch, ring):
    me = lax.axis_index("patch")
    feat = lax.axis_index("feat")
    return me, lax.div(me, ring), lax.rem(me, ring), feat


def meet(n_patch, ring):
    planes = n_patch // ring
    me, xy, z, feat = place(n_patch, ring)
    barrier = pltpu.get_barrier_semaphore()

    def greet(patch, core):
        pl.semaphore_signal(barrier, inc=1, device_id=(patch, core), device_id_type=MESH)

    def greet_plane(d, carry):
        greet(lax.rem(xy + d, planes) * ring + z, feat)
        return carry

    def greet_ring(d, carry):
        greet(xy * ring + lax.rem(z + d, ring), feat)
        return carry

    lax.fori_loop(1, planes, greet_plane, 0)
    lax.fori_loop(1, ring, greet_ring, 0)
    greet(lax.rem(me + 1, n_patch), feat)
    greet(lax.rem(me + n_patch - 1, n_patch), feat)
    greet(me, 1 - feat)
    pl.semaphore_wait(barrier, planes - 1 + ring - 1 + 3)


def remote(src, dst, send, recv, patch, core):
    return pltpu.make_async_remote_copy(
        src_ref=src, dst_ref=dst, send_sem=send, recv_sem=recv,
        device_id=(patch, core), device_id_type=MESH,
    )


def loop(low, high, body):
    def step(i, carry):
        body(i)
        return carry

    lax.fori_loop(low, high, step, 0)


def forward_kernel(
    n_patch, ring,
    feats, cot, lists,
    table, cots, asked,
    coarse, packed,
    zs_s, zs_r, ls_s, ls_r, ps_s, ps_r, fs_s, fs_r, hs_s, hs_r, os_s, os_r, loc,
):
    planes = n_patch // ring
    per = ring * QUOTA
    me, xy, z, feat = place(n_patch, ring)
    up = lax.rem(me + 1, n_patch)
    down = lax.rem(me + n_patch - 1, n_patch)
    other = 1 - feat
    meet(n_patch, ring)

    def ring_peer(d):
        return lax.rem(z + d, ring)

    def plane_peer(d):
        return lax.rem(xy + d, planes)

    def plane_from(d):
        return lax.rem(xy + planes - d, planes)

    def ring_from(d):
        return lax.rem(z + ring - d, ring)

    def coarse_copy(d):
        return remote(feats.at[0:COARSE], coarse.at[z, 0:COARSE], zs_s.at[d], zs_r.at[d], xy * ring + ring_peer(d), feat)

    def list_copy(d):
        to = plane_peer(d)
        return remote(
            lists.at[pl.ds(to * QUOTA, QUOTA)], asked.at[pl.ds(xy * QUOTA, QUOTA)],
            ls_s.at[d], ls_r.at[d], to * ring + z, feat,
        )

    def far_rows(p):
        return table.at[feat, pl.ds(NEAR + p * per, per)]

    def plane_copy(d):
        to = plane_peer(d)
        return remote(packed.at[to], far_rows(xy), ps_s.at[d], ps_r.at[d], to * ring + z, feat)

    loop(1, ring, lambda d: coarse_copy(d).start())
    loop(1, planes, lambda d: list_copy(d).start())
    own_list = pltpu.make_async_copy(lists.at[pl.ds(xy * QUOTA, QUOTA)], asked.at[pl.ds(xy * QUOTA, QUOTA)], loc.at[0])
    own_list.start()
    own_coarse = pltpu.make_async_copy(feats.at[0:COARSE], coarse.at[z, 0:COARSE], loc.at[1])
    own_coarse.start()
    low_rim = table.at[feat, 0:HALO]
    high_rim = table.at[feat, HALO + ROWS : NEAR]
    to_up = remote(feats.at[ROWS - HALO : ROWS], low_rim, hs_s.at[0], hs_r.at[0], up, feat)
    to_down = remote(feats.at[0:HALO], high_rim, hs_s.at[1], hs_r.at[1], down, feat)
    to_up.start()
    to_down.start()
    own_rows = table.at[feat, HALO : HALO + ROWS]
    swap_own = remote(feats, own_rows, os_s.at[0], os_r.at[0], me, other)
    swap_cot = remote(cot, cots.at[feat], os_s.at[1], os_r.at[1], me, other)
    swap_own.start()
    swap_cot.start()
    keep_own = pltpu.make_async_copy(feats, own_rows, loc.at[2])
    keep_cot = pltpu.make_async_copy(cot, cots.at[feat], loc.at[3])
    keep_own.start()
    keep_cot.start()

    for k in range(ring):
        coarse[k, COARSE:HALO] = jnp.zeros((HALO - COARSE, HALF), BF16)

    own_list.wait()
    own_coarse.wait()

    def wait_list(d):
        at = asked.at[pl.ds(plane_from(d) * QUOTA, QUOTA)]
        remote(at, at, ls_s.at[d], ls_r.at[d], me, other).wait_recv()

    def wait_coarse(d):
        at = coarse.at[ring_from(d), 0:COARSE]
        remote(at, at, zs_s.at[d], zs_r.at[d], me, other).wait_recv()

    loop(1, planes, wait_list)
    loop(1, ring, wait_coarse)
    lane = lax.broadcasted_iota(I32, (planes * QUOTA, HALO), 1)
    for k in range(ring):
        pick = jnp.where(asked[:, k : k + 1] == lane, 1.0, 0.0).astype(BF16)
        rows = mm(pick, coarse[k]).astype(BF16)
        packed[:, k * QUOTA : (k + 1) * QUOTA, :] = rows.reshape(planes, QUOTA, HALF)
    loop(1, planes, lambda d: plane_copy(d).start())
    own_far = pltpu.make_async_copy(packed.at[xy], far_rows(xy), loc.at[4])
    own_far.start()
    swap_far = remote(packed.at[xy], far_rows(xy), fs_s.at[0], fs_r.at[0], me, other)
    swap_far.start()

    def pass_on(p, slot):
        at = far_rows(p)
        return remote(at, at, fs_s.at[slot], fs_r.at[slot], me, other)

    def rim_copy(rim, slot):
        return remote(rim, rim, os_s.at[slot], os_r.at[slot], me, other)

    to_up.wait()
    rim_copy(low_rim, 2).start()
    to_down.wait()
    rim_copy(high_rim, 3).start()

    def forward_one(d):
        at = far_rows(plane_from(d))
        remote(at, at, ps_s.at[d], ps_r.at[d], me, other).wait_recv()
        pass_on(plane_from(d), d).start()

    loop(1, planes, forward_one)

    loop(1, planes, lambda d: list_copy(d).wait_send())
    loop(1, ring, lambda d: coarse_copy(d).wait_send())
    loop(1, planes, lambda d: plane_copy(d).wait_send())
    keep_own.wait()
    keep_cot.wait()
    own_far.wait()
    swap_own.wait()
    swap_cot.wait()
    swap_far.wait()
    rim_copy(low_rim, 2).wait()
    rim_copy(high_rim, 3).wait()
    loop(1, planes, lambda d: pass_on(plane_from(d), d).wait())


def forward_exchange(n_patch, ring, feats, cot, lists):
    planes = n_patch // ring
    table_rows = NEAR + n_patch * QUOTA
    vmem = pl.BlockSpec(memory_space=pltpu.VMEM)
    anyspace = pl.BlockSpec(memory_space=pl.ANY)
    dma = pltpu.SemaphoreType.DMA
    return pl.pallas_call(
        functools.partial(forward_kernel, n_patch, ring),
        out_shape=(
            jax.ShapeDtypeStruct((2, table_rows, HALF), BF16),
            jax.ShapeDtypeStruct((2, ROWS, HALF), BF16),
            jax.ShapeDtypeStruct((planes * QUOTA, HALO), I32),
        ),
        in_specs=[vmem] * 3,
        out_specs=(anyspace, anyspace, vmem),
        scratch_shapes=[
            pltpu.VMEM((ring, HALO, HALF), BF16),
            pltpu.VMEM((planes, ring * QUOTA, HALF), BF16),
            dma((ring,)), dma((ring,)),
            dma((planes,)), dma((planes,)),
            dma((planes,)), dma((planes,)),
            dma((planes,)), dma((planes,)),
            dma((2,)), dma((2,)),
            dma((4,)), dma((4,)),
            dma((5,)),
        ],
        compiler_params=pltpu.CompilerParams(
            collective_id=0, has_side_effects=True, vmem_limit_bytes=32 * 2**20
        ),
        name="forward_exchange",
    )(feats, cot, lists)


def edge_kernel(
    table_rows, chunk_count,
    bounds,
    keys, table, cots, send_w, recv_w, out_w, bias,
    far_out, rim_out, own_out, wire, mix, back,
    send_s, pair_s, gsum, dtab, acc, cols, pre_s, gat_s,
):
    tiles = pl.cdiv(table_rows, TILE)
    padded = tiles * TILE
    own = slice(HALO, HALO + ROWS)

    for start in range(0, table_rows, 736 if table_rows % 736 == 0 else 128):
        size = 736 if table_rows % 736 == 0 else 128
        rows = slice(start, start + size)
        send_s[rows, :] = (
            mm(table[0, rows, :], send_w[0:HALF, :]) + mm(table[1, rows, :], send_w[HALF:, :])
        ).astype(BF16)
    if padded > table_rows:
        send_s[table_rows:padded, :] = jnp.zeros((padded - table_rows, HALF), BF16)
    pair_s[:, 0:HALF] = (
        mm(table[0, own, :], recv_w[0:HALF, :]) + mm(table[1, own, :], recv_w[HALF:, :]) + bias[...]
    ).astype(BF16)
    grad_sum = mm(cots[0], out_w[:, 0:HALF], NT) + mm(cots[1], out_w[:, HALF:], NT)
    gsum[...] = grad_sum
    pair_s[:, HALF:] = grad_sum.astype(BF16)
    dtab[...] = jnp.zeros_like(dtab)
    acc[...] = jnp.zeros_like(acc)

    turned = jnp.transpose(keys[...])
    for r in range(EDGES // 128):
        cols[r] = jnp.broadcast_to(turned[:, r : r + 1], (128, 128))

    lane = lax.broadcasted_iota(I32, (BLOCK, 128), 1)
    sub = lax.broadcasted_iota(I32, (ROWS, 128), 0)
    sub_t = lax.broadcasted_iota(I32, (TILE, 128), 0)

    def hot(mask):
        return jnp.where(mask, 1.0, 0.0).astype(BF16)

    def block(b, carry):
        col = cols[pl.ds(2 * b, 2)].reshape(BLOCK, 128)
        recv_col = jnp.bitwise_and(col, 1023)
        send_col = jnp.right_shift(col, 10)
        pick = jnp.concatenate([hot(recv_col == lane + 128 * j) for j in range(ROWS // 128)], axis=1)
        both = mm(pick, pair_s[...])
        pre_s[...] = both[:, 0:HALF]
        gat_s[...] = both[:, HALF:]
        first = bounds[2 * b]
        last = bounds[2 * b + 1]

        def gather(t, c):
            shifted = send_col - t * TILE
            oh = jnp.concatenate([hot(shifted == lane), hot(shifted == lane + 128)], axis=1)
            pre_s[...] += mm(oh, send_s[pl.ds(pl.multiple_of(t * TILE, TILE), TILE), :])
            return c

        lax.fori_loop(first, last + 1, gather, 0)
        pre = pre_s[...]
        sig = 0.5 * jnp.tanh(0.5 * pre) + 0.5
        hidden = pre * sig
        slope = sig + hidden * (1.0 - sig)
        row = keys[pl.ds(2 * b, 2), :]
        recv_row = jnp.bitwise_and(row, 1023)
        send_row = jnp.right_shift(row, 10)
        spread = jnp.concatenate([hot(sub == recv_row[0:1]), hot(sub == recv_row[1:2])], axis=1)
        acc[...] += mm(spread, jnp.concatenate([hidden, slope], axis=1).astype(BF16))
        grad_pre = (gat_s[...] * slope).astype(BF16)

        def scatter(t, c):
            shifted = send_row - t * TILE
            oh = jnp.concatenate([hot(sub_t == shifted[0:1]), hot(sub_t == shifted[1:2])], axis=1)
            dtab[pl.ds(pl.multiple_of(t * TILE, TILE), TILE), :] += mm(oh, grad_pre)
            return c

        lax.fori_loop(first, last + 1, scatter, 0)
        return carry

    lax.fori_loop(0, EDGES // BLOCK, block, 0)

    edge_sum = acc[:, 0:HALF].astype(BF16)
    mixed = mm(edge_sum, out_w[...])
    mix[0] = mixed[:, 0:HALF]
    mix[1] = mixed[:, HALF:]
    recv_grad = gsum[...] * acc[:, HALF:]
    bias_part = jnp.sum(recv_grad, axis=0, keepdims=True)
    recv_grad_b = recv_grad.astype(BF16)
    back[...] = mm(recv_grad_b, recv_w[...], NT)
    own_out[...] = dtab[own, :]
    far_out[...] = dtab[NEAR:table_rows, :].astype(BF16)
    rim_out[0] = dtab[0:HALO, :].astype(BF16)
    rim_out[1] = dtab[HALO + ROWS : NEAR, :].astype(BF16)

    chunk = 3072 // chunk_count

    def put(start, value):
        at = 0
        while at < value.shape[0]:
            c, r = divmod(start + at, chunk)
            size = min(chunk - r, value.shape[0] - at)
            wire[c, r : r + size, :] = value[at : at + size, :]
            at += size

    def put_weight(start, value):
        value = value.astype(BF16)
        for j in range(value.shape[1] // 128):
            put(start + j * value.shape[0], value[:, j * 128 : (j + 1) * 128])

    dtab_b = dtab[0:table_rows, :].astype(BF16)
    send_grad = jnp.concatenate([mm(table[0], dtab_b, TN), mm(table[1], dtab_b, TN)], axis=0)
    put_weight(0, send_grad)
    recv_w_grad = jnp.concatenate(
        [mm(table[0, own, :], recv_grad_b, TN), mm(table[1, own, :], recv_grad_b, TN)], axis=0
    )
    put_weight(1024, recv_w_grad)
    put_weight(2048, jnp.concatenate([mm(edge_sum, cots[0], TN), mm(edge_sum, cots[1], TN)], axis=1))
    sub16 = lax.broadcasted_iota(I32, (16, 128), 0)
    tail = jnp.where(sub16 == 0, bias_part[:, 0:128], jnp.where(sub16 == 1, bias_part[:, 128:], 0.0)).astype(BF16)
    for c in range(chunk_count):
        wire[c, chunk : chunk + 16, :] = tail


def edge_pass(n_patch, ring, bounds, keys, table, cots, send_w, recv_w, out_w, bias):
    planes = n_patch // ring
    table_rows = NEAR + n_patch * QUOTA
    padded = pl.cdiv(table_rows, TILE) * TILE
    vmem = pl.BlockSpec(memory_space=pltpu.VMEM)
    return pl.pallas_call(
        functools.partial(edge_kernel, table_rows, planes),
        out_shape=(
            jax.ShapeDtypeStruct((n_patch * QUOTA, HALF), BF16),
            jax.ShapeDtypeStruct((2, HALO, HALF), BF16),
            jax.ShapeDtypeStruct((ROWS, HALF), F32),
            jax.ShapeDtypeStruct((planes, 3072 // planes + 16, 128), BF16),
            jax.ShapeDtypeStruct((2, ROWS, HALF), F32),
            jax.ShapeDtypeStruct((ROWS, 2 * HALF), F32),
        ),
        in_specs=[pl.BlockSpec(memory_space=pltpu.SMEM)] + [vmem] * 7,
        out_specs=(vmem,) * 6,
        scratch_shapes=[
            pltpu.VMEM((padded, HALF), BF16),
            pltpu.VMEM((ROWS, 2 * HALF), BF16),
            pltpu.VMEM((ROWS, HALF), F32),
            pltpu.VMEM((padded, HALF), F32),
            pltpu.VMEM((ROWS, 2 * HALF), F32),
            pltpu.VMEM((EDGES // 128, 128, 128), I32),
            pltpu.VMEM((BLOCK, HALF), F32),
            pltpu.VMEM((BLOCK, HALF), F32),
        ],
        compiler_params=pltpu.CompilerParams(vmem_limit_bytes=48 * 2**20),
        name="edge_pass",
    )(bounds, keys, table, cots, send_w, recv_w, out_w, bias)


def backward_kernel(
    n_patch, ring,
    feats, cot, send_w, asked, far, rims, own, wire, mix, back,
    updated, grad_nodes, g_send, g_recv, g_out, g_bias,
    far_r, wire_r, rim_r, mix_r, back_s, back_r, zfar_s, zfar_r, zsum_s, zsum_r, zall, plane_s, plane_all,
    rs_s, rs_r, fs_s, fs_r, zf_s, zf_r, zs_s, zs_r, za_s, za_r, pa_s, pa_r, hs_s, hs_r, os_s, os_r,
):
    planes = n_patch // ring
    per = ring * QUOTA
    chunk = 3072 // planes
    part = chunk // ring
    me, xy, z, feat = place(n_patch, ring)
    up = lax.rem(me + 1, n_patch)
    down = lax.rem(me + n_patch - 1, n_patch)
    other = 1 - feat
    meet(n_patch, ring)

    def ring_peer(d):
        return lax.rem(z + d, ring)

    def plane_peer(d):
        return lax.rem(xy + d, planes)

    def plane_from(d):
        return lax.rem(xy + planes - d, planes)

    def ring_from(d):
        return lax.rem(z + ring - d, ring)

    def wire_copy(d):
        to = plane_peer(d)
        return remote(wire.at[to], wire_r.at[xy], rs_s.at[d], rs_r.at[d], to * ring + z, feat)

    def far_copy(d):
        to = plane_peer(d)
        return remote(far.at[pl.ds(to * per, per)], far_r.at[xy], fs_s.at[d], fs_r.at[d], to * ring + z, feat)

    def arrived(at, send, recv):
        remote(at, at, send, recv, me, other).wait_recv()

    loop(1, planes, lambda d: wire_copy(d).start())
    swap_mix = remote(mix.at[other], mix_r, os_s.at[0], os_r.at[0], me, other)
    swap_mix.start()
    to_down = remote(rims.at[0], rim_r.at[1], hs_s.at[0], hs_r.at[0], down, feat)
    to_up = remote(rims.at[1], rim_r.at[0], hs_s.at[1], hs_r.at[1], up, feat)
    to_down.start()
    to_up.start()
    loop(1, planes, lambda d: far_copy(d).start())

    wire_r[xy] = wire[xy]
    far_r[xy] = far[pl.ds(pl.multiple_of(xy * per, per), per), :]
    swap_mix.wait()
    updated[...] = (feats[...].astype(F32) + mix[feat] + mix_r[...]).astype(BF16)

    loop(1, planes, lambda d: arrived(wire_r.at[plane_from(d)], rs_s.at[d], rs_r.at[d]))
    total = wire_r[0].astype(F32)
    for p in range(1, planes):
        total = total + wire_r[p].astype(F32)
    for k in range(ring):
        zsum_s[k, 0:part, :] = total[k * part : (k + 1) * part, :]
        zsum_s[k, part : part + 8, :] = total[chunk : chunk + 8, :]

    def zsum_copy(d):
        to = ring_peer(d)
        return remote(zsum_s.at[to], zsum_r.at[z], zs_s.at[d], zs_r.at[d], xy * ring + to, feat)

    loop(1, ring, lambda d: zsum_copy(d).start())
    zsum_r[z] = zsum_s[z]

    loop(1, planes, lambda d: arrived(far_r.at[plane_from(d)], fs_s.at[d], fs_r.at[d]))
    lane = lax.broadcasted_iota(I32, (planes * QUOTA, HALO), 1)
    for k in range(ring):
        pick = jnp.where(asked[:, k : k + 1] == lane, 1.0, 0.0).astype(BF16)
        rows = far_r[:, k * QUOTA : (k + 1) * QUOTA, :].reshape(planes * QUOTA, HALF)
        zfar_s[k] = mm(pick, rows, TN)[0:COARSE].astype(BF16)

    def zfar_copy(d):
        to = ring_peer(d)
        return remote(zfar_s.at[to], zfar_r.at[z], zf_s.at[d], zf_r.at[d], xy * ring + to, feat)

    loop(1, ring, lambda d: arrived(zsum_r.at[ring_from(d)], zs_s.at[d], zs_r.at[d]))
    whole = zsum_r[0]
    for k in range(1, ring):
        whole = whole + zsum_r[k]
    g_bias[...] = jnp.concatenate([whole[part : part + 1], whole[part + 1 : part + 2]], axis=1)
    zall[z] = whole[0:part]

    def zall_copy(d):
        return remote(zall.at[z], zall.at[z], za_s.at[d], za_r.at[d], xy * ring + ring_peer(d), feat)

    loop(1, ring, lambda d: zall_copy(d).start())
    loop(1, ring, lambda d: zfar_copy(d).start())
    zfar_r[z] = zfar_s[z]
    loop(1, ring, lambda d: arrived(zall.at[ring_from(d)], za_s.at[d], za_r.at[d]))
    plane_s[...] = zall[...].reshape(chunk, 128).astype(BF16)

    def all_rows(p):
        return plane_all.at[pl.ds(pl.multiple_of(p * chunk, chunk), chunk)]

    def plane_copy(d):
        return remote(plane_s, all_rows(xy), pa_s.at[d], pa_r.at[d], plane_peer(d) * ring + z, feat)

    loop(1, planes, lambda d: plane_copy(d).start())
    plane_all[pl.ds(pl.multiple_of(xy * chunk, chunk), chunk), :] = plane_s[...]

    loop(1, ring, lambda d: arrived(zfar_r.at[ring_from(d)], zf_s.at[d], zf_r.at[d]))
    to_down.wait()
    to_up.wait()
    coarse = zfar_r[0].astype(F32)
    for k in range(1, ring):
        coarse = coarse + zfar_r[k].astype(F32)
    coarse = coarse + own[0:COARSE, :] + rim_r[0, 0:COARSE, :].astype(F32)
    rest = own[COARSE:HALO, :] + rim_r[0, COARSE:HALO, :].astype(F32)
    last = own[ROWS - HALO : ROWS, :] + rim_r[1].astype(F32)
    send_grad = jnp.concatenate([coarse, rest, own[HALO : ROWS - HALO, :], last], axis=0).astype(BF16)
    terms = back[...] + mm(send_grad, send_w[...], NT)
    back_s[0] = terms[:, 0:HALF]
    back_s[1] = terms[:, HALF:]
    swap_back = remote(back_s.at[other], back_r, os_s.at[1], os_r.at[1], me, other)
    swap_back.start()
    swap_back.wait()
    grad_nodes[...] = (cot[...].astype(F32) + back_s[feat] + back_r[...]).astype(BF16)

    loop(1, planes, lambda d: arrived(all_rows(plane_from(d)), pa_s.at[d], pa_r.at[d]))
    for j in range(2):
        cols = slice(128 * j, 128 * (j + 1))
        g_send[:, cols] = plane_all[512 * j : 512 * (j + 1), :].astype(F32)
        g_recv[:, cols] = plane_all[1024 + 512 * j : 1024 + 512 * (j + 1), :].astype(F32)
    for j in range(4):
        g_out[:, 128 * j : 128 * (j + 1)] = plane_all[2048 + 256 * j : 2048 + 256 * (j + 1), :].astype(F32)

    loop(1, planes, lambda d: wire_copy(d).wait_send())
    loop(1, planes, lambda d: far_copy(d).wait_send())
    loop(1, planes, lambda d: plane_copy(d).wait_send())
    loop(1, ring, lambda d: zsum_copy(d).wait_send())
    loop(1, ring, lambda d: zfar_copy(d).wait_send())
    loop(1, ring, lambda d: zall_copy(d).wait_send())


def backward_exchange(n_patch, ring, *args):
    planes = n_patch // ring
    chunk = 3072 // planes
    part = chunk // ring
    vmem = pl.BlockSpec(memory_space=pltpu.VMEM)
    dma = pltpu.SemaphoreType.DMA
    return pl.pallas_call(
        functools.partial(backward_kernel, n_patch, ring),
        out_shape=(
            jax.ShapeDtypeStruct((ROWS, HALF), BF16),
            jax.ShapeDtypeStruct((ROWS, HALF), BF16),
            jax.ShapeDtypeStruct((2 * HALF, HALF), F32),
            jax.ShapeDtypeStruct((2 * HALF, HALF), F32),
            jax.ShapeDtypeStruct((HALF, 2 * HALF), F32),
            jax.ShapeDtypeStruct((1, HALF), F32),
        ),
        in_specs=[vmem] * len(args),
        out_specs=(vmem,) * 6,
        scratch_shapes=[
            pltpu.VMEM((planes, ring * QUOTA, HALF), BF16),
            pltpu.VMEM((planes, chunk + 16, 128), BF16),
            pltpu.VMEM((2, HALO, HALF), BF16),
            pltpu.VMEM((ROWS, HALF), F32),
            pltpu.VMEM((2, ROWS, HALF), F32),
            pltpu.VMEM((ROWS, HALF), F32),
            pltpu.VMEM((ring, COARSE, HALF), BF16),
            pltpu.VMEM((ring, COARSE, HALF), BF16),
            pltpu.VMEM((ring, part + 8, 128), F32),
            pltpu.VMEM((ring, part + 8, 128), F32),
            pltpu.VMEM((ring, part, 128), F32),
            pltpu.VMEM((chunk, 128), BF16),
            pltpu.VMEM((3072, 128), BF16),
            dma((planes,)), dma((planes,)),
            dma((planes,)), dma((planes,)),
            dma((ring,)), dma((ring,)),
            dma((ring,)), dma((ring,)),
            dma((ring,)), dma((ring,)),
            dma((planes,)), dma((planes,)),
            dma((2,)), dma((2,)),
            dma((2,)), dma((2,)),
        ],
        compiler_params=pltpu.CompilerParams(
            collective_id=1, has_side_effects=True, vmem_limit_bytes=48 * 2**20
        ),
        name="backward_exchange",
    )(*args)


def shards(n_patch, ring, feats, cot, send_w, recv_w, out_w, bias, sender, receiver, wanted):
    planes = n_patch // ring
    keys = lax.sort(sender * 1024 + receiver, is_stable=False)
    ends = keys.reshape(EDGES // BLOCK, BLOCK)
    bounds = jnp.stack([ends[:, 0], ends[:, BLOCK - 1]], axis=1).reshape(-1) // (1024 * TILE)
    keys = keys.reshape(EDGES // 128, 128)
    lists = wanted.reshape(planes, ring, QUOTA).transpose(0, 2, 1).reshape(planes * QUOTA, ring)
    lists = jnp.pad(lists, ((0, 0), (0, HALO - ring)))
    table, cots, asked = forward_exchange(n_patch, ring, feats, cot, lists)
    far, rims, own, wire, mix, back = edge_pass(
        n_patch, ring, bounds, keys, table, cots, send_w, recv_w, out_w, bias.reshape(1, HALF)
    )
    updated, grad_nodes, g_send, g_recv, g_out, g_bias = backward_exchange(
        n_patch, ring, feats, cot, send_w, asked, far, rims, own, wire, mix, back
    )
    return (updated, grad_nodes, g_send, g_recv, g_out, g_bias.reshape(HALF))


def solution(mesh):
    n_patch = mesh.shape["patch"]
    ring = 8 if n_patch % 128 == 0 else 2
    in_specs = (
        P("patch", "feat"),
        P("patch", "feat"),
        P(None, "feat"),
        P(None, "feat"),
        P("feat", None),
        P("feat"),
        P("patch"),
        P("patch"),
        P("patch", None, None),
    )
    out_specs = (
        P("patch", "feat"),
        P("patch", "feat"),
        P(None, "feat"),
        P(None, "feat"),
        P("feat", None),
        P("feat"),
    )
    return jax.shard_map(
        functools.partial(shards, n_patch, ring), mesh=mesh, in_specs=in_specs, out_specs=out_specs, check_vma=False
    )
```

```python
import functools

import jax
import jax.numpy as jnp
from jax import lax
from jax.experimental import pallas as pl
from jax.experimental.pallas import tpu as pltpu
from jax.sharding import PartitionSpec as P

HALO = 128
COARSE = 80
QUOTA = 16
ROWS = 640
HALF = 256
EDGES = 8192
NEAR = ROWS + 2 * HALO
BLOCK = 256
TILE = 256
BLOCKS = EDGES // BLOCK
ITEMS = 44
UNROLL = 11
WIDE = 8
SPAN = 1024
MESH = pl.DeviceIdType.MESH
F32 = jnp.float32
BF16 = jnp.bfloat16
I32 = jnp.int32
I16 = jnp.int16
NN = (((1,), (0,)), ((), ()))
TN = (((0,), (0,)), ((), ()))
NT = (((1,), (1,)), ((), ()))


def mm(a, b, dims=NN):
    return lax.dot_general(a, b, dims, preferred_element_type=F32)


def place(n_patch, ring):
    me = lax.axis_index("patch")
    feat = lax.axis_index("feat")
    return me, lax.div(me, ring), lax.rem(me, ring), feat


def meet(n_patch, ring):
    planes = n_patch // ring
    me, xy, z, feat = place(n_patch, ring)
    barrier = pltpu.get_barrier_semaphore()

    def greet(patch, core):
        pl.semaphore_signal(barrier, inc=1, device_id=(patch, core), device_id_type=MESH)

    def greet_plane(d, carry):
        greet(lax.rem(xy + d, planes) * ring + z, feat)
        return carry

    def greet_ring(d, carry):
        greet(xy * ring + lax.rem(z + d, ring), feat)
        return carry

    lax.fori_loop(1, planes, greet_plane, 0)
    lax.fori_loop(1, ring, greet_ring, 0)
    greet(lax.rem(me + 1, n_patch), feat)
    greet(lax.rem(me + n_patch - 1, n_patch), feat)
    greet(me, 1 - feat)
    pl.semaphore_wait(barrier, planes - 1 + ring - 1 + 3)


def remote(src, dst, send, recv, patch, core):
    return pltpu.make_async_remote_copy(
        src_ref=src, dst_ref=dst, send_sem=send, recv_sem=recv,
        device_id=(patch, core), device_id_type=MESH,
    )


def loop(low, high, body):
    def step(i, carry):
        body(i)
        return carry

    lax.fori_loop(low, high, step, 0)


def forward_kernel(
    n_patch, ring,
    feats, cot, lists,
    table, cots, asked,
    coarse, packed,
    zs_s, zs_r, ls_s, ls_r, ps_s, ps_r, fs_s, fs_r, hs_s, hs_r, os_s, os_r, loc,
):
    planes = n_patch // ring
    per = ring * QUOTA
    me, xy, z, feat = place(n_patch, ring)
    up = lax.rem(me + 1, n_patch)
    down = lax.rem(me + n_patch - 1, n_patch)
    other = 1 - feat
    meet(n_patch, ring)

    def ring_peer(d):
        return lax.rem(z + d, ring)

    def plane_peer(d):
        return lax.rem(xy + d, planes)

    def plane_from(d):
        return lax.rem(xy + planes - d, planes)

    def ring_from(d):
        return lax.rem(z + ring - d, ring)

    def coarse_copy(d):
        return remote(feats.at[0:COARSE], coarse.at[z, 0:COARSE], zs_s.at[d], zs_r.at[d], xy * ring + ring_peer(d), feat)

    def list_copy(d):
        to = plane_peer(d)
        return remote(
            lists.at[pl.ds(to * QUOTA, QUOTA)], asked.at[pl.ds(xy * QUOTA, QUOTA)],
            ls_s.at[d], ls_r.at[d], to * ring + z, feat,
        )

    def far_rows(p):
        return table.at[feat, pl.ds(NEAR + p * per, per)]

    def plane_copy(d):
        to = plane_peer(d)
        return remote(packed.at[to], far_rows(xy), ps_s.at[d], ps_r.at[d], to * ring + z, feat)

    loop(1, ring, lambda d: coarse_copy(d).start())
    loop(1, planes, lambda d: list_copy(d).start())
    own_list = pltpu.make_async_copy(lists.at[pl.ds(xy * QUOTA, QUOTA)], asked.at[pl.ds(xy * QUOTA, QUOTA)], loc.at[0])
    own_list.start()
    own_coarse = pltpu.make_async_copy(feats.at[0:COARSE], coarse.at[z, 0:COARSE], loc.at[1])
    own_coarse.start()
    low_rim = table.at[feat, 0:HALO]
    high_rim = table.at[feat, HALO + ROWS : NEAR]
    to_up = remote(feats.at[ROWS - HALO : ROWS], low_rim, hs_s.at[0], hs_r.at[0], up, feat)
    to_down = remote(feats.at[0:HALO], high_rim, hs_s.at[1], hs_r.at[1], down, feat)
    to_up.start()
    to_down.start()
    own_rows = table.at[feat, HALO : HALO + ROWS]
    swap_own = remote(feats, own_rows, os_s.at[0], os_r.at[0], me, other)
    swap_cot = remote(cot, cots.at[feat], os_s.at[1], os_r.at[1], me, other)
    swap_own.start()
    swap_cot.start()
    keep_own = pltpu.make_async_copy(feats, own_rows, loc.at[2])
    keep_cot = pltpu.make_async_copy(cot, cots.at[feat], loc.at[3])
    keep_own.start()
    keep_cot.start()

    for k in range(ring):
        coarse[k, COARSE:HALO] = jnp.zeros((HALO - COARSE, HALF), BF16)

    own_list.wait()
    own_coarse.wait()

    def wait_list(d):
        at = asked.at[pl.ds(plane_from(d) * QUOTA, QUOTA)]
        remote(at, at, ls_s.at[d], ls_r.at[d], me, other).wait_recv()

    def wait_coarse(d):
        at = coarse.at[ring_from(d), 0:COARSE]
        remote(at, at, zs_s.at[d], zs_r.at[d], me, other).wait_recv()

    loop(1, planes, wait_list)
    loop(1, ring, wait_coarse)
    lane = lax.broadcasted_iota(I32, (planes * QUOTA, HALO), 1)
    for k in range(ring):
        pick = jnp.where(asked[:, k : k + 1] == lane, 1.0, 0.0).astype(BF16)
        rows = mm(pick, coarse[k]).astype(BF16)
        packed[:, k * QUOTA : (k + 1) * QUOTA, :] = rows.reshape(planes, QUOTA, HALF)
    loop(1, planes, lambda d: plane_copy(d).start())
    own_far = pltpu.make_async_copy(packed.at[xy], far_rows(xy), loc.at[4])
    own_far.start()
    swap_far = remote(packed.at[xy], far_rows(xy), fs_s.at[0], fs_r.at[0], me, other)
    swap_far.start()

    def pass_on(p, slot):
        at = far_rows(p)
        return remote(at, at, fs_s.at[slot], fs_r.at[slot], me, other)

    def rim_copy(rim, slot):
        return remote(rim, rim, os_s.at[slot], os_r.at[slot], me, other)

    to_up.wait()
    rim_copy(low_rim, 2).start()
    to_down.wait()
    rim_copy(high_rim, 3).start()

    def forward_one(d):
        at = far_rows(plane_from(d))
        remote(at, at, ps_s.at[d], ps_r.at[d], me, other).wait_recv()
        pass_on(plane_from(d), d).start()

    loop(1, planes, forward_one)

    loop(1, planes, lambda d: list_copy(d).wait_send())
    loop(1, ring, lambda d: coarse_copy(d).wait_send())
    loop(1, planes, lambda d: plane_copy(d).wait_send())
    keep_own.wait()
    keep_cot.wait()
    own_far.wait()
    swap_own.wait()
    swap_cot.wait()
    swap_far.wait()
    rim_copy(low_rim, 2).wait()
    rim_copy(high_rim, 3).wait()
    loop(1, planes, lambda d: pass_on(plane_from(d), d).wait())


def forward_exchange(n_patch, ring, feats, cot, lists):
    planes = n_patch // ring
    table_rows = NEAR + n_patch * QUOTA
    vmem = pl.BlockSpec(memory_space=pltpu.VMEM)
    anyspace = pl.BlockSpec(memory_space=pl.ANY)
    dma = pltpu.SemaphoreType.DMA
    return pl.pallas_call(
        functools.partial(forward_kernel, n_patch, ring),
        out_shape=(
            jax.ShapeDtypeStruct((2, table_rows, HALF), BF16),
            jax.ShapeDtypeStruct((2, ROWS, HALF), BF16),
            jax.ShapeDtypeStruct((planes * QUOTA, HALO), I32),
        ),
        in_specs=[vmem] * 3,
        out_specs=(anyspace, anyspace, vmem),
        scratch_shapes=[
            pltpu.VMEM((ring, HALO, HALF), BF16),
            pltpu.VMEM((planes, ring * QUOTA, HALF), BF16),
            dma((ring,)), dma((ring,)),
            dma((planes,)), dma((planes,)),
            dma((planes,)), dma((planes,)),
            dma((planes,)), dma((planes,)),
            dma((2,)), dma((2,)),
            dma((4,)), dma((4,)),
            dma((5,)),
        ],
        compiler_params=pltpu.CompilerParams(
            collective_id=0, has_side_effects=True, vmem_limit_bytes=32 * 2**20
        ),
        name="forward_exchange",
    )(feats, cot, lists)


def edge_kernel(
    table_rows, chunk_count,
    bounds,
    keys, table, cots, send_w, recv_w, out_w, bias,
    far_out, rim_out, own_out, wire, mix, back,
    send_s, pair_s, gsum, dtab, acc, cols, cols_r, pre_s, act_s, gat_s, item_b, item_t,
):
    tiles = pl.cdiv(table_rows, TILE)
    padded = tiles * TILE
    own = slice(HALO, HALO + ROWS)

    for start in range(0, table_rows, 736 if table_rows % 736 == 0 else 128):
        size = 736 if table_rows % 736 == 0 else 128
        rows = slice(start, start + size)
        send_s[rows, :] = (
            mm(table[0, rows, :], send_w[0:HALF, :]) + mm(table[1, rows, :], send_w[HALF:, :])
        ).astype(BF16)
    if padded > table_rows:
        send_s[table_rows:padded, :] = jnp.zeros((padded - table_rows, HALF), BF16)
    pair_s[:, 0:HALF] = (
        mm(table[0, own, :], recv_w[0:HALF, :]) + mm(table[1, own, :], recv_w[HALF:, :]) + bias[...]
    ).astype(BF16)
    grad_sum = mm(cots[0], out_w[:, 0:HALF], NT) + mm(cots[1], out_w[:, HALF:], NT)
    gsum[...] = grad_sum
    pair_s[:, HALF:] = grad_sum.astype(BF16)
    dtab[...] = jnp.zeros_like(dtab)
    acc[...] = jnp.zeros_like(acc)

    turned = jnp.transpose(keys[...])
    for r in range(EDGES // 128):
        spread = jnp.broadcast_to(turned[:, r : r + 1], (128, 128))
        cols[r] = jnp.right_shift(spread, 10).astype(I16)
        cols_r[r] = jnp.bitwise_and(spread, 1023).astype(I16)

    def list_block(b, at):
        def push(t, at):
            item_b[at] = b
            item_t[at] = t
            return at + 1

        return lax.fori_loop(bounds[2 * b], bounds[2 * b + 1] + 1, push, at)

    count = lax.fori_loop(0, BLOCKS, list_block, 0)

    def fill(at, c):
        item_b[at] = 0
        item_t[at] = tiles
        return c

    lax.fori_loop(count, ITEMS, fill, 0)

    lane = lax.broadcasted_iota(I32, (BLOCK, 128), 1).astype(I16)
    sub = lax.broadcasted_iota(I32, (ROWS, 128), 0).astype(I16)
    sub_t = lax.broadcasted_iota(I32, (TILE, 128), 0).astype(I16)

    def hot(mask):
        return jnp.where(mask, BF16(1.0), BF16(0.0))

    def down(row, rows):
        packed = jnp.broadcast_to(row, (16, 128)).astype(I16)
        return jnp.concatenate([packed] * (rows // 16), axis=0)

    def rows_of(b, size=BLOCK):
        return pl.ds(pl.multiple_of(b * size, size), size)

    def gather_item(i):
        b = item_b[i]
        t = item_t[i]
        shifted = cols[pl.ds(2 * b, 2)].reshape(BLOCK, 128) - jnp.full((BLOCK, 128), t * TILE, I32).astype(I16)
        oh = jnp.concatenate([hot(shifted == lane), hot(shifted == lane + I16(128))], axis=1)
        return b, mm(oh, send_s[rows_of(jnp.minimum(t, tiles - 1)), :])

    def gather(i, c):
        parts = [gather_item(i * UNROLL + u) for u in range(UNROLL)]
        for b, part in parts:
            pre_s[rows_of(b), :] += part
        return c

    def clear(b, c):
        pre_s[rows_of(b), :] = jnp.zeros((BLOCK, HALF), F32)
        return c

    lax.fori_loop(0, BLOCKS, clear, 0)
    lax.fori_loop(0, ITEMS // UNROLL, gather, 0)

    def block(b, carry):
        for u in range(WIDE):
            bu = b * WIDE + u
            recv_col = cols_r[pl.ds(2 * bu, 2)].reshape(BLOCK, 128)
            pick = jnp.concatenate([hot(recv_col == lane + I16(128 * j)) for j in range(ROWS // 128)], axis=1)
            both = mm(pick, pair_s[...])
            pre = pre_s[rows_of(bu), :] + both[:, 0:HALF]
            sig = 0.5 * jnp.tanh(0.5 * pre) + 0.5
            hidden = pre * sig
            slope = sig + hidden * (1.0 - sig)
            act_s[rows_of(bu), 0:HALF] = hidden.astype(BF16)
            act_s[rows_of(bu), HALF:] = slope.astype(BF16)
            gat_s[rows_of(bu), :] = (both[:, HALF:] * slope).astype(BF16)
        return carry

    lax.fori_loop(0, BLOCKS // WIDE, block, 0)

    def collect(i, c):
        rows = keys[pl.ds(pl.multiple_of(i * (SPAN // 128), SPAN // 128), SPAN // 128), :]
        recv_row = jnp.bitwise_and(rows, 1023)
        spread = jnp.concatenate([hot(sub == down(recv_row[j : j + 1], ROWS)) for j in range(SPAN // 128)], axis=1)
        acc[...] += mm(spread, act_s[rows_of(i, SPAN), :])
        return c

    lax.fori_loop(0, EDGES // SPAN, collect, 0)

    def scatter_item(i):
        b = item_b[i]
        t = item_t[i]
        shifted = jnp.right_shift(keys[pl.ds(2 * b, 2), :], 10) - t * TILE
        oh = jnp.concatenate([hot(sub_t == down(shifted[0:1], TILE)), hot(sub_t == down(shifted[1:2], TILE))], axis=1)
        return jnp.minimum(t, tiles - 1), mm(oh, gat_s[rows_of(b), :])

    def scatter(i, c):
        parts = [scatter_item(i * UNROLL + u) for u in range(UNROLL)]
        for t, part in parts:
            dtab[rows_of(t), :] += part
        return c

    lax.fori_loop(0, ITEMS // UNROLL, scatter, 0)

    edge_sum = acc[:, 0:HALF].astype(BF16)
    mixed = mm(edge_sum, out_w[...])
    mix[0] = mixed[:, 0:HALF]
    mix[1] = mixed[:, HALF:]
    recv_grad = gsum[...] * acc[:, HALF:]
    bias_part = jnp.sum(recv_grad, axis=0, keepdims=True)
    recv_grad_b = recv_grad.astype(BF16)
    back[...] = mm(recv_grad_b, recv_w[...], NT)
    own_out[...] = dtab[own, :]
    far_out[...] = dtab[NEAR:table_rows, :].astype(BF16)
    rim_out[0] = dtab[0:HALO, :].astype(BF16)
    rim_out[1] = dtab[HALO + ROWS : NEAR, :].astype(BF16)

    chunk = 3072 // chunk_count

    def put(start, value):
        at = 0
        while at < value.shape[0]:
            c, r = divmod(start + at, chunk)
            size = min(chunk - r, value.shape[0] - at)
            wire[c, r : r + size, :] = value[at : at + size, :]
            at += size

    def put_weight(start, value):
        value = value.astype(BF16)
        for j in range(value.shape[1] // 128):
            put(start + j * value.shape[0], value[:, j * 128 : (j + 1) * 128])

    dtab_b = dtab[0:table_rows, :].astype(BF16)
    send_grad = jnp.concatenate([mm(table[0], dtab_b, TN), mm(table[1], dtab_b, TN)], axis=0)
    put_weight(0, send_grad)
    recv_w_grad = jnp.concatenate(
        [mm(table[0, own, :], recv_grad_b, TN), mm(table[1, own, :], recv_grad_b, TN)], axis=0
    )
    put_weight(1024, recv_w_grad)
    put_weight(2048, jnp.concatenate([mm(edge_sum, cots[0], TN), mm(edge_sum, cots[1], TN)], axis=1))
    sub16 = lax.broadcasted_iota(I32, (16, 128), 0)
    tail = jnp.where(sub16 == 0, bias_part[:, 0:128], jnp.where(sub16 == 1, bias_part[:, 128:], 0.0)).astype(BF16)
    for c in range(chunk_count):
        wire[c, chunk : chunk + 16, :] = tail


def edge_pass(n_patch, ring, bounds, keys, table, cots, send_w, recv_w, out_w, bias):
    planes = n_patch // ring
    table_rows = NEAR + n_patch * QUOTA
    padded = pl.cdiv(table_rows, TILE) * TILE
    vmem = pl.BlockSpec(memory_space=pltpu.VMEM)
    return pl.pallas_call(
        functools.partial(edge_kernel, table_rows, planes),
        out_shape=(
            jax.ShapeDtypeStruct((n_patch * QUOTA, HALF), BF16),
            jax.ShapeDtypeStruct((2, HALO, HALF), BF16),
            jax.ShapeDtypeStruct((ROWS, HALF), F32),
            jax.ShapeDtypeStruct((planes, 3072 // planes + 16, 128), BF16),
            jax.ShapeDtypeStruct((2, ROWS, HALF), F32),
            jax.ShapeDtypeStruct((ROWS, 2 * HALF), F32),
        ),
        in_specs=[pl.BlockSpec(memory_space=pltpu.SMEM)] + [vmem] * 7,
        out_specs=(vmem,) * 6,
        scratch_shapes=[
            pltpu.VMEM((padded, HALF), BF16),
            pltpu.VMEM((ROWS, 2 * HALF), BF16),
            pltpu.VMEM((ROWS, HALF), F32),
            pltpu.VMEM((padded, HALF), F32),
            pltpu.VMEM((ROWS, 2 * HALF), F32),
            pltpu.VMEM((EDGES // 128, 128, 128), I16),
            pltpu.VMEM((EDGES // 128, 128, 128), I16),
            pltpu.VMEM((EDGES, HALF), F32),
            pltpu.VMEM((EDGES, 2 * HALF), BF16),
            pltpu.VMEM((EDGES, HALF), BF16),
            pltpu.SMEM((ITEMS,), I32),
            pltpu.SMEM((ITEMS,), I32),
        ],
        compiler_params=pltpu.CompilerParams(vmem_limit_bytes=56 * 2**20),
        name="edge_pass",
    )(bounds, keys, table, cots, send_w, recv_w, out_w, bias)


def backward_kernel(
    n_patch, ring,
    feats, cot, send_w, asked, far, rims, own, wire, mix, back,
    updated, grad_nodes, g_send, g_recv, g_out, g_bias,
    far_r, wire_r, rim_r, mix_r, back_s, back_r, zfar_s, zfar_r, zsum_s, zsum_r, zall, plane_s, plane_all,
    rs_s, rs_r, fs_s, fs_r, zf_s, zf_r, zs_s, zs_r, za_s, za_r, pa_s, pa_r, hs_s, hs_r, os_s, os_r,
):
    planes = n_patch // ring
    per = ring * QUOTA
    chunk = 3072 // planes
    part = chunk // ring
    me, xy, z, feat = place(n_patch, ring)
    up = lax.rem(me + 1, n_patch)
    down = lax.rem(me + n_patch - 1, n_patch)
    other = 1 - feat
    meet(n_patch, ring)

    def ring_peer(d):
        return lax.rem(z + d, ring)

    def plane_peer(d):
        return lax.rem(xy + d, planes)

    def plane_from(d):
        return lax.rem(xy + planes - d, planes)

    def ring_from(d):
        return lax.rem(z + ring - d, ring)

    def wire_copy(d):
        to = plane_peer(d)
        return remote(wire.at[to], wire_r.at[xy], rs_s.at[d], rs_r.at[d], to * ring + z, feat)

    def far_copy(d):
        to = plane_peer(d)
        return remote(far.at[pl.ds(to * per, per)], far_r.at[xy], fs_s.at[d], fs_r.at[d], to * ring + z, feat)

    def arrived(at, send, recv):
        remote(at, at, send, recv, me, other).wait_recv()

    loop(1, planes, lambda d: wire_copy(d).start())
    swap_mix = remote(mix.at[other], mix_r, os_s.at[0], os_r.at[0], me, other)
    swap_mix.start()
    to_down = remote(rims.at[0], rim_r.at[1], hs_s.at[0], hs_r.at[0], down, feat)
    to_up = remote(rims.at[1], rim_r.at[0], hs_s.at[1], hs_r.at[1], up, feat)
    to_down.start()
    to_up.start()
    loop(1, planes, lambda d: far_copy(d).start())

    wire_r[xy] = wire[xy]
    far_r[xy] = far[pl.ds(pl.multiple_of(xy * per, per), per), :]
    swap_mix.wait()
    updated[...] = (feats[...].astype(F32) + mix[feat] + mix_r[...]).astype(BF16)

    loop(1, planes, lambda d: arrived(wire_r.at[plane_from(d)], rs_s.at[d], rs_r.at[d]))
    total = wire_r[0].astype(F32)
    for p in range(1, planes):
        total = total + wire_r[p].astype(F32)
    for k in range(ring):
        zsum_s[k, 0:part, :] = total[k * part : (k + 1) * part, :]
        zsum_s[k, part : part + 8, :] = total[chunk : chunk + 8, :]

    def zsum_copy(d):
        to = ring_peer(d)
        return remote(zsum_s.at[to], zsum_r.at[z], zs_s.at[d], zs_r.at[d], xy * ring + to, feat)

    loop(1, ring, lambda d: zsum_copy(d).start())
    zsum_r[z] = zsum_s[z]

    loop(1, planes, lambda d: arrived(far_r.at[plane_from(d)], fs_s.at[d], fs_r.at[d]))
    lane = lax.broadcasted_iota(I32, (planes * QUOTA, HALO), 1)
    for k in range(ring):
        pick = jnp.where(asked[:, k : k + 1] == lane, 1.0, 0.0).astype(BF16)
        rows = far_r[:, k * QUOTA : (k + 1) * QUOTA, :].reshape(planes * QUOTA, HALF)
        zfar_s[k] = mm(pick, rows, TN)[0:COARSE].astype(BF16)

    def zfar_copy(d):
        to = ring_peer(d)
        return remote(zfar_s.at[to], zfar_r.at[z], zf_s.at[d], zf_r.at[d], xy * ring + to, feat)

    loop(1, ring, lambda d: arrived(zsum_r.at[ring_from(d)], zs_s.at[d], zs_r.at[d]))
    whole = zsum_r[0]
    for k in range(1, ring):
        whole = whole + zsum_r[k]
    g_bias[...] = jnp.concatenate([whole[part : part + 1], whole[part + 1 : part + 2]], axis=1)
    zall[z] = whole[0:part]

    def zall_copy(d):
        return remote(zall.at[z], zall.at[z], za_s.at[d], za_r.at[d], xy * ring + ring_peer(d), feat)

    loop(1, ring, lambda d: zall_copy(d).start())
    loop(1, ring, lambda d: zfar_copy(d).start())
    zfar_r[z] = zfar_s[z]
    loop(1, ring, lambda d: arrived(zall.at[ring_from(d)], za_s.at[d], za_r.at[d]))
    plane_s[...] = zall[...].reshape(chunk, 128).astype(BF16)

    def all_rows(p):
        return plane_all.at[pl.ds(pl.multiple_of(p * chunk, chunk), chunk)]

    def plane_copy(d):
        return remote(plane_s, all_rows(xy), pa_s.at[d], pa_r.at[d], plane_peer(d) * ring + z, feat)

    loop(1, planes, lambda d: plane_copy(d).start())
    plane_all[pl.ds(pl.multiple_of(xy * chunk, chunk), chunk), :] = plane_s[...]

    loop(1, ring, lambda d: arrived(zfar_r.at[ring_from(d)], zf_s.at[d], zf_r.at[d]))
    to_down.wait()
    to_up.wait()
    coarse = zfar_r[0].astype(F32)
    for k in range(1, ring):
        coarse = coarse + zfar_r[k].astype(F32)
    coarse = coarse + own[0:COARSE, :] + rim_r[0, 0:COARSE, :].astype(F32)
    rest = own[COARSE:HALO, :] + rim_r[0, COARSE:HALO, :].astype(F32)
    last = own[ROWS - HALO : ROWS, :] + rim_r[1].astype(F32)
    send_grad = jnp.concatenate([coarse, rest, own[HALO : ROWS - HALO, :], last], axis=0).astype(BF16)
    terms = back[...] + mm(send_grad, send_w[...], NT)
    back_s[0] = terms[:, 0:HALF]
    back_s[1] = terms[:, HALF:]
    swap_back = remote(back_s.at[other], back_r, os_s.at[1], os_r.at[1], me, other)
    swap_back.start()
    swap_back.wait()
    grad_nodes[...] = (cot[...].astype(F32) + back_s[feat] + back_r[...]).astype(BF16)

    loop(1, planes, lambda d: arrived(all_rows(plane_from(d)), pa_s.at[d], pa_r.at[d]))
    for j in range(2):
        cols = slice(128 * j, 128 * (j + 1))
        g_send[:, cols] = plane_all[512 * j : 512 * (j + 1), :].astype(F32)
        g_recv[:, cols] = plane_all[1024 + 512 * j : 1024 + 512 * (j + 1), :].astype(F32)
    for j in range(4):
        g_out[:, 128 * j : 128 * (j + 1)] = plane_all[2048 + 256 * j : 2048 + 256 * (j + 1), :].astype(F32)

    loop(1, planes, lambda d: wire_copy(d).wait_send())
    loop(1, planes, lambda d: far_copy(d).wait_send())
    loop(1, planes, lambda d: plane_copy(d).wait_send())
    loop(1, ring, lambda d: zsum_copy(d).wait_send())
    loop(1, ring, lambda d: zfar_copy(d).wait_send())
    loop(1, ring, lambda d: zall_copy(d).wait_send())


def backward_exchange(n_patch, ring, *args):
    planes = n_patch // ring
    chunk = 3072 // planes
    part = chunk // ring
    vmem = pl.BlockSpec(memory_space=pltpu.VMEM)
    dma = pltpu.SemaphoreType.DMA
    return pl.pallas_call(
        functools.partial(backward_kernel, n_patch, ring),
        out_shape=(
            jax.ShapeDtypeStruct((ROWS, HALF), BF16),
            jax.ShapeDtypeStruct((ROWS, HALF), BF16),
            jax.ShapeDtypeStruct((2 * HALF, HALF), F32),
            jax.ShapeDtypeStruct((2 * HALF, HALF), F32),
            jax.ShapeDtypeStruct((HALF, 2 * HALF), F32),
            jax.ShapeDtypeStruct((1, HALF), F32),
        ),
        in_specs=[vmem] * len(args),
        out_specs=(vmem,) * 6,
        scratch_shapes=[
            pltpu.VMEM((planes, ring * QUOTA, HALF), BF16),
            pltpu.VMEM((planes, chunk + 16, 128), BF16),
            pltpu.VMEM((2, HALO, HALF), BF16),
            pltpu.VMEM((ROWS, HALF), F32),
            pltpu.VMEM((2, ROWS, HALF), F32),
            pltpu.VMEM((ROWS, HALF), F32),
            pltpu.VMEM((ring, COARSE, HALF), BF16),
            pltpu.VMEM((ring, COARSE, HALF), BF16),
            pltpu.VMEM((ring, part + 8, 128), F32),
            pltpu.VMEM((ring, part + 8, 128), F32),
            pltpu.VMEM((ring, part, 128), F32),
            pltpu.VMEM((chunk, 128), BF16),
            pltpu.VMEM((3072, 128), BF16),
            dma((planes,)), dma((planes,)),
            dma((planes,)), dma((planes,)),
            dma((ring,)), dma((ring,)),
            dma((ring,)), dma((ring,)),
            dma((ring,)), dma((ring,)),
            dma((planes,)), dma((planes,)),
            dma((2,)), dma((2,)),
            dma((2,)), dma((2,)),
        ],
        compiler_params=pltpu.CompilerParams(
            collective_id=1, has_side_effects=True, vmem_limit_bytes=48 * 2**20
        ),
        name="backward_exchange",
    )(*args)


def shards(n_patch, ring, feats, cot, send_w, recv_w, out_w, bias, sender, receiver, wanted):
    planes = n_patch // ring
    keys = lax.sort(sender * 1024 + receiver, is_stable=False)
    ends = keys.reshape(EDGES // BLOCK, BLOCK)
    bounds = jnp.stack([ends[:, 0], ends[:, BLOCK - 1]], axis=1).reshape(-1) // (1024 * TILE)
    keys = keys.reshape(EDGES // 128, 128)
    lists = wanted.reshape(planes, ring, QUOTA).transpose(0, 2, 1).reshape(planes * QUOTA, ring)
    lists = jnp.pad(lists, ((0, 0), (0, HALO - ring)))
    table, cots, asked = forward_exchange(n_patch, ring, feats, cot, lists)
    far, rims, own, wire, mix, back = edge_pass(
        n_patch, ring, bounds, keys, table, cots, send_w, recv_w, out_w, bias.reshape(1, HALF)
    )
    updated, grad_nodes, g_send, g_recv, g_out, g_bias = backward_exchange(
        n_patch, ring, feats, cot, send_w, asked, far, rims, own, wire, mix, back
    )
    return (updated, grad_nodes, g_send, g_recv, g_out, g_bias.reshape(HALF))


def solution(mesh):
    n_patch = mesh.shape["patch"]
    ring = 8 if n_patch % 128 == 0 else 2
    in_specs = (
        P("patch", "feat"),
        P("patch", "feat"),
        P(None, "feat"),
        P(None, "feat"),
        P("feat", None),
        P("feat"),
        P("patch"),
        P("patch"),
        P("patch", None, None),
    )
    out_specs = (
        P("patch", "feat"),
        P("patch", "feat"),
        P(None, "feat"),
        P(None, "feat"),
        P("feat", None),
        P("feat"),
    )
    return jax.shard_map(
        functools.partial(shards, n_patch, ring), mesh=mesh, in_specs=in_specs, out_specs=out_specs, check_vma=False
    )
```

```python
import functools

import jax
import jax.numpy as jnp
from jax import lax
from jax.experimental import pallas as pl
from jax.experimental.pallas import tpu as pltpu
from jax.sharding import PartitionSpec as P

HALO = 128
COARSE = 80
QUOTA = 16
ROWS = 640
HALF = 256
EDGES = 8192
NEAR = ROWS + 2 * HALO
BLOCK = 256
BLOCKS = EDGES // BLOCK
TILE = 256
SPAN = 1024
UNROLL = 11
PAIRS = EDGES // 128
RING = 8
PER = RING * QUOTA
ORDER = (0, 1, 7, 2, 6, 3, 5, 4)
GROUPS = ((0, 1), (1, 3), (3, 8))
MESH = pl.DeviceIdType.MESH
F32 = jnp.float32
BF16 = jnp.bfloat16
I32 = jnp.int32
I16 = jnp.int16
NN = (((1,), (0,)), ((), ()))
TN = (((0,), (0,)), ((), ()))
NT = (((1,), (1,)), ((), ()))


def mm(a, b, dims=NN):
    return lax.dot_general(a, b, dims, preferred_element_type=F32)


def loop(low, high, body):
    def step(i, carry):
        body(i)
        return carry

    lax.fori_loop(low, high, step, 0)


def hot(mask):
    return jnp.where(mask, BF16(1.0), BF16(0.0))


def hot32(mask):
    return jnp.where(mask, 1.0, 0.0).astype(BF16)


def down(row, rows):
    packed = jnp.broadcast_to(row, (16, 128)).astype(I16)
    return jnp.concatenate([packed] * (rows // 16), axis=0)


def rows_of(b, size=BLOCK):
    return pl.ds(pl.multiple_of(b * size, size), size)


def remote(src, dst, send, recv, patch, core):
    return pltpu.make_async_remote_copy(
        src_ref=src, dst_ref=dst, send_sem=send, recv_sem=recv,
        device_id=(patch, core), device_id_type=MESH,
    )


def sort_steps(first, last):
    return [(k, j) for k in range(first, last + 1) for j in range(k - 1, -1, -1)]


def bitonic(xs, steps):
    lane = lax.broadcasted_iota(I32, (8, 128), 1)
    sub = lax.broadcasted_iota(I32, (8, 128), 0)

    def bit(j, v):
        if j >= 13:
            return True
        if j < 3:
            return (v >> j) & 1 == 0
        if j < 6:
            return jnp.bitwise_and(sub, 1 << (j - 3)) == 0
        return jnp.bitwise_and(lane, 1 << (j - 6)) == 0

    def pick(cond, a, b):
        if isinstance(cond, bool):
            return a if cond else b
        return jnp.where(cond, a, b)

    for k, j in steps:
        out = list(xs)
        if j < 3:
            for v in range(8):
                if v & (1 << j):
                    continue
                w = v | (1 << j)
                small, large = jnp.minimum(xs[v], xs[w]), jnp.maximum(xs[v], xs[w])
                rising = bit(k, v)
                out[v], out[w] = pick(rising, small, large), pick(rising, large, small)
        else:
            axis, size, far = (0, 8, 1 << (j - 3)) if j < 6 else (1, 128, 1 << (j - 6))
            low = bit(j, 0)
            for v in range(8):
                x = xs[v]
                mate = jnp.where(low, pltpu.roll(x, size - far, axis), pltpu.roll(x, far, axis))
                rising = bit(k, v)
                if isinstance(rising, bool):
                    least = low if rising else jnp.logical_not(low)
                else:
                    least = low == rising
                out[v] = jnp.where(least, jnp.minimum(x, mate), jnp.maximum(x, mate))
        xs = out
    return xs


def layer_kernel(
    n_patch,
    sender, receiver, lists, bias, feats, cot, send_w_in, recv_w_in, out_w_in,
    updated, grad_nodes, weights_out, bias_out,
    table, cots, send_w, recv_w, out_w, asked, asked_z, coarse, packed,
    keys, turned, plan_v, plan, cols_s, cols_r, rows_k, pairs_k,
    send_s, pair_s, gsum, pre_s, gat_s, items, act_a, act_b, acc, dtab,
    far_s, rim_s, mix, mix_r, back, back_s, back_r,
    wire_a, wire_b, wire_ar, wire_br, far_r, rim_r,
    zfar_s, zfar_r, zsum_s, zsum_r, zall, plane_s, plane_all,
    loc, zs_s, zs_r, ls_s, ls_r, ps_s, ps_r, pass_s, pass_r, hs_s, hs_r, os_s, os_r,
    wa_s, wa_r, wb_s, wb_r, fb_s, fb_r, hb_s, hb_r, zf_s, zf_r, zw_s, zw_r, za_s, za_r, pa_s, pa_r,
):
    planes = n_patch // RING
    table_rows = NEAR + n_patch * QUOTA
    tiles = pl.cdiv(table_rows, TILE)
    padded = tiles * TILE
    n_items = pl.cdiv(BLOCKS + tiles - 1, UNROLL) * UNROLL
    own = slice(HALO, HALO + ROWS)
    me = lax.axis_index("patch")
    feat = lax.axis_index("feat")
    other = 1 - feat
    xy, z = lax.div(me, RING), lax.rem(me, RING)
    up = lax.rem(me + 1, n_patch)
    below = lax.rem(me + n_patch - 1, n_patch)

    def ring_peer(d):
        return xy * RING + lax.rem(z + d, RING)

    def plane_at(d):
        return lax.rem(xy + d, planes)

    def plane_from(d):
        return lax.rem(xy + planes - d, planes)

    def ring_from(d):
        return lax.rem(z + RING - d, RING)

    def arrived(at, send, recv):
        remote(at, at, send, recv, me, other).wait_recv()

    own_rows = table.at[feat, HALO : HALO + ROWS]
    local = [
        pltpu.make_async_copy(feats.at[0:COARSE], coarse.at[0, 0:COARSE], loc.at[0]),
        pltpu.make_async_copy(feats, own_rows, loc.at[1]),
        pltpu.make_async_copy(cot, cots.at[feat], loc.at[2]),
        pltpu.make_async_copy(send_w_in, send_w, loc.at[3]),
        pltpu.make_async_copy(recv_w_in, recv_w, loc.at[4]),
        pltpu.make_async_copy(out_w_in, out_w, loc.at[5]),
        pltpu.make_async_copy(lists.at[rows_of(xy, QUOTA)], asked.at[rows_of(xy, QUOTA)], loc.at[6]),
    ]
    for copy in local:
        copy.start()

    barrier = pltpu.get_barrier_semaphore()

    def greet(patch, core):
        pl.semaphore_signal(barrier, inc=1, device_id=(patch, core), device_id_type=MESH)

    loop(1, RING, lambda d: greet(ring_peer(d), feat))
    loop(1, planes, lambda d: greet(plane_at(d) * RING + z, feat))
    greet(up, feat)
    greet(below, feat)
    greet(me, other)
    pl.semaphore_wait(barrier, planes - 1 + RING - 1 + 3)

    def coarse_copy(d):
        return remote(feats.at[0:COARSE], coarse.at[RING - d, 0:COARSE], zs_s.at[d], zs_r.at[RING - d], ring_peer(d), feat)

    def list_copy(d):
        to = plane_at(d)
        return remote(lists.at[rows_of(to, QUOTA)], asked.at[rows_of(xy, QUOTA)], ls_s.at[d], ls_r.at[d], to * RING + z, feat)

    def far_rows(p, low=0, high=RING):
        return table.at[feat, pl.ds(pl.multiple_of(NEAR + p * PER + low * QUOTA, QUOTA), (high - low) * QUOTA)]

    def plane_copy(g, d):
        low, high = GROUPS[g]
        to = plane_at(d)
        return remote(
            packed.at[to, low * QUOTA : high * QUOTA], far_rows(xy, low, high), ps_s.at[g, d], ps_r.at[g, d], to * RING + z, feat
        )

    def swap(ref, slot):
        return remote(ref, ref, os_s.at[slot], os_r.at[slot], me, other)

    loop(1, planes, lambda d: list_copy(d).start())
    for d in ORDER[1:]:
        coarse_copy(d).start()
    low_rim = table.at[feat, 0:HALO]
    high_rim = table.at[feat, HALO + ROWS : NEAR]
    to_up = remote(feats.at[ROWS - HALO : ROWS], low_rim, hs_s.at[0], hs_r.at[0], up, feat)
    to_below = remote(feats.at[0:HALO], high_rim, hs_s.at[1], hs_r.at[1], below, feat)
    to_up.start()
    to_below.start()
    swap_own = remote(feats, own_rows, os_s.at[0], os_r.at[0], me, other)
    swap_cot = remote(cot, cots.at[feat], os_s.at[1], os_r.at[1], me, other)
    swap_own.start()
    swap_cot.start()

    lane32 = lax.broadcasted_iota(I32, (planes * QUOTA, HALO), 1)
    for k in range(RING):
        coarse[k, COARSE:HALO] = jnp.zeros((HALO - COARSE, HALF), BF16)

    def pack(g):
        for at in range(*GROUPS[g]):
            k = ORDER[at]
            pick = hot32(asked_z[:, k : k + 1] == lane32)
            rows = mm(pick, coarse[k]).astype(BF16)
            packed[:, at * QUOTA : (at + 1) * QUOTA, :] = rows.reshape(planes, QUOTA, HALF)
        loop(1, planes, lambda d: plane_copy(g, d).start())

    s = sender[...]
    j = s - NEAR
    away = jnp.bitwise_and(jnp.right_shift(j, 4) - z, RING - 1)
    spot = jnp.where(away <= 4, jnp.maximum(2 * away - 1, 0), 2 * RING - 2 * away)
    row = NEAR + j - jnp.bitwise_and(j, PER - 1) + spot * QUOTA + jnp.bitwise_and(j, QUOTA - 1)
    word = jnp.where(s < NEAR, s, row) * 1024 + receiver[...]
    xs = [word[8 * v : 8 * v + 8] for v in range(8)]

    local[6].wait()
    loop(1, planes, lambda d: arrived(asked.at[rows_of(plane_from(d), QUOTA)], ls_s.at[d], ls_r.at[d]))
    asked_z[...] = pltpu.roll(asked[...], lax.rem(128 - z, 128), 1)
    local[0].wait()
    pack(0)
    for k in ORDER[1:3]:
        arrived(coarse.at[k, 0:COARSE], zs_s.at[k], zs_r.at[k])
    pack(1)
    xs = bitonic(xs, sort_steps(1, 9))
    for k in ORDER[3:]:
        arrived(coarse.at[k, 0:COARSE], zs_s.at[k], zs_r.at[k])
    pack(2)
    own_far = pltpu.make_async_copy(packed.at[xy], far_rows(xy), loc.at[7])
    own_far.start()
    swap_far = remote(packed.at[xy], far_rows(xy), pass_s.at[0], pass_r.at[0], me, other)
    swap_far.start()
    xs = bitonic(xs, sort_steps(10, 13))

    for v in range(8):
        keys[8 * v : 8 * v + 8, :] = xs[v]
    flat = keys[...]
    turned[...] = jnp.transpose(jnp.concatenate([flat, flat], axis=0))
    lane64 = lax.broadcasted_iota(I32, (PAIRS, 128), 1)
    rows_k[...] = jnp.where(
        lane64 < 64, turned[pl.ds(0, PAIRS, stride=2), :], turned[pl.ds(1, PAIRS, stride=2), :]
    )
    for r in range(128):
        spread = jnp.broadcast_to(flat[:, r : r + 1], (64, 128))
        rows = slice(64 * (r % 4), 64 * (r % 4) + 64)
        cols_s[r // 4, rows, :] = jnp.right_shift(spread, 10).astype(I16)
        cols_r[r // 4, rows, :] = jnp.bitwise_and(spread, 1023).astype(I16)
    for b in range(BLOCKS):
        pairs_k[b] = jnp.concatenate([rows_k[2 * b : 2 * b + 2, :], jnp.zeros((6, 128), I32)], axis=0)

    tall = lax.broadcasted_iota(I32, (128, 128), 0)
    wide = lax.broadcasted_iota(I32, (128, 128), 1)
    heads = jnp.logical_and(jnp.bitwise_and(tall, 3) == 0, tall > 0)
    first_tile = jnp.right_shift(jnp.broadcast_to(turned[:, 0:1], (128, 128)), 18)
    first_item = first_tile + jnp.right_shift(tall, 2)
    block_of = jnp.sum(jnp.where(jnp.logical_and(heads, first_item <= wide), 1, 0), axis=0, keepdims=True)
    last_of = jnp.sum(jnp.where(jnp.logical_and(heads, first_tile <= wide), 1, 0), axis=0, keepdims=True) + wide[0:1]
    first_of = jnp.right_shift(flat[0:1], 18) + jnp.right_shift(wide[0:1], 2)
    plan_v[...] = jnp.concatenate([block_of, last_of, first_of, jnp.zeros((5, 128), I32)], axis=0)
    to_scalars = pltpu.make_async_copy(plan_v, plan, loc.at[8])
    to_scalars.start()
    to_scalars.wait()

    for copy in local[1:6]:
        copy.wait()
    swap_own.wait()
    swap_cot.wait()
    pair_s[:, 0:HALF] = (
        mm(table[0, own, :], recv_w[0:HALF, :]) + mm(table[1, own, :], recv_w[HALF:, :]) + bias[...]
    ).astype(BF16)
    grad_sum = mm(cots[0], out_w[:, 0:HALF], NT) + mm(cots[1], out_w[:, HALF:], NT)
    gsum[...] = grad_sum
    pair_s[:, HALF:] = grad_sum.astype(BF16)
    acc[...] = jnp.zeros_like(acc)
    lane = lax.broadcasted_iota(I32, (BLOCK, 128), 1).astype(I16)
    sub = lax.broadcasted_iota(I32, (ROWS, 128), 0).astype(I16)
    sub_t = lax.broadcasted_iota(I32, (TILE, 128), 0).astype(I16)

    def receive(i):
        for u in range(4):
            b = 4 * i + u
            col = cols_r[b]
            pick = jnp.concatenate([hot(col == lane + I16(128 * m)) for m in range(ROWS // 128)], axis=1)
            both = mm(pick, pair_s[...])
            pre_s[b] = both[:, 0:HALF]
            gat_s[b] = both[:, HALF:].astype(BF16)

    loop(0, BLOCKS // 4, receive)

    def pass_on(p, slot):
        return remote(far_rows(p), far_rows(p), pass_s.at[slot], pass_r.at[slot], me, other)

    to_up.wait()
    swap(low_rim, 2).start()
    to_below.wait()
    swap(high_rim, 3).start()

    def hand_on(d):
        for g, (low, high) in enumerate(GROUPS):
            arrived(far_rows(plane_from(d), low, high), ps_s.at[g, d], ps_r.at[g, d])
        pass_on(plane_from(d), d).start()

    loop(1, planes, hand_on)
    own_far.wait()
    swap_far.wait()
    swap(low_rim, 2).wait()
    swap(high_rim, 3).wait()
    loop(1, planes, lambda d: pass_on(plane_from(d), d).wait())

    size = 736 if table_rows % 736 == 0 else 128
    for start in range(0, table_rows, size):
        part = slice(start, start + size)
        value = (mm(table[0, part, :], send_w[0:HALF, :]) + mm(table[1, part, :], send_w[HALF:, :])).astype(BF16)
        at = 0
        while at < size:
            t, r = divmod(start + at, TILE)
            count = min(TILE - r, size - at)
            send_s[t, r : r + count, :] = value[at : at + count]
            at += count
    if padded > table_rows:
        send_s[tiles - 1, table_rows - padded + TILE :, :] = jnp.zeros((padded - table_rows, HALF), BF16)
    send_s[tiles] = jnp.zeros((TILE, HALF), BF16)

    def gather(i):
        for u in range(UNROLL):
            at = i * UNROLL + u
            b = plan[0, at]
            before = plan[0, jnp.maximum(at - 1, 0)]
            t = at - b
            col = cols_s[b] - jnp.full((BLOCK, 128), t * TILE, I32).astype(I16)
            pick = jnp.concatenate([hot(col == lane), hot(col == lane + I16(128))], axis=1)
            part = mm(pick, send_s[t])
            keep = 1.0 - (b - before).astype(F32)
            items[at] = part + keep * items[jnp.maximum(at - 1, 0)]

    items[0] = jnp.zeros((BLOCK, HALF), F32)
    loop(0, n_items // UNROLL, gather)

    def messages(i, act):
        for u in range(SPAN // BLOCK):
            b = i * (SPAN // BLOCK) + u
            last = jnp.where(b == BLOCKS - 1, BLOCKS + tiles - 1, plan[2, jnp.minimum(4 * b + 4, 127)]) - 1
            pre = pre_s[b] + items[last]
            sig = 0.5 * jnp.tanh(0.5 * pre) + 0.5
            hidden = pre * sig
            slope = sig + hidden * (1.0 - sig)
            act[u * BLOCK : (u + 1) * BLOCK, 0:HALF] = hidden.astype(BF16)
            act[u * BLOCK : (u + 1) * BLOCK, HALF:] = slope.astype(BF16)
            gat_s[b] = (gat_s[b].astype(F32) * slope).astype(BF16)

    def collect(i, act):
        words = jnp.bitwise_and(rows_k[rows_of(i, SPAN // 128), :], 1023)
        spread = jnp.concatenate([hot(sub == down(words[m : m + 1], ROWS)) for m in range(SPAN // 128)], axis=1)
        acc[...] += mm(spread, act[...])

    act_b[...] = jnp.zeros_like(act_b)

    def two_spans(i):
        messages(2 * i, act_a)
        collect(jnp.maximum(2 * i - 1, 0), act_b)
        messages(2 * i + 1, act_b)
        collect(2 * i, act_a)

    loop(0, EDGES // SPAN // 2, two_spans)
    collect(EDGES // SPAN - 1, act_b)

    edge_sum = acc[:, 0:HALF].astype(BF16)
    mixed = mm(edge_sum, out_w[...])
    mix[0] = mixed[:, 0:HALF]
    mix[1] = mixed[:, HALF:]
    swap_mix = remote(mix.at[other], mix_r, os_s.at[4], os_r.at[4], me, other)
    swap_mix.start()
    recv_grad = gsum[...] * acc[:, HALF:]
    bias_part = jnp.sum(recv_grad, axis=0, keepdims=True)
    recv_grad_b = recv_grad.astype(BF16)

    chunk_a, chunk_b = 2048 // planes, 1024 // planes

    def put(wire, chunk, start, value):
        value = value.astype(BF16)
        for m in range(value.shape[1] // 128):
            at = 0
            while at < value.shape[0]:
                c, r = divmod(start + m * value.shape[0] + at, chunk)
                count = min(chunk - r, value.shape[0] - at)
                wire[c, r : r + count, :] = value[at : at + count, m * 128 : (m + 1) * 128]
                at += count

    put(
        wire_a, chunk_a, 0,
        jnp.concatenate([mm(table[0, own, :], recv_grad_b, TN), mm(table[1, own, :], recv_grad_b, TN)], axis=0),
    )
    put(wire_a, chunk_a, 1024, jnp.concatenate([mm(edge_sum, cots[0], TN), mm(edge_sum, cots[1], TN)], axis=1))
    sub16 = lax.broadcasted_iota(I32, (16, 128), 0)
    tail = jnp.where(sub16 == 0, bias_part[:, 0:128], jnp.where(sub16 == 1, bias_part[:, 128:], 0.0)).astype(BF16)
    for c in range(planes):
        wire_a[c, chunk_a : chunk_a + 16, :] = tail

    def wire_copy(src, dst, send, recv, d):
        to = plane_at(d)
        return remote(src.at[to], dst.at[xy], send.at[d], recv.at[d], to * RING + z, feat)

    loop(1, planes, lambda d: wire_copy(wire_a, wire_ar, wa_s, wa_r, d).start())
    wire_ar[xy] = wire_a[xy]

    def scatter(i):
        for u in range(UNROLL):
            at = i * UNROLL + u
            b = plan[0, at]
            before = plan[0, jnp.maximum(at - 1, 0)]
            t = at - b
            words = jnp.right_shift(pairs_k[b], 10) - t * TILE
            spread = jnp.concatenate([hot(sub_t == down(words[0:1], TILE)), hot(sub_t == down(words[1:2], TILE))], axis=1)
            part = mm(spread, gat_s[b])
            keep = (b - before).astype(F32)
            items[at] = part + keep * items[jnp.maximum(at - 1, 0)]

    items[0] = jnp.zeros((BLOCK, HALF), F32)
    loop(0, n_items // UNROLL, scatter)
    for t in range(tiles):
        dtab[t * TILE : (t + 1) * TILE, :] = items[plan[1, t]]

    dtab_b = dtab[0:table_rows, :].astype(BF16)
    put(wire_b, chunk_b, 0, jnp.concatenate([mm(table[0], dtab_b, TN), mm(table[1], dtab_b, TN)], axis=0))
    loop(1, planes, lambda d: wire_copy(wire_b, wire_br, wb_s, wb_r, d).start())
    wire_br[xy] = wire_b[xy]
    rim_s[0] = dtab[0:HALO, :].astype(BF16)
    rim_s[1] = dtab[HALO + ROWS : NEAR, :].astype(BF16)
    back_below = remote(rim_s.at[0], rim_r.at[1], hb_s.at[0], hb_r.at[0], below, feat)
    back_up = remote(rim_s.at[1], rim_r.at[0], hb_s.at[1], hb_r.at[1], up, feat)
    back_below.start()
    back_up.start()
    far_s[...] = dtab[NEAR:table_rows, :].astype(BF16)

    def far_copy(d):
        to = plane_at(d)
        return remote(far_s.at[rows_of(to, PER)], far_r.at[xy], fb_s.at[d], fb_r.at[d], to * RING + z, feat)

    loop(1, planes, lambda d: far_copy(d).start())
    far_r[xy] = far_s[rows_of(xy, PER), :]
    back[...] = mm(recv_grad_b, recv_w[...], NT)
    swap_mix.wait()
    updated[...] = (table[feat, own, :].astype(F32) + mix[feat] + mix_r[...]).astype(BF16)

    part_a, part_b = chunk_a // RING, chunk_b // RING
    part = part_a + part_b
    loop(1, planes, lambda d: arrived(wire_ar.at[plane_from(d)], wa_s.at[d], wa_r.at[d]))
    total = wire_ar[0].astype(F32)
    for p in range(1, planes):
        total = total + wire_ar[p].astype(F32)
    for k in range(RING):
        zsum_s[k, 0:part_a, :] = total[k * part_a : (k + 1) * part_a, :]
        zsum_s[k, part : part + 8, :] = total[chunk_a : chunk_a + 8, :]
    loop(1, planes, lambda d: arrived(wire_br.at[plane_from(d)], wb_s.at[d], wb_r.at[d]))
    total = wire_br[0].astype(F32)
    for p in range(1, planes):
        total = total + wire_br[p].astype(F32)
    for k in range(RING):
        zsum_s[k, part_a:part, :] = total[k * part_b : (k + 1) * part_b, :]

    def zsum_copy(d):
        to = lax.rem(z + d, RING)
        return remote(zsum_s.at[to], zsum_r.at[z], zw_s.at[d], zw_r.at[d], ring_peer(d), feat)

    loop(1, RING, lambda d: zsum_copy(d).start())
    zsum_r[z] = zsum_s[z]
    loop(1, RING, lambda d: arrived(zsum_r.at[ring_from(d)], zw_s.at[d], zw_r.at[d]))
    whole = zsum_r[0]
    for k in range(1, RING):
        whole = whole + zsum_r[k]
    bias_out[...] = jnp.concatenate([whole[part : part + 1], whole[part + 1 : part + 2]], axis=1)
    zall[z] = whole[0:part]

    def zall_copy(d):
        return remote(zall.at[z], zall.at[z], za_s.at[d], za_r.at[d], ring_peer(d), feat)

    loop(1, RING, lambda d: zall_copy(d).start())
    loop(1, RING, lambda d: arrived(zall.at[ring_from(d)], za_s.at[d], za_r.at[d]))
    for k in range(RING):
        plane_s[k * part_a : (k + 1) * part_a, :] = zall[k, 0:part_a, :].astype(BF16)
    plane_s[chunk_a:, :] = zall[:, part_a:part, :].reshape(chunk_b, 128).astype(BF16)

    def all_copy(d):
        return remote(plane_s, plane_all.at[xy], pa_s.at[d], pa_r.at[d], plane_at(d) * RING + z, feat)

    loop(1, planes, lambda d: all_copy(d).start())
    plane_all[xy] = plane_s[...]

    loop(1, planes, lambda d: arrived(far_r.at[plane_from(d)], fb_s.at[d], fb_r.at[d]))
    for at in range(RING):
        k = ORDER[at]
        pick = hot32(asked_z[:, k : k + 1] == lane32)
        rows = far_r[:, at * QUOTA : (at + 1) * QUOTA, :].reshape(planes * QUOTA, HALF)
        zfar_s[k] = mm(pick, rows, TN)[0:COARSE].astype(BF16)

    def zfar_copy(d):
        return remote(zfar_s.at[d], zfar_r.at[d], zf_s.at[d], zf_r.at[d], ring_peer(d), feat)

    loop(1, RING, lambda d: zfar_copy(d).start())
    zfar_r[0] = zfar_s[0]
    back_below.wait()
    back_up.wait()
    loop(1, RING, lambda d: arrived(zfar_r.at[d], zf_s.at[d], zf_r.at[d]))
    head = zfar_r[0].astype(F32)
    for k in range(1, RING):
        head = head + zfar_r[k].astype(F32)
    head = head + dtab[HALO : HALO + COARSE, :] + rim_r[0, 0:COARSE, :].astype(F32)
    rest = dtab[HALO + COARSE : 2 * HALO, :] + rim_r[0, COARSE:HALO, :].astype(F32)
    end = dtab[ROWS : ROWS + HALO, :] + rim_r[1].astype(F32)
    send_grad = jnp.concatenate([head, rest, dtab[2 * HALO : ROWS, :], end], axis=0).astype(BF16)
    terms = back[...] + mm(send_grad, send_w[...], NT)
    back_s[0] = terms[:, 0:HALF]
    back_s[1] = terms[:, HALF:]
    swap_back = remote(back_s.at[other], back_r, os_s.at[5], os_r.at[5], me, other)
    swap_back.start()
    swap_back.wait()
    grad_nodes[...] = (cots[feat].astype(F32) + back_s[feat] + back_r[...]).astype(BF16)

    loop(1, planes, lambda d: arrived(plane_all.at[plane_from(d)], pa_s.at[d], pa_r.at[d]))
    weights_out[...] = plane_all[...]

    loop(1, planes, lambda d: list_copy(d).wait_send())
    loop(1, RING, lambda d: coarse_copy(d).wait_send())
    for g in range(len(GROUPS)):
        loop(1, planes, lambda d: plane_copy(g, d).wait_send())
    loop(1, planes, lambda d: wire_copy(wire_a, wire_ar, wa_s, wa_r, d).wait_send())
    loop(1, planes, lambda d: wire_copy(wire_b, wire_br, wb_s, wb_r, d).wait_send())
    loop(1, planes, lambda d: far_copy(d).wait_send())
    loop(1, planes, lambda d: all_copy(d).wait_send())
    loop(1, RING, lambda d: zsum_copy(d).wait_send())
    loop(1, RING, lambda d: zall_copy(d).wait_send())
    loop(1, RING, lambda d: zfar_copy(d).wait_send())


def layer(n_patch, *args):
    planes = n_patch // RING
    table_rows = NEAR + n_patch * QUOTA
    tiles = pl.cdiv(table_rows, TILE)
    padded = tiles * TILE
    n_items = pl.cdiv(BLOCKS + tiles - 1, UNROLL) * UNROLL
    chunk_a, chunk_b = 2048 // planes, 1024 // planes
    part = (chunk_a + chunk_b) // RING
    vmem = pl.BlockSpec(memory_space=pltpu.VMEM)
    anyspace = pl.BlockSpec(memory_space=pl.ANY)
    dma = pltpu.SemaphoreType.DMA

    def both(*shape):
        return [dma(shape), dma(shape)]

    return pl.pallas_call(
        functools.partial(layer_kernel, n_patch),
        out_shape=(
            jax.ShapeDtypeStruct((ROWS, HALF), BF16),
            jax.ShapeDtypeStruct((ROWS, HALF), BF16),
            jax.ShapeDtypeStruct((planes, chunk_a + chunk_b, 128), BF16),
            jax.ShapeDtypeStruct((1, HALF), F32),
        ),
        in_specs=[vmem] * 4 + [anyspace] * 5,
        out_specs=(vmem,) * 4,
        scratch_shapes=[
            pltpu.VMEM((2, table_rows, HALF), BF16),
            pltpu.VMEM((2, ROWS, HALF), BF16),
            pltpu.VMEM((2 * HALF, HALF), BF16),
            pltpu.VMEM((2 * HALF, HALF), BF16),
            pltpu.VMEM((HALF, 2 * HALF), BF16),
            pltpu.VMEM((planes * QUOTA, 128), I32),
            pltpu.VMEM((planes * QUOTA, 128), I32),
            pltpu.VMEM((RING, HALO, HALF), BF16),
            pltpu.VMEM((planes, PER, HALF), BF16),
            pltpu.VMEM((PAIRS, 128), I32),
            pltpu.VMEM((128, 128), I32),
            pltpu.VMEM((8, 128), I32),
            pltpu.SMEM((8, 128), I32),
            pltpu.VMEM((BLOCKS, BLOCK, 128), I16),
            pltpu.VMEM((BLOCKS, BLOCK, 128), I16),
            pltpu.VMEM((PAIRS, 128), I32),
            pltpu.VMEM((BLOCKS, 8, 128), I32),
            pltpu.VMEM((tiles + 1, TILE, HALF), BF16),
            pltpu.VMEM((ROWS, 2 * HALF), BF16),
            pltpu.VMEM((ROWS, HALF), F32),
            pltpu.VMEM((BLOCKS, BLOCK, HALF), F32),
            pltpu.VMEM((BLOCKS, BLOCK, HALF), BF16),
            pltpu.VMEM((n_items, BLOCK, HALF), F32),
            pltpu.VMEM((SPAN, 2 * HALF), BF16),
            pltpu.VMEM((SPAN, 2 * HALF), BF16),
            pltpu.VMEM((ROWS, 2 * HALF), F32),
            pltpu.VMEM((padded, HALF), F32),
            pltpu.VMEM((n_patch * QUOTA, HALF), BF16),
            pltpu.VMEM((2, HALO, HALF), BF16),
            pltpu.VMEM((2, ROWS, HALF), F32),
            pltpu.VMEM((ROWS, HALF), F32),
            pltpu.VMEM((ROWS, 2 * HALF), F32),
            pltpu.VMEM((2, ROWS, HALF), F32),
            pltpu.VMEM((ROWS, HALF), F32),
            pltpu.VMEM((planes, chunk_a + 16, 128), BF16),
            pltpu.VMEM((planes, chunk_b, 128), BF16),
            pltpu.VMEM((planes, chunk_a + 16, 128), BF16),
            pltpu.VMEM((planes, chunk_b, 128), BF16),
            pltpu.VMEM((planes, PER, HALF), BF16),
            pltpu.VMEM((2, HALO, HALF), BF16),
            pltpu.VMEM((RING, COARSE, HALF), BF16),
            pltpu.VMEM((RING, COARSE, HALF), BF16),
            pltpu.VMEM((RING, part + 8, 128), F32),
            pltpu.VMEM((RING, part + 8, 128), F32),
            pltpu.VMEM((RING, part, 128), F32),
            pltpu.VMEM((chunk_a + chunk_b, 128), BF16),
            pltpu.VMEM((planes, chunk_a + chunk_b, 128), BF16),
            dma((9,)),
            *both(RING), *both(planes), *both(len(GROUPS), planes), *both(planes), *both(2), *both(6),
            *both(planes), *both(planes), *both(planes), *both(2), *both(RING), *both(RING), *both(RING), *both(planes),
        ],
        compiler_params=pltpu.CompilerParams(
            collective_id=0, has_side_effects=True, vmem_limit_bytes=60 * 2**20
        ),
        name="layer",
    )(*args)


def finish_kernel(chunk_a, updated, grad_nodes, weights, bias, updated_o, grad_nodes_o, g_send, g_recv, g_out, g_bias):
    updated_o[...] = updated[...]
    grad_nodes_o[...] = grad_nodes[...]
    g_bias[...] = bias[...]
    planes, chunk, _ = weights.shape
    chunk_b = chunk - chunk_a
    a = weights[:, 0:chunk_a, :].reshape(planes * chunk_a, 128).astype(F32)
    b = weights[:, chunk_a:, :].reshape(planes * chunk_b, 128).astype(F32)
    for m in range(2):
        lanes = slice(128 * m, 128 * (m + 1))
        g_recv[:, lanes] = a[512 * m : 512 * (m + 1)]
        g_send[:, lanes] = b[512 * m : 512 * (m + 1)]
    for m in range(4):
        g_out[:, 128 * m : 128 * (m + 1)] = a[1024 + 256 * m : 1024 + 256 * (m + 1)]


def finish(n_patch, *args):
    vmem = pl.BlockSpec(memory_space=pltpu.VMEM)
    return pl.pallas_call(
        functools.partial(finish_kernel, 2048 // (n_patch // RING)),
        out_shape=(
            jax.ShapeDtypeStruct((ROWS, HALF), BF16),
            jax.ShapeDtypeStruct((ROWS, HALF), BF16),
            jax.ShapeDtypeStruct((2 * HALF, HALF), F32),
            jax.ShapeDtypeStruct((2 * HALF, HALF), F32),
            jax.ShapeDtypeStruct((HALF, 2 * HALF), F32),
            jax.ShapeDtypeStruct((1, HALF), F32),
        ),
        in_specs=[vmem] * 4,
        out_specs=(vmem,) * 6,
        compiler_params=pltpu.CompilerParams(vmem_limit_bytes=32 * 2**20),
        name="finish",
    )(*args)


def shards(n_patch, feats, cot, send_w, recv_w, out_w, bias, sender, receiver, wanted):
    planes = n_patch // RING
    lists = wanted.reshape(planes, RING, QUOTA).transpose(0, 2, 1).reshape(planes * QUOTA, RING)
    lists = jnp.pad(jnp.concatenate([lists, lists], axis=1), ((0, 0), (0, 128 - 2 * RING)))
    parts = layer(
        n_patch, sender.reshape(PAIRS, 128), receiver.reshape(PAIRS, 128), lists, bias.reshape(1, HALF),
        feats, cot, send_w, recv_w, out_w,
    )
    updated, grad_nodes, g_send, g_recv, g_out, g_bias = finish(n_patch, *parts)
    return (updated, grad_nodes, g_send, g_recv, g_out, g_bias.reshape(HALF))


def solution(mesh):
    n_patch = mesh.shape["patch"]
    in_specs = (
        P("patch", "feat"),
        P("patch", "feat"),
        P(None, "feat"),
        P(None, "feat"),
        P("feat", None),
        P("feat"),
        P("patch"),
        P("patch"),
        P("patch", None, None),
    )
    out_specs = (
        P("patch", "feat"),
        P("patch", "feat"),
        P(None, "feat"),
        P(None, "feat"),
        P("feat", None),
        P("feat"),
    )
    return jax.shard_map(
        functools.partial(shards, n_patch), mesh=mesh, in_specs=in_specs, out_specs=out_specs, check_vma=False
    )
```

```python
import functools

import jax
import jax.numpy as jnp
from jax import lax
from jax.experimental import pallas as pl
from jax.experimental.pallas import tpu as pltpu
from jax.sharding import PartitionSpec as P

HALO = 128
COARSE = 80
QUOTA = 16
ROWS = 640
HALF = 256
EDGES = 8192
NEAR = ROWS + 2 * HALO
BLOCK = 256
BLOCKS = EDGES // BLOCK
TILE = 256
SPAN = 1024
UNROLL = 11
PAIRS = EDGES // 128
RING = 8
PER = RING * QUOTA
ORDER = (0, 1, 7, 2, 6, 3, 5, 4)
GROUPS = ((0, 1), (1, 3), (3, 8))
HALVES = ((0, 3), (3, 8))
MESH = pl.DeviceIdType.MESH
F32 = jnp.float32
BF16 = jnp.bfloat16
I32 = jnp.int32
I16 = jnp.int16
NN = (((1,), (0,)), ((), ()))
TN = (((0,), (0,)), ((), ()))
NT = (((1,), (1,)), ((), ()))


def mm(a, b, dims=NN):
    return lax.dot_general(a, b, dims, preferred_element_type=F32)


def loop(low, high, body):
    def step(i, carry):
        body(i)
        return carry

    lax.fori_loop(low, high, step, 0)


def hot(mask):
    return jnp.where(mask, BF16(1.0), BF16(0.0))


def hot32(mask):
    return jnp.where(mask, 1.0, 0.0).astype(BF16)


def down(row, rows):
    packed = jnp.broadcast_to(row, (16, 128)).astype(I16)
    return jnp.concatenate([packed] * (rows // 16), axis=0)


def rows_of(b, size=BLOCK):
    return pl.ds(pl.multiple_of(b * size, size), size)


def remote(src, dst, send, recv, patch, core):
    return pltpu.make_async_remote_copy(
        src_ref=src, dst_ref=dst, send_sem=send, recv_sem=recv,
        device_id=(patch, core), device_id_type=MESH,
    )


def sort_steps(first, last):
    return [(k, j) for k in range(first, last + 1) for j in range(k - 1, -1, -1)]


def bitonic(xs, steps):
    lane = lax.broadcasted_iota(I32, (8, 128), 1)
    sub = lax.broadcasted_iota(I32, (8, 128), 0)

    def bit(j, v):
        if j >= 13:
            return True
        if j < 3:
            return (v >> j) & 1 == 0
        if j < 6:
            return jnp.bitwise_and(sub, 1 << (j - 3)) == 0
        return jnp.bitwise_and(lane, 1 << (j - 6)) == 0

    def pick(cond, a, b):
        if isinstance(cond, bool):
            return a if cond else b
        return jnp.where(cond, a, b)

    for k, j in steps:
        out = list(xs)
        if j < 3:
            for v in range(8):
                if v & (1 << j):
                    continue
                w = v | (1 << j)
                small, large = jnp.minimum(xs[v], xs[w]), jnp.maximum(xs[v], xs[w])
                rising = bit(k, v)
                out[v], out[w] = pick(rising, small, large), pick(rising, large, small)
        else:
            axis, size, far = (0, 8, 1 << (j - 3)) if j < 6 else (1, 128, 1 << (j - 6))
            low = bit(j, 0)
            for v in range(8):
                x = xs[v]
                mate = jnp.where(low, pltpu.roll(x, size - far, axis), pltpu.roll(x, far, axis))
                rising = bit(k, v)
                if isinstance(rising, bool):
                    least = low if rising else jnp.logical_not(low)
                else:
                    least = low == rising
                out[v] = jnp.where(least, jnp.minimum(x, mate), jnp.maximum(x, mate))
        xs = out
    return xs


def layer_kernel(
    n_patch,
    sender, receiver, wanted, bias, feats, cot, send_w_in, recv_w_in, out_w_in,
    updated, grad_nodes, plane_all, bias_out,
    table, cots, send_w, recv_w, out_w, asked, asked_z, coarse, packed,
    lists, keys, turned, plan_v, plan, cols_s, cols_r, rows_k, pairs_k,
    send_s, pair_s, gsum, pre_s, gat_s, items, act_a, act_b, acc, dtab,
    far_s, rim_s, mix, mix_r, back, back_s, back_r,
    wire_a, wire_b, wire_ar, wire_br, far_r, rim_r,
    zfar_s, zfar_r, zsum_s, zsum_r, zall, plane_s, psum_s, psum_r, updated_v, nodes_v,
    loc, zs_s, zs_r, ls_s, ls_r, ps_s, ps_r, pass_s, pass_r, hs_s, hs_r, os_s, os_r,
    wa_s, wa_r, wb_s, wb_r, fb_s, fb_r, hb_s, hb_r, zf_s, zf_r, zw_s, zw_r, za_s, za_r, pa_s, pa_r, pb_s, pb_r,
):
    planes = n_patch // RING
    table_rows = NEAR + n_patch * QUOTA
    tiles = pl.cdiv(table_rows, TILE)
    padded = tiles * TILE
    n_items = pl.cdiv(BLOCKS + tiles - 1, UNROLL) * UNROLL
    own = slice(HALO, HALO + ROWS)
    me = lax.axis_index("patch")
    feat = lax.axis_index("feat")
    other = 1 - feat
    xy, z = lax.div(me, RING), lax.rem(me, RING)
    up = lax.rem(me + 1, n_patch)
    below = lax.rem(me + n_patch - 1, n_patch)

    def ring_peer(d):
        return xy * RING + lax.rem(z + d, RING)

    def plane_at(d):
        return lax.rem(xy + d, planes)

    def plane_from(d):
        return lax.rem(xy + planes - d, planes)

    def ring_from(d):
        return lax.rem(z + RING - d, RING)

    def arrived(at, send, recv):
        remote(at, at, send, recv, me, other).wait_recv()

    own_rows = table.at[feat, HALO : HALO + ROWS]
    local = [
        pltpu.make_async_copy(feats.at[0:COARSE], coarse.at[0, 0:COARSE], loc.at[0]),
        pltpu.make_async_copy(feats, own_rows, loc.at[1]),
        pltpu.make_async_copy(cot, cots.at[feat], loc.at[2]),
        pltpu.make_async_copy(send_w_in, send_w, loc.at[3]),
        pltpu.make_async_copy(recv_w_in, recv_w, loc.at[4]),
        pltpu.make_async_copy(out_w_in, out_w, loc.at[5]),
    ]
    for copy in local:
        copy.start()

    barrier = pltpu.get_barrier_semaphore()

    def greet(patch, core):
        pl.semaphore_signal(barrier, inc=1, device_id=(patch, core), device_id_type=MESH)

    loop(1, RING, lambda d: greet(ring_peer(d), feat))
    loop(1, planes, lambda d: greet(plane_at(d) * RING + z, feat))
    greet(up, feat)
    greet(below, feat)
    greet(me, other)

    grid = wanted[...]
    lane_q = lax.broadcasted_iota(I32, (QUOTA, 128), 1)
    for p in range(planes):
        first = pltpu.roll(grid, (128 - RING * p) % 128, 1) if p else grid
        lists[p * QUOTA : (p + 1) * QUOTA, :] = jnp.where(lane_q < RING, first, pltpu.roll(first, RING, 1))
    pl.semaphore_wait(barrier, planes - 1 + RING - 1 + 3)

    def coarse_copy(d):
        return remote(feats.at[0:COARSE], coarse.at[RING - d, 0:COARSE], zs_s.at[d], zs_r.at[RING - d], ring_peer(d), feat)

    def list_copy(d):
        to = plane_at(d)
        return remote(lists.at[rows_of(to, QUOTA)], asked.at[rows_of(xy, QUOTA)], ls_s.at[d], ls_r.at[d], to * RING + z, feat)

    def far_rows(p, low=0, high=RING):
        return table.at[feat, pl.ds(pl.multiple_of(NEAR + p * PER + low * QUOTA, QUOTA), (high - low) * QUOTA)]

    def plane_copy(g, d):
        low, high = GROUPS[g]
        to = plane_at(d)
        return remote(
            packed.at[to, low * QUOTA : high * QUOTA], far_rows(xy, low, high), ps_s.at[g, d], ps_r.at[g, d], to * RING + z, feat
        )

    def swap(ref, slot):
        return remote(ref, ref, os_s.at[slot], os_r.at[slot], me, other)

    loop(1, planes, lambda d: list_copy(d).start())
    for d in ORDER[1:]:
        coarse_copy(d).start()
    low_rim = table.at[feat, 0:HALO]
    high_rim = table.at[feat, HALO + ROWS : NEAR]
    to_up = remote(feats.at[ROWS - HALO : ROWS], low_rim, hs_s.at[0], hs_r.at[0], up, feat)
    to_below = remote(feats.at[0:HALO], high_rim, hs_s.at[1], hs_r.at[1], below, feat)
    to_up.start()
    to_below.start()
    swap_own = remote(feats, own_rows, os_s.at[0], os_r.at[0], me, other)
    swap_cot = remote(cot, cots.at[feat], os_s.at[1], os_r.at[1], me, other)
    swap_own.start()
    swap_cot.start()

    lane32 = lax.broadcasted_iota(I32, (planes * QUOTA, HALO), 1)
    for k in range(RING):
        coarse[k, COARSE:HALO] = jnp.zeros((HALO - COARSE, HALF), BF16)

    def pack(g):
        for at in range(*GROUPS[g]):
            k = ORDER[at]
            pick = hot32(asked_z[:, k : k + 1] == lane32)
            rows = mm(pick, coarse[k]).astype(BF16)
            packed[:, at * QUOTA : (at + 1) * QUOTA, :] = rows.reshape(planes, QUOTA, HALF)
        loop(1, planes, lambda d: plane_copy(g, d).start())

    s = sender[...]
    j = s - NEAR
    away = jnp.bitwise_and(jnp.right_shift(j, 4) - z, RING - 1)
    spot = jnp.where(away <= 4, jnp.maximum(2 * away - 1, 0), 2 * RING - 2 * away)
    row = NEAR + j - jnp.bitwise_and(j, PER - 1) + spot * QUOTA + jnp.bitwise_and(j, QUOTA - 1)
    word = jnp.where(s < NEAR, s, row) * 1024 + receiver[...]
    xs = [word[8 * v : 8 * v + 8] for v in range(8)]

    xs = bitonic(xs, sort_steps(1, 13))
    for v in range(8):
        keys[8 * v : 8 * v + 8, :] = xs[v]
    asked[rows_of(xy, QUOTA), :] = lists[rows_of(xy, QUOTA), :]
    loop(1, planes, lambda d: arrived(asked.at[rows_of(plane_from(d), QUOTA)], ls_s.at[d], ls_r.at[d]))
    asked_z[...] = pltpu.roll(asked[...], lax.rem(128 - z, 128), 1)
    local[0].wait()
    pack(0)
    for k in ORDER[1:3]:
        arrived(coarse.at[k, 0:COARSE], zs_s.at[k], zs_r.at[k])
    pack(1)
    flat = keys[...]
    turned[...] = jnp.transpose(jnp.concatenate([flat, flat], axis=0))
    lane64 = lax.broadcasted_iota(I32, (PAIRS, 128), 1)
    rows_k[...] = jnp.where(
        lane64 < 64, turned[pl.ds(0, PAIRS, stride=2), :], turned[pl.ds(1, PAIRS, stride=2), :]
    )
    for r in range(128):
        spread = jnp.broadcast_to(flat[:, r : r + 1], (64, 128))
        rows = slice(64 * (r % 4), 64 * (r % 4) + 64)
        cols_s[r // 4, rows, :] = jnp.right_shift(spread, 10).astype(I16)
        cols_r[r // 4, rows, :] = jnp.bitwise_and(spread, 1023).astype(I16)
    for b in range(BLOCKS):
        pairs_k[b] = jnp.concatenate([rows_k[2 * b : 2 * b + 2, :], jnp.zeros((6, 128), I32)], axis=0)

    tall = lax.broadcasted_iota(I32, (128, 128), 0)
    wide = lax.broadcasted_iota(I32, (128, 128), 1)
    heads = jnp.logical_and(jnp.bitwise_and(tall, 3) == 0, tall > 0)
    first_tile = jnp.right_shift(jnp.broadcast_to(turned[:, 0:1], (128, 128)), 18)
    first_item = first_tile + jnp.right_shift(tall, 2)
    block_of = jnp.sum(jnp.where(jnp.logical_and(heads, first_item <= wide), 1, 0), axis=0, keepdims=True)
    last_of = jnp.sum(jnp.where(jnp.logical_and(heads, first_tile <= wide), 1, 0), axis=0, keepdims=True) + wide[0:1]
    first_of = jnp.right_shift(flat[0:1], 18) + jnp.right_shift(wide[0:1], 2)
    plan_v[...] = jnp.concatenate([block_of, last_of, first_of, jnp.zeros((5, 128), I32)], axis=0)
    to_scalars = pltpu.make_async_copy(plan_v, plan, loc.at[8])
    to_scalars.start()

    for k in ORDER[3:]:
        arrived(coarse.at[k, 0:COARSE], zs_s.at[k], zs_r.at[k])
    pack(2)
    own_far = pltpu.make_async_copy(packed.at[xy], far_rows(xy), loc.at[7])
    own_far.start()
    swap_far = remote(packed.at[xy], far_rows(xy), pass_s.at[0, 0], pass_r.at[0, 0], me, other)
    swap_far.start()
    to_scalars.wait()

    for copy in local[1:]:
        copy.wait()
    swap_own.wait()
    swap_cot.wait()
    pair_s[:, 0:HALF] = (
        mm(table[0, own, :], recv_w[0:HALF, :]) + mm(table[1, own, :], recv_w[HALF:, :]) + bias[...]
    ).astype(BF16)
    grad_sum = mm(cots[0], out_w[:, 0:HALF], NT) + mm(cots[1], out_w[:, HALF:], NT)
    gsum[...] = grad_sum
    pair_s[:, HALF:] = grad_sum.astype(BF16)
    acc[...] = jnp.zeros_like(acc)
    lane = lax.broadcasted_iota(I32, (BLOCK, 128), 1).astype(I16)
    sub = lax.broadcasted_iota(I32, (ROWS, 128), 0).astype(I16)
    sub_t = lax.broadcasted_iota(I32, (TILE, 128), 0).astype(I16)

    def receive(i):
        for u in range(4):
            b = 4 * i + u
            col = cols_r[b]
            pick = jnp.concatenate([hot(col == lane + I16(128 * m)) for m in range(ROWS // 128)], axis=1)
            both = mm(pick, pair_s[...])
            pre_s[b] = both[:, 0:HALF]
            gat_s[b] = both[:, HALF:].astype(BF16)

    loop(0, BLOCKS // 8, receive)

    def pass_on(p, half, slot):
        low, high = HALVES[half]
        return remote(far_rows(p, low, high), far_rows(p, low, high), pass_s.at[half, slot], pass_r.at[half, slot], me, other)

    def arrive(g, d):
        low, high = GROUPS[g]
        arrived(far_rows(plane_from(d), low, high), ps_s.at[g, d], ps_r.at[g, d])

    def hand_first(d):
        arrive(0, d)
        arrive(1, d)
        pass_on(plane_from(d), 0, d).start()

    def hand_second(d):
        arrive(2, d)
        pass_on(plane_from(d), 1, d).start()

    to_up.wait()
    swap(low_rim, 2).start()
    to_below.wait()
    swap(high_rim, 3).start()
    loop(1, planes, hand_first)
    loop(BLOCKS // 8, BLOCKS // 4, receive)
    loop(1, planes, hand_second)

    def project(start, size):
        part = slice(start, start + size)
        value = (mm(table[0, part, :], send_w[0:HALF, :]) + mm(table[1, part, :], send_w[HALF:, :])).astype(BF16)
        at = 0
        while at < size:
            t, r = divmod(start + at, TILE)
            count = min(TILE - r, size - at)
            send_s[t, r : r + count, :] = value[at : at + count]
            at += count

    swap(low_rim, 2).wait()
    swap(high_rim, 3).wait()
    project(0, NEAR)
    if padded > table_rows:
        send_s[tiles - 1, table_rows - padded + TILE :, :] = jnp.zeros((padded - table_rows, HALF), BF16)
    send_s[tiles] = jnp.zeros((TILE, HALF), BF16)
    own_far.wait()
    swap_far.wait()
    for half in range(2):
        loop(1, planes, lambda d: pass_on(plane_from(d), half, d).wait())
    for start in range(NEAR, table_rows, 1024):
        project(start, min(1024, table_rows - start))

    def gather(i):
        for u in range(UNROLL):
            at = i * UNROLL + u
            b = plan[0, at]
            before = plan[0, jnp.maximum(at - 1, 0)]
            t = at - b
            col = cols_s[b] - jnp.full((BLOCK, 128), t * TILE, I32).astype(I16)
            pick = jnp.concatenate([hot(col == lane), hot(col == lane + I16(128))], axis=1)
            part = mm(pick, send_s[t])
            keep = 1.0 - (b - before).astype(F32)
            items[at] = part + keep * items[jnp.maximum(at - 1, 0)]

    items[0] = jnp.zeros((BLOCK, HALF), F32)
    loop(0, n_items // UNROLL, gather)

    def messages(i, act):
        for u in range(SPAN // BLOCK):
            b = i * (SPAN // BLOCK) + u
            last = jnp.where(b == BLOCKS - 1, BLOCKS + tiles - 1, plan[2, jnp.minimum(4 * b + 4, 127)]) - 1
            pre = pre_s[b] + items[last]
            sig = 0.5 * jnp.tanh(0.5 * pre) + 0.5
            hidden = pre * sig
            slope = sig + hidden * (1.0 - sig)
            act[u * BLOCK : (u + 1) * BLOCK, 0:HALF] = hidden.astype(BF16)
            act[u * BLOCK : (u + 1) * BLOCK, HALF:] = slope.astype(BF16)
            gat_s[b] = (gat_s[b].astype(F32) * slope).astype(BF16)

    def collect(i, act):
        words = jnp.bitwise_and(rows_k[rows_of(i, SPAN // 128), :], 1023)
        spread = jnp.concatenate([hot(sub == down(words[m : m + 1], ROWS)) for m in range(SPAN // 128)], axis=1)
        acc[...] += mm(spread, act[...])

    act_b[...] = jnp.zeros_like(act_b)

    def two_spans(i):
        messages(2 * i, act_a)
        collect(jnp.maximum(2 * i - 1, 0), act_b)
        messages(2 * i + 1, act_b)
        collect(2 * i, act_a)

    loop(0, EDGES // SPAN // 2, two_spans)
    collect(EDGES // SPAN - 1, act_b)

    edge_sum = acc[:, 0:HALF].astype(BF16)
    recv_grad = gsum[...] * acc[:, HALF:]
    bias_part = jnp.sum(recv_grad, axis=0, keepdims=True)
    recv_grad_b = recv_grad.astype(BF16)

    chunk_a, chunk_b = 2048 // planes, 1024 // RING

    def put(wire, chunk, start, value):
        value = value.astype(BF16)
        for m in range(value.shape[1] // 128):
            at = 0
            while at < value.shape[0]:
                c, r = divmod(start + m * value.shape[0] + at, chunk)
                count = min(chunk - r, value.shape[0] - at)
                wire[c, r : r + count, :] = value[at : at + count, m * 128 : (m + 1) * 128]
                at += count

    put(
        wire_a, chunk_a, 0,
        jnp.concatenate([mm(table[0, own, :], recv_grad_b, TN), mm(table[1, own, :], recv_grad_b, TN)], axis=0),
    )
    put(wire_a, chunk_a, 1024, jnp.concatenate([mm(edge_sum, cots[0], TN), mm(edge_sum, cots[1], TN)], axis=1))
    sub16 = lax.broadcasted_iota(I32, (16, 128), 0)
    tail = jnp.where(sub16 == 0, bias_part[:, 0:128], jnp.where(sub16 == 1, bias_part[:, 128:], 0.0)).astype(BF16)
    for c in range(planes):
        wire_a[c, chunk_a : chunk_a + 16, :] = tail

    def wire_copy(src, dst, send, recv, d):
        to = plane_at(d)
        return remote(src.at[to], dst.at[xy], send.at[d], recv.at[d], to * RING + z, feat)

    loop(1, planes, lambda d: wire_copy(wire_a, wire_ar, wa_s, wa_r, d).start())
    wire_ar[xy] = wire_a[xy]
    mixed = mm(edge_sum, out_w[...])
    mix[0] = mixed[:, 0:HALF]
    mix[1] = mixed[:, HALF:]
    swap_mix = remote(mix.at[other], mix_r, os_s.at[4], os_r.at[4], me, other)
    swap_mix.start()

    def scatter(i):
        for u in range(UNROLL):
            at = i * UNROLL + u
            b = plan[0, at]
            before = plan[0, jnp.maximum(at - 1, 0)]
            t = at - b
            words = jnp.right_shift(pairs_k[b], 10) - t * TILE
            spread = jnp.concatenate([hot(sub_t == down(words[0:1], TILE)), hot(sub_t == down(words[1:2], TILE))], axis=1)
            part = mm(spread, gat_s[b])
            keep = (b - before).astype(F32)
            items[at] = part + keep * items[jnp.maximum(at - 1, 0)]

    items[0] = jnp.zeros((BLOCK, HALF), F32)
    loop(0, n_items // UNROLL, scatter)
    for t in range(tiles):
        dtab[t * TILE : (t + 1) * TILE, :] = items[plan[1, t]]

    dtab_b = dtab[0:table_rows, :].astype(BF16)
    rim_s[0] = dtab_b[0:HALO]
    rim_s[1] = dtab_b[HALO + ROWS : NEAR]
    far_s[...] = dtab_b[NEAR:table_rows]
    back_below = remote(rim_s.at[0], rim_r.at[1], hb_s.at[0], hb_r.at[0], below, feat)
    back_up = remote(rim_s.at[1], rim_r.at[0], hb_s.at[1], hb_r.at[1], up, feat)
    back_below.start()
    back_up.start()

    def far_copy(g, d):
        low, high = GROUPS[g]
        to = plane_at(d)
        src = far_s.at[pl.ds(pl.multiple_of(to * PER + low * QUOTA, QUOTA), (high - low) * QUOTA)]
        return remote(src, far_r.at[xy, low * QUOTA : high * QUOTA], fb_s.at[g, d], fb_r.at[g, d], to * RING + z, feat)

    for g in (2, 1, 0):
        loop(1, planes, lambda d: far_copy(g, d).start())
    put(wire_b, chunk_b, 0, jnp.concatenate([mm(table[0], dtab_b, TN), mm(table[1], dtab_b, TN)], axis=0))

    def wire_b_copy(d):
        to = lax.rem(z + d, RING)
        return remote(wire_b.at[to], wire_br.at[z], wb_s.at[d], wb_r.at[d], ring_peer(d), feat)

    loop(1, RING, lambda d: wire_b_copy(d).start())
    wire_br[z] = wire_b[z]
    far_r[xy] = far_s[rows_of(xy, PER), :]
    back[...] = mm(recv_grad_b, recv_w[...], NT)
    swap_mix.wait()
    updated_v[...] = (table[feat, own, :].astype(F32) + mix[feat] + mix_r[...]).astype(BF16)
    keep_updated = pltpu.make_async_copy(updated_v, updated, loc.at[6])
    keep_updated.start()

    part = chunk_a // RING
    chunk_c = chunk_b * RING // planes
    loop(1, planes, lambda d: arrived(wire_ar.at[plane_from(d)], wa_s.at[d], wa_r.at[d]))
    total = wire_ar[0].astype(F32)
    for p in range(1, planes):
        total = total + wire_ar[p].astype(F32)
    for k in range(RING):
        zsum_s[k, 0:part, :] = total[k * part : (k + 1) * part, :]
        zsum_s[k, part : part + 8, :] = total[chunk_a : chunk_a + 8, :]

    def zsum_copy(d):
        to = lax.rem(z + d, RING)
        return remote(zsum_s.at[to], zsum_r.at[z], zw_s.at[d], zw_r.at[d], ring_peer(d), feat)

    loop(1, RING, lambda d: zsum_copy(d).start())
    zsum_r[z] = zsum_s[z]

    loop(1, RING, lambda d: arrived(wire_br.at[ring_from(d)], wb_s.at[d], wb_r.at[d]))
    total = wire_br[0].astype(F32)
    for k in range(1, RING):
        total = total + wire_br[k].astype(F32)
    psum_s[...] = total.reshape(planes, chunk_b // planes, 128)

    def psum_copy(d):
        to = plane_at(d)
        return remote(psum_s.at[to], psum_r.at[xy], pb_s.at[d], pb_r.at[d], to * RING + z, feat)

    loop(1, planes, lambda d: psum_copy(d).start())
    psum_r[xy] = psum_s[xy]

    loop(1, RING, lambda d: arrived(zsum_r.at[ring_from(d)], zw_s.at[d], zw_r.at[d]))
    whole = zsum_r[0]
    for k in range(1, RING):
        whole = whole + zsum_r[k]
    bias_out[...] = jnp.concatenate([whole[part : part + 1], whole[part + 1 : part + 2]], axis=1)
    zall[z, 0:part, :] = whole[0:part]

    loop(1, planes, lambda d: arrived(psum_r.at[plane_from(d)], pb_s.at[d], pb_r.at[d]))
    whole = psum_r[0]
    for p in range(1, planes):
        whole = whole + psum_r[p]
    zall[z, part:, :] = whole

    def zall_copy(d):
        return remote(zall.at[z], zall.at[z], za_s.at[d], za_r.at[d], ring_peer(d), feat)

    loop(1, RING, lambda d: zall_copy(d).start())
    loop(1, RING, lambda d: arrived(zall.at[ring_from(d)], za_s.at[d], za_r.at[d]))
    plane_s[0:chunk_a, :] = zall[:, 0:part, :].reshape(chunk_a, 128).astype(BF16)
    plane_s[chunk_a:, :] = zall[:, part:, :].reshape(chunk_c, 128).astype(BF16)

    def all_copy(d):
        return remote(plane_s, plane_all.at[xy], pa_s.at[d], pa_r.at[d], plane_at(d) * RING + z, feat)

    loop(1, planes, lambda d: all_copy(d).start())
    keep_plane = pltpu.make_async_copy(plane_s, plane_all.at[xy], loc.at[7])
    keep_plane.start()

    def sum_owners(g):
        low, high = GROUPS[g]
        for d in range(1, planes):
            arrived(far_r.at[plane_from(d), low * QUOTA : high * QUOTA], fb_s.at[g, d], fb_r.at[g, d])
        for at in range(low, high):
            k = ORDER[at]
            pick = hot32(asked_z[:, k : k + 1] == lane32)
            rows = far_r[:, at * QUOTA : (at + 1) * QUOTA, :].reshape(planes * QUOTA, HALF)
            zfar_s[k] = mm(pick, rows, TN)[0:COARSE].astype(BF16)
            if k:
                zfar_copy(k).start()

    def zfar_copy(d):
        return remote(zfar_s.at[d], zfar_r.at[d], zf_s.at[d], zf_r.at[d], ring_peer(d), feat)

    sum_owners(2)

    sum_owners(1)
    sum_owners(0)
    zfar_r[0] = zfar_s[0]
    back_below.wait()
    back_up.wait()
    loop(1, RING, lambda d: arrived(zfar_r.at[d], zf_s.at[d], zf_r.at[d]))
    head = zfar_r[0].astype(F32)
    for k in range(1, RING):
        head = head + zfar_r[k].astype(F32)
    head = head + dtab[HALO : HALO + COARSE, :] + rim_r[0, 0:COARSE, :].astype(F32)
    rest = dtab[HALO + COARSE : 2 * HALO, :] + rim_r[0, COARSE:HALO, :].astype(F32)
    end = dtab[ROWS : ROWS + HALO, :] + rim_r[1].astype(F32)
    send_grad = jnp.concatenate([head, rest, dtab[2 * HALO : ROWS, :], end], axis=0).astype(BF16)
    terms = back[...] + mm(send_grad, send_w[...], NT)
    back_s[0] = terms[:, 0:HALF]
    back_s[1] = terms[:, HALF:]
    swap_back = remote(back_s.at[other], back_r, os_s.at[5], os_r.at[5], me, other)
    swap_back.start()
    swap_back.wait()
    nodes_v[...] = (cots[feat].astype(F32) + back_s[feat] + back_r[...]).astype(BF16)
    keep_nodes = pltpu.make_async_copy(nodes_v, grad_nodes, loc.at[0])
    keep_nodes.start()

    loop(1, planes, lambda d: arrived(plane_all.at[plane_from(d)], pa_s.at[d], pa_r.at[d]))
    keep_updated.wait()
    keep_nodes.wait()
    keep_plane.wait()

    loop(1, planes, lambda d: list_copy(d).wait_send())
    loop(1, RING, lambda d: coarse_copy(d).wait_send())
    for g in range(len(GROUPS)):
        loop(1, planes, lambda d: plane_copy(g, d).wait_send())
    loop(1, planes, lambda d: wire_copy(wire_a, wire_ar, wa_s, wa_r, d).wait_send())
    loop(1, RING, lambda d: wire_b_copy(d).wait_send())
    for g in range(len(GROUPS)):
        loop(1, planes, lambda d: far_copy(g, d).wait_send())
    loop(1, planes, lambda d: psum_copy(d).wait_send())
    loop(1, planes, lambda d: all_copy(d).wait_send())
    loop(1, RING, lambda d: zsum_copy(d).wait_send())
    loop(1, RING, lambda d: zall_copy(d).wait_send())
    loop(1, RING, lambda d: zfar_copy(d).wait_send())


def layer(n_patch, *args):
    planes = n_patch // RING
    table_rows = NEAR + n_patch * QUOTA
    tiles = pl.cdiv(table_rows, TILE)
    padded = tiles * TILE
    n_items = pl.cdiv(BLOCKS + tiles - 1, UNROLL) * UNROLL
    chunk_a, chunk_b, chunk_c = 2048 // planes, 1024 // RING, 1024 // planes
    part = chunk_a // RING
    vmem = pl.BlockSpec(memory_space=pltpu.VMEM)
    hbm = pl.BlockSpec(memory_space=pltpu.HBM)
    dma = pltpu.SemaphoreType.DMA

    def both(*shape):
        return [dma(shape), dma(shape)]

    return pl.pallas_call(
        functools.partial(layer_kernel, n_patch),
        out_shape=(
            jax.ShapeDtypeStruct((ROWS, HALF), BF16),
            jax.ShapeDtypeStruct((ROWS, HALF), BF16),
            jax.ShapeDtypeStruct((planes, chunk_a + chunk_c, 128), BF16),
            jax.ShapeDtypeStruct((1, HALF), F32),
        ),
        in_specs=[vmem] * 4 + [hbm] * 5,
        out_specs=(hbm,) * 3 + (vmem,),
        scratch_shapes=[
            pltpu.VMEM((2, table_rows, HALF), BF16),
            pltpu.VMEM((2, ROWS, HALF), BF16),
            pltpu.VMEM((2 * HALF, HALF), BF16),
            pltpu.VMEM((2 * HALF, HALF), BF16),
            pltpu.VMEM((HALF, 2 * HALF), BF16),
            pltpu.VMEM((planes * QUOTA, 128), I32),
            pltpu.VMEM((planes * QUOTA, 128), I32),
            pltpu.VMEM((RING, HALO, HALF), BF16),
            pltpu.VMEM((planes, PER, HALF), BF16),
            pltpu.VMEM((planes * QUOTA, 128), I32),
            pltpu.VMEM((PAIRS, 128), I32),
            pltpu.VMEM((128, 128), I32),
            pltpu.VMEM((8, 128), I32),
            pltpu.SMEM((8, 128), I32),
            pltpu.VMEM((BLOCKS, BLOCK, 128), I16),
            pltpu.VMEM((BLOCKS, BLOCK, 128), I16),
            pltpu.VMEM((PAIRS, 128), I32),
            pltpu.VMEM((BLOCKS, 8, 128), I32),
            pltpu.VMEM((tiles + 1, TILE, HALF), BF16),
            pltpu.VMEM((ROWS, 2 * HALF), BF16),
            pltpu.VMEM((ROWS, HALF), F32),
            pltpu.VMEM((BLOCKS, BLOCK, HALF), F32),
            pltpu.VMEM((BLOCKS, BLOCK, HALF), BF16),
            pltpu.VMEM((n_items, BLOCK, HALF), F32),
            pltpu.VMEM((SPAN, 2 * HALF), BF16),
            pltpu.VMEM((SPAN, 2 * HALF), BF16),
            pltpu.VMEM((ROWS, 2 * HALF), F32),
            pltpu.VMEM((padded, HALF), F32),
            pltpu.VMEM((n_patch * QUOTA, HALF), BF16),
            pltpu.VMEM((2, HALO, HALF), BF16),
            pltpu.VMEM((2, ROWS, HALF), F32),
            pltpu.VMEM((ROWS, HALF), F32),
            pltpu.VMEM((ROWS, 2 * HALF), F32),
            pltpu.VMEM((2, ROWS, HALF), F32),
            pltpu.VMEM((ROWS, HALF), F32),
            pltpu.VMEM((planes, chunk_a + 16, 128), BF16),
            pltpu.VMEM((RING, chunk_b, 128), BF16),
            pltpu.VMEM((planes, chunk_a + 16, 128), BF16),
            pltpu.VMEM((RING, chunk_b, 128), BF16),
            pltpu.VMEM((planes, PER, HALF), BF16),
            pltpu.VMEM((2, HALO, HALF), BF16),
            pltpu.VMEM((RING, COARSE, HALF), BF16),
            pltpu.VMEM((RING, COARSE, HALF), BF16),
            pltpu.VMEM((RING, part + 8, 128), F32),
            pltpu.VMEM((RING, part + 8, 128), F32),
            pltpu.VMEM((RING, part + chunk_b // planes, 128), F32),
            pltpu.VMEM((chunk_a + chunk_c, 128), BF16),
            pltpu.VMEM((planes, chunk_b // planes, 128), F32),
            pltpu.VMEM((planes, chunk_b // planes, 128), F32),
            pltpu.VMEM((ROWS, HALF), BF16),
            pltpu.VMEM((ROWS, HALF), BF16),
            dma((9,)),
            *both(RING), *both(planes), *both(len(GROUPS), planes), *both(2, planes), *both(2), *both(6),
            *both(planes), *both(RING), *both(len(GROUPS), planes), *both(2), *both(RING), *both(RING), *both(RING),
            *both(planes), *both(planes),
        ],
        compiler_params=pltpu.CompilerParams(
            collective_id=0, has_side_effects=True, vmem_limit_bytes=60 * 2**20
        ),
        name="layer",
    )(*args)


def finish_kernel(
    chunk_a, updated, grad_nodes, weights, bias,
    updated_o, grad_nodes_o, g_send, g_recv, g_out, g_bias,
    weights_v, sems,
):
    copies = [
        pltpu.make_async_copy(weights, weights_v, sems.at[0]),
        pltpu.make_async_copy(updated, updated_o, sems.at[1]),
        pltpu.make_async_copy(grad_nodes, grad_nodes_o, sems.at[2]),
    ]
    for copy in copies:
        copy.start()
    g_bias[...] = bias[...]
    copies[0].wait()
    a = weights_v[:, 0:chunk_a, :].reshape(2048, 128).astype(F32)
    for m in range(2):
        g_recv[:, 128 * m : 128 * (m + 1)] = a[512 * m : 512 * (m + 1)]
    for m in range(4):
        g_out[:, 128 * m : 128 * (m + 1)] = a[1024 + 256 * m : 1024 + 256 * (m + 1)]
    each = 1024 // (RING * weights_v.shape[0])
    b = weights_v[:, chunk_a:, :].astype(F32)
    for k in range(RING):
        rows = b[:, k * each : (k + 1) * each, :].reshape(1024 // RING, 128)
        at = k * (1024 // RING) % 512
        lanes = slice(128 * (k * 2 // RING), 128 * (k * 2 // RING) + 128)
        g_send[at : at + 1024 // RING, lanes] = rows
    copies[1].wait()
    copies[2].wait()


def finish(*args):
    vmem = pl.BlockSpec(memory_space=pltpu.VMEM)
    hbm = pl.BlockSpec(memory_space=pltpu.HBM)
    return pl.pallas_call(
        functools.partial(finish_kernel, 2048 // args[2].shape[0]),
        out_shape=(
            jax.ShapeDtypeStruct((ROWS, HALF), BF16),
            jax.ShapeDtypeStruct((ROWS, HALF), BF16),
            jax.ShapeDtypeStruct((2 * HALF, HALF), F32),
            jax.ShapeDtypeStruct((2 * HALF, HALF), F32),
            jax.ShapeDtypeStruct((HALF, 2 * HALF), F32),
            jax.ShapeDtypeStruct((1, HALF), F32),
        ),
        in_specs=[hbm] * 3 + [vmem],
        out_specs=(vmem,) * 6,
        scratch_shapes=[
            pltpu.VMEM(args[2].shape, BF16),
            pltpu.SemaphoreType.DMA((3,)),
        ],
        compiler_params=pltpu.CompilerParams(vmem_limit_bytes=62 * 2**20),
        name="finish",
    )(*args)


def shards(n_patch, feats, cot, send_w, recv_w, out_w, bias, sender, receiver, wanted):
    parts = layer(
        n_patch, sender.reshape(PAIRS, 128), receiver.reshape(PAIRS, 128), wanted.reshape(n_patch, QUOTA).T, bias.reshape(1, HALF),
        feats, cot, send_w, recv_w, out_w,
    )
    updated, grad_nodes, g_send, g_recv, g_out, g_bias = finish(*parts)
    return (updated, grad_nodes, g_send, g_recv, g_out, g_bias.reshape(HALF))


def solution(mesh):
    n_patch = mesh.shape["patch"]
    in_specs = (
        P("patch", "feat"),
        P("patch", "feat"),
        P(None, "feat"),
        P(None, "feat"),
        P("feat", None),
        P("feat"),
        P("patch"),
        P("patch"),
        P("patch", None, None),
    )
    out_specs = (
        P("patch", "feat"),
        P("patch", "feat"),
        P(None, "feat"),
        P(None, "feat"),
        P("feat", None),
        P("feat"),
    )
    return jax.shard_map(
        functools.partial(shards, n_patch), mesh=mesh, in_specs=in_specs, out_specs=out_specs, check_vma=False
    )
```

```python
import functools

import jax
import jax.numpy as jnp
from jax import lax
from jax.experimental import pallas as pl
from jax.experimental.pallas import tpu as pltpu
from jax.sharding import PartitionSpec as P

HALO = 128
COARSE = 80
QUOTA = 16
ROWS = 640
HALF = 256
EDGES = 8192
NEAR = ROWS + 2 * HALO
BLOCK = 256
BLOCKS = EDGES // BLOCK
TILE = 256
SPAN = 1024
UNROLL = 11
PAIRS = EDGES // 128
RING = 8
PER = RING * QUOTA
ORDER = (0, 1, 7, 2, 6, 3, 5, 4)
GROUPS = ((0, 1), (1, 3), (3, 8))
HALVES = ((0, 3), (3, 8))
MESH = pl.DeviceIdType.MESH
F32 = jnp.float32
BF16 = jnp.bfloat16
I32 = jnp.int32
I16 = jnp.int16
NN = (((1,), (0,)), ((), ()))
TN = (((0,), (0,)), ((), ()))
NT = (((1,), (1,)), ((), ()))


def mm(a, b, dims=NN):
    return lax.dot_general(a, b, dims, preferred_element_type=F32)


def loop(low, high, body):
    def step(i, carry):
        body(i)
        return carry

    lax.fori_loop(low, high, step, 0)


def hot(mask):
    return jnp.where(mask, BF16(1.0), BF16(0.0))


def hot32(mask):
    return jnp.where(mask, 1.0, 0.0).astype(BF16)


def down(row, rows):
    packed = jnp.broadcast_to(row, (16, 128)).astype(I16)
    return jnp.concatenate([packed] * (rows // 16), axis=0)


def rows_of(b, size=BLOCK):
    return pl.ds(pl.multiple_of(b * size, size), size)


def remote(src, dst, send, recv, patch, core):
    return pltpu.make_async_remote_copy(
        src_ref=src, dst_ref=dst, send_sem=send, recv_sem=recv,
        device_id=(patch, core), device_id_type=MESH,
    )


def sort_steps(first, last):
    return [(k, j) for k in range(first, last + 1) for j in range(k - 1, -1, -1)]


def bitonic(xs, steps):
    lane = lax.broadcasted_iota(I32, (8, 128), 1)
    sub = lax.broadcasted_iota(I32, (8, 128), 0)

    def bit(j, v):
        if j >= 13:
            return True
        if j < 3:
            return (v >> j) & 1 == 0
        if j < 6:
            return jnp.bitwise_and(sub, 1 << (j - 3)) == 0
        return jnp.bitwise_and(lane, 1 << (j - 6)) == 0

    def pick(cond, a, b):
        if isinstance(cond, bool):
            return a if cond else b
        return jnp.where(cond, a, b)

    for k, j in steps:
        out = list(xs)
        if j < 3:
            for v in range(8):
                if v & (1 << j):
                    continue
                w = v | (1 << j)
                small, large = jnp.minimum(xs[v], xs[w]), jnp.maximum(xs[v], xs[w])
                rising = bit(k, v)
                out[v], out[w] = pick(rising, small, large), pick(rising, large, small)
        else:
            axis, size, far = (0, 8, 1 << (j - 3)) if j < 6 else (1, 128, 1 << (j - 6))
            low = bit(j, 0)
            for v in range(8):
                x = xs[v]
                mate = jnp.where(low, pltpu.roll(x, size - far, axis), pltpu.roll(x, far, axis))
                rising = bit(k, v)
                if isinstance(rising, bool):
                    least = low if rising else jnp.logical_not(low)
                else:
                    least = low == rising
                out[v] = jnp.where(least, jnp.minimum(x, mate), jnp.maximum(x, mate))
        xs = out
    return xs


def layer_kernel(
    n_patch,
    sender, receiver, wanted, bias, feats, cot, send_w_in, recv_w_in, out_w_in,
    updated, grad_nodes, plane_all, bias_out,
    table, cots, send_w, recv_w, out_w, asked, asked_z, coarse, packed,
    lists, keys, turned, plan_v, plan, cols_s, cols_r, rows_k, pairs_k,
    send_s, pair_s, gsum, pre_s, gat_s, items, act_a, act_b, acc, dtab,
    far_s, rim_s, mix, mix_r, back, back_s, back_r,
    wire_a, wire_b, wire_ar, wire_br, far_r, rim_r,
    zfar_s, zfar_r, zsum_s, zsum_r, zall, plane_s, zsum_bs, zsum_br, zall_b, plane_bs, updated_v, nodes_v,
    loc, zs_s, zs_r, ls_s, ls_r, ps_s, ps_r, pass_s, pass_r, hs_s, hs_r, os_s, os_r,
    wa_s, wa_r, wb_s, wb_r, fb_s, fb_r, hb_s, hb_r, zf_s, zf_r, zw_s, zw_r, za_s, za_r, pa_s, pa_r, pb_s, pb_r, zx_s, zx_r, zy_s, zy_r,
):
    planes = n_patch // RING
    table_rows = NEAR + n_patch * QUOTA
    tiles = pl.cdiv(table_rows, TILE)
    padded = tiles * TILE
    n_items = pl.cdiv(BLOCKS + tiles - 1, UNROLL) * UNROLL
    own = slice(HALO, HALO + ROWS)
    me = lax.axis_index("patch")
    feat = lax.axis_index("feat")
    other = 1 - feat
    xy, z = lax.div(me, RING), lax.rem(me, RING)
    up = lax.rem(me + 1, n_patch)
    below = lax.rem(me + n_patch - 1, n_patch)

    def ring_peer(d):
        return xy * RING + lax.rem(z + d, RING)

    def plane_at(d):
        return lax.rem(xy + d, planes)

    def plane_from(d):
        return lax.rem(xy + planes - d, planes)

    def arrived(at, send, recv):
        remote(at, at, send, recv, me, other).wait_recv()

    def departed(at, send, recv):
        remote(at, at, send, recv, me, other).wait_send()

    others, around = planes - 1, RING - 1

    own_rows = table.at[feat, HALO : HALO + ROWS]
    local = [
        pltpu.make_async_copy(feats.at[0:COARSE], coarse.at[0, 0:COARSE], loc.at[0]),
        pltpu.make_async_copy(feats, own_rows, loc.at[1]),
        pltpu.make_async_copy(cot, cots.at[feat], loc.at[2]),
        pltpu.make_async_copy(send_w_in, send_w, loc.at[3]),
        pltpu.make_async_copy(recv_w_in, recv_w, loc.at[4]),
        pltpu.make_async_copy(out_w_in, out_w, loc.at[5]),
    ]
    for copy in local:
        copy.start()

    barrier = pltpu.get_barrier_semaphore()

    def greet(patch, core):
        pl.semaphore_signal(barrier, inc=1, device_id=(patch, core), device_id_type=MESH)

    loop(1, RING, lambda d: greet(ring_peer(d), feat))
    loop(1, planes, lambda d: greet(plane_at(d) * RING + z, feat))
    greet(up, feat)
    greet(below, feat)
    greet(me, other)

    grid = wanted[...]
    lane_q = lax.broadcasted_iota(I32, (QUOTA, 128), 1)
    for p in range(planes):
        first = pltpu.roll(grid, (128 - RING * p) % 128, 1) if p else grid
        lists[p * QUOTA : (p + 1) * QUOTA, :] = jnp.where(lane_q < RING, first, pltpu.roll(first, RING, 1))
    pl.semaphore_wait(barrier, planes - 1 + RING - 1 + 3)

    def coarse_copy(d):
        return remote(feats.at[0:COARSE], coarse.at[RING - d, 0:COARSE], zs_s.at[0], zs_r.at[0 if d in (1, RING - 1) else 1], ring_peer(d), feat)

    def list_copy(d):
        to = plane_at(d)
        return remote(lists.at[rows_of(to, QUOTA)], asked.at[rows_of(xy, QUOTA)], ls_s.at[0], ls_r.at[0], to * RING + z, feat)

    def far_rows(p, low=0, high=RING):
        return table.at[feat, pl.ds(pl.multiple_of(NEAR + p * PER + low * QUOTA, QUOTA), (high - low) * QUOTA)]

    def plane_copy(g, d):
        low, high = GROUPS[g]
        to = plane_at(d)
        return remote(
            packed.at[to, low * QUOTA : high * QUOTA], far_rows(xy, low, high), ps_s.at[g], ps_r.at[g], to * RING + z, feat
        )

    def swap(ref, slot):
        return remote(ref, ref, os_s.at[slot], os_r.at[slot], me, other)

    loop(1, planes, lambda d: list_copy(d).start())
    for d in ORDER[1:]:
        coarse_copy(d).start()
    low_rim = table.at[feat, 0:HALO]
    high_rim = table.at[feat, HALO + ROWS : NEAR]
    to_up = remote(feats.at[ROWS - HALO : ROWS], low_rim, hs_s.at[0], hs_r.at[0], up, feat)
    to_below = remote(feats.at[0:HALO], high_rim, hs_s.at[1], hs_r.at[1], below, feat)
    to_up.start()
    to_below.start()
    swap_own = remote(feats, own_rows, os_s.at[0], os_r.at[0], me, other)
    swap_cot = remote(cot, cots.at[feat], os_s.at[1], os_r.at[1], me, other)
    swap_own.start()
    swap_cot.start()

    lane32 = lax.broadcasted_iota(I32, (planes * QUOTA, HALO), 1)
    for k in range(RING):
        coarse[k, COARSE:HALO] = jnp.zeros((HALO - COARSE, HALF), BF16)

    def pack(g):
        for at in range(*GROUPS[g]):
            k = ORDER[at]
            pick = hot32(asked_z[:, k : k + 1] == lane32)
            rows = mm(pick, coarse[k]).astype(BF16)
            packed[:, at * QUOTA : (at + 1) * QUOTA, :] = rows.reshape(planes, QUOTA, HALF)
        loop(1, planes, lambda d: plane_copy(g, d).start())

    s = sender[...]
    j = s - NEAR
    away = jnp.bitwise_and(jnp.right_shift(j, 4) - z, RING - 1)
    spot = jnp.where(away <= 4, jnp.maximum(2 * away - 1, 0), 2 * RING - 2 * away)
    row = NEAR + j - jnp.bitwise_and(j, PER - 1) + spot * QUOTA + jnp.bitwise_and(j, QUOTA - 1)
    word = jnp.where(s < NEAR, s, row) * 1024 + receiver[...]
    xs = [word[8 * v : 8 * v + 8] for v in range(8)]

    xs = bitonic(xs, sort_steps(1, 13))
    for v in range(8):
        keys[8 * v : 8 * v + 8, :] = xs[v]
    asked[rows_of(xy, QUOTA), :] = lists[rows_of(xy, QUOTA), :]
    arrived(asked.at[0 : others * QUOTA], ls_s.at[0], ls_r.at[0])
    asked_z[...] = pltpu.roll(asked[...], lax.rem(128 - z, 128), 1)
    local[0].wait()
    pack(0)
    arrived(coarse.at[1:3, 0:COARSE], zs_s.at[0], zs_r.at[0])
    pack(1)
    flat = keys[...]
    turned[...] = jnp.transpose(jnp.concatenate([flat, flat], axis=0))
    lane64 = lax.broadcasted_iota(I32, (PAIRS, 128), 1)
    rows_k[...] = jnp.where(
        lane64 < 64, turned[pl.ds(0, PAIRS, stride=2), :], turned[pl.ds(1, PAIRS, stride=2), :]
    )
    for r in range(128):
        spread = jnp.broadcast_to(flat[:, r : r + 1], (64, 128))
        rows = slice(64 * (r % 4), 64 * (r % 4) + 64)
        cols_s[r // 4, rows, :] = jnp.right_shift(spread, 10).astype(I16)
        cols_r[r // 4, rows, :] = jnp.bitwise_and(spread, 1023).astype(I16)
    for b in range(BLOCKS):
        pairs_k[b] = jnp.concatenate([rows_k[2 * b : 2 * b + 2, :], jnp.zeros((6, 128), I32)], axis=0)

    tall = lax.broadcasted_iota(I32, (128, 128), 0)
    wide = lax.broadcasted_iota(I32, (128, 128), 1)
    heads = jnp.logical_and(jnp.bitwise_and(tall, 3) == 0, tall > 0)
    first_tile = jnp.right_shift(jnp.broadcast_to(turned[:, 0:1], (128, 128)), 18)
    first_item = first_tile + jnp.right_shift(tall, 2)
    block_of = jnp.sum(jnp.where(jnp.logical_and(heads, first_item <= wide), 1, 0), axis=0, keepdims=True)
    last_of = jnp.sum(jnp.where(jnp.logical_and(heads, first_tile <= wide), 1, 0), axis=0, keepdims=True) + wide[0:1]
    first_of = jnp.right_shift(flat[0:1], 18) + jnp.right_shift(wide[0:1], 2)
    plan_v[...] = jnp.concatenate([block_of, last_of, first_of, jnp.zeros((5, 128), I32)], axis=0)
    to_scalars = pltpu.make_async_copy(plan_v, plan, loc.at[8])
    to_scalars.start()

    arrived(coarse.at[2:7, 0:COARSE], zs_s.at[0], zs_r.at[1])
    pack(2)
    own_far = pltpu.make_async_copy(packed.at[xy], far_rows(xy), loc.at[7])
    own_far.start()
    swap_far = remote(packed.at[xy], far_rows(xy), pass_s.at[2], pass_r.at[2], me, other)
    swap_far.start()
    to_scalars.wait()

    for copy in local[1:]:
        copy.wait()
    swap_own.wait()
    swap_cot.wait()
    pair_s[:, 0:HALF] = (
        mm(table[0, own, :], recv_w[0:HALF, :]) + mm(table[1, own, :], recv_w[HALF:, :]) + bias[...]
    ).astype(BF16)
    grad_sum = mm(cots[0], out_w[:, 0:HALF], NT) + mm(cots[1], out_w[:, HALF:], NT)
    gsum[...] = grad_sum
    pair_s[:, HALF:] = grad_sum.astype(BF16)
    acc[...] = jnp.zeros_like(acc)
    lane = lax.broadcasted_iota(I32, (BLOCK, 128), 1).astype(I16)
    sub = lax.broadcasted_iota(I32, (ROWS, 128), 0).astype(I16)
    sub_t = lax.broadcasted_iota(I32, (TILE, 128), 0).astype(I16)

    def receive(i):
        for u in range(4):
            b = 4 * i + u
            col = cols_r[b]
            pick = jnp.concatenate([hot(col == lane + I16(128 * m)) for m in range(ROWS // 128)], axis=1)
            both = mm(pick, pair_s[...])
            pre_s[b] = both[:, 0:HALF]
            gat_s[b] = both[:, HALF:].astype(BF16)

    loop(0, BLOCKS // 8, receive)

    def pass_on(p, half):
        low, high = HALVES[half]
        return remote(far_rows(p, low, high), far_rows(p, low, high), pass_s.at[half], pass_r.at[half], me, other)

    def all_far(core, low, high):
        return table.at[core, NEAR : NEAR + others * (high - low) * QUOTA]

    to_up.wait()
    swap(low_rim, 2).start()
    to_below.wait()
    swap(high_rim, 3).start()
    for g in range(2):
        arrived(all_far(feat, *GROUPS[g]), ps_s.at[g], ps_r.at[g])
    loop(1, planes, lambda d: pass_on(plane_from(d), 0).start())
    loop(BLOCKS // 8, BLOCKS // 4, receive)
    arrived(all_far(feat, *GROUPS[2]), ps_s.at[2], ps_r.at[2])
    loop(1, planes, lambda d: pass_on(plane_from(d), 1).start())

    def project(start, size):
        part = slice(start, start + size)
        value = (mm(table[0, part, :], send_w[0:HALF, :]) + mm(table[1, part, :], send_w[HALF:, :])).astype(BF16)
        at = 0
        while at < size:
            t, r = divmod(start + at, TILE)
            count = min(TILE - r, size - at)
            send_s[t, r : r + count, :] = value[at : at + count]
            at += count

    swap(low_rim, 2).wait()
    swap(high_rim, 3).wait()
    project(0, NEAR)
    if padded > table_rows:
        send_s[tiles - 1, table_rows - padded + TILE :, :] = jnp.zeros((padded - table_rows, HALF), BF16)
    send_s[tiles] = jnp.zeros((TILE, HALF), BF16)
    own_far.wait()
    swap_far.wait()
    for half in range(2):
        departed(all_far(feat, *HALVES[half]), pass_s.at[half], pass_r.at[half])
        arrived(all_far(other, *HALVES[half]), pass_s.at[half], pass_r.at[half])
    for start in range(NEAR, table_rows, 1024):
        project(start, min(1024, table_rows - start))

    def gather(i):
        for u in range(UNROLL):
            at = i * UNROLL + u
            b = plan[0, at]
            before = plan[0, jnp.maximum(at - 1, 0)]
            t = at - b
            col = cols_s[b] - jnp.full((BLOCK, 128), t * TILE, I32).astype(I16)
            pick = jnp.concatenate([hot(col == lane), hot(col == lane + I16(128))], axis=1)
            part = mm(pick, send_s[t])
            keep = 1.0 - (b - before).astype(F32)
            items[at] = part + keep * items[jnp.maximum(at - 1, 0)]

    items[0] = jnp.zeros((BLOCK, HALF), F32)
    loop(0, n_items // UNROLL, gather)

    def messages(i, act):
        for u in range(SPAN // BLOCK):
            b = i * (SPAN // BLOCK) + u
            last = jnp.where(b == BLOCKS - 1, BLOCKS + tiles - 1, plan[2, jnp.minimum(4 * b + 4, 127)]) - 1
            pre = pre_s[b] + items[last]
            sig = 0.5 * jnp.tanh(0.5 * pre) + 0.5
            hidden = pre * sig
            slope = sig + hidden * (1.0 - sig)
            act[u * BLOCK : (u + 1) * BLOCK, 0:HALF] = hidden.astype(BF16)
            act[u * BLOCK : (u + 1) * BLOCK, HALF:] = slope.astype(BF16)
            gat_s[b] = (gat_s[b].astype(F32) * slope).astype(BF16)

    def collect(i, act):
        words = jnp.bitwise_and(rows_k[rows_of(i, SPAN // 128), :], 1023)
        spread = jnp.concatenate([hot(sub == down(words[m : m + 1], ROWS)) for m in range(SPAN // 128)], axis=1)
        acc[...] += mm(spread, act[...])

    act_b[...] = jnp.zeros_like(act_b)

    def two_spans(i):
        messages(2 * i, act_a)
        collect(jnp.maximum(2 * i - 1, 0), act_b)
        messages(2 * i + 1, act_b)
        collect(2 * i, act_a)

    loop(0, EDGES // SPAN // 2, two_spans)
    collect(EDGES // SPAN - 1, act_b)

    edge_sum = acc[:, 0:HALF].astype(BF16)
    recv_grad = gsum[...] * acc[:, HALF:]
    bias_part = jnp.sum(recv_grad, axis=0, keepdims=True)
    recv_grad_b = recv_grad.astype(BF16)

    chunk_a, chunk_b = 2048 // planes, 1024 // planes

    def put(wire, chunk, start, value):
        value = value.astype(BF16)
        for m in range(value.shape[1] // 128):
            at = 0
            while at < value.shape[0]:
                c, r = divmod(start + m * value.shape[0] + at, chunk)
                count = min(chunk - r, value.shape[0] - at)
                wire[c, r : r + count, :] = value[at : at + count, m * 128 : (m + 1) * 128]
                at += count

    put(
        wire_a, chunk_a, 0,
        jnp.concatenate([mm(table[0, own, :], recv_grad_b, TN), mm(table[1, own, :], recv_grad_b, TN)], axis=0),
    )
    put(wire_a, chunk_a, 1024, jnp.concatenate([mm(edge_sum, cots[0], TN), mm(edge_sum, cots[1], TN)], axis=1))
    sub16 = lax.broadcasted_iota(I32, (16, 128), 0)
    tail = jnp.where(sub16 == 0, bias_part[:, 0:128], jnp.where(sub16 == 1, bias_part[:, 128:], 0.0)).astype(BF16)
    for c in range(planes):
        wire_a[c, chunk_a : chunk_a + 16, :] = tail

    def wire_copy(src, dst, send, recv, d):
        to = plane_at(d)
        return remote(src.at[to], dst.at[xy], send.at[0], recv.at[0], to * RING + z, feat)

    loop(1, planes, lambda d: wire_copy(wire_a, wire_ar, wa_s, wa_r, d).start())
    wire_ar[xy] = wire_a[xy]
    mixed = mm(edge_sum, out_w[...])
    mix[0] = mixed[:, 0:HALF]
    mix[1] = mixed[:, HALF:]
    swap_mix = remote(mix.at[other], mix_r, os_s.at[4], os_r.at[4], me, other)
    swap_mix.start()

    def scatter(i):
        for u in range(UNROLL):
            at = i * UNROLL + u
            b = plan[0, at]
            before = plan[0, jnp.maximum(at - 1, 0)]
            t = at - b
            words = jnp.right_shift(pairs_k[b], 10) - t * TILE
            spread = jnp.concatenate([hot(sub_t == down(words[0:1], TILE)), hot(sub_t == down(words[1:2], TILE))], axis=1)
            part = mm(spread, gat_s[b])
            keep = (b - before).astype(F32)
            items[at] = part + keep * items[jnp.maximum(at - 1, 0)]

    items[0] = jnp.zeros((BLOCK, HALF), F32)
    loop(0, n_items // UNROLL, scatter)
    for t in range(tiles):
        dtab[t * TILE : (t + 1) * TILE, :] = items[plan[1, t]]

    dtab_b = dtab[0:table_rows, :].astype(BF16)
    put(wire_b, chunk_b, 0, jnp.concatenate([mm(table[0], dtab_b, TN), mm(table[1], dtab_b, TN)], axis=0))
    loop(1, planes, lambda d: wire_copy(wire_b, wire_br, wb_s, wb_r, d).start())
    wire_br[xy] = wire_b[xy]
    rim_s[0] = dtab_b[0:HALO]
    rim_s[1] = dtab_b[HALO + ROWS : NEAR]
    far_s[...] = dtab_b[NEAR:table_rows]
    back_below = remote(rim_s.at[0], rim_r.at[1], hb_s.at[0], hb_r.at[0], below, feat)
    back_up = remote(rim_s.at[1], rim_r.at[0], hb_s.at[1], hb_r.at[1], up, feat)
    back_below.start()
    back_up.start()

    def far_copy(g, d):
        low, high = GROUPS[g]
        to = plane_at(d)
        src = far_s.at[pl.ds(pl.multiple_of(to * PER + low * QUOTA, QUOTA), (high - low) * QUOTA)]
        return remote(src, far_r.at[xy, low * QUOTA : high * QUOTA], fb_s.at[g], fb_r.at[g], to * RING + z, feat)

    for g in (2, 1, 0):
        loop(1, planes, lambda d: far_copy(g, d).start())
    far_r[xy] = far_s[rows_of(xy, PER), :]
    back[...] = mm(recv_grad_b, recv_w[...], NT)
    swap_mix.wait()
    updated_v[...] = (table[feat, own, :].astype(F32) + mix[feat] + mix_r[...]).astype(BF16)
    keep_updated = pltpu.make_async_copy(updated_v, updated, loc.at[6])
    keep_updated.start()

    part = chunk_a // RING
    arrived(wire_ar.at[0:others], wa_s.at[0], wa_r.at[0])
    total = wire_ar[0].astype(F32)
    for p in range(1, planes):
        total = total + wire_ar[p].astype(F32)
    for k in range(RING):
        zsum_s[k, 0:part, :] = total[k * part : (k + 1) * part, :]
        zsum_s[k, part : part + 8, :] = total[chunk_a : chunk_a + 8, :]

    def zsum_copy(d):
        to = lax.rem(z + d, RING)
        return remote(zsum_s.at[to], zsum_r.at[z], zw_s.at[0], zw_r.at[0], ring_peer(d), feat)

    loop(1, RING, lambda d: zsum_copy(d).start())
    zsum_r[z] = zsum_s[z]

    arrived(zsum_r.at[0:around], zw_s.at[0], zw_r.at[0])
    whole = zsum_r[0]
    for k in range(1, RING):
        whole = whole + zsum_r[k]
    bias_out[...] = jnp.concatenate([whole[part : part + 1], whole[part + 1 : part + 2]], axis=1)
    zall[z] = whole[0:part]

    def zall_copy(d):
        return remote(zall.at[z], zall.at[z], za_s.at[0], za_r.at[0], ring_peer(d), feat)

    loop(1, RING, lambda d: zall_copy(d).start())

    arrived(wire_br.at[0:others], wb_s.at[0], wb_r.at[0])
    total = wire_br[0].astype(F32)
    for p in range(1, planes):
        total = total + wire_br[p].astype(F32)
    part_b = chunk_b // RING
    zsum_bs[...] = total.reshape(RING, part_b, 128)

    def zsum_b_copy(d):
        to = lax.rem(z + d, RING)
        return remote(zsum_bs.at[to], zsum_br.at[z], zx_s.at[0], zx_r.at[0], ring_peer(d), feat)

    loop(1, RING, lambda d: zsum_b_copy(d).start())
    zsum_br[z] = zsum_bs[z]

    arrived(zall.at[0:around], za_s.at[0], za_r.at[0])
    plane_s[...] = zall[...].reshape(chunk_a, 128).astype(BF16)

    def all_copy(d):
        return remote(
            plane_s, plane_all.at[xy, 0:chunk_a], pa_s.at[0], pa_r.at[0], plane_at(d) * RING + z, feat
        )

    loop(1, planes, lambda d: all_copy(d).start())
    keep_plane = pltpu.make_async_copy(plane_s, plane_all.at[xy, 0:chunk_a], loc.at[7])
    keep_plane.start()

    arrived(zsum_br.at[0:around], zx_s.at[0], zx_r.at[0])
    whole = zsum_br[0]
    for k in range(1, RING):
        whole = whole + zsum_br[k]
    zall_b[z] = whole

    def zall_b_copy(d):
        return remote(zall_b.at[z], zall_b.at[z], zy_s.at[0], zy_r.at[0], ring_peer(d), feat)

    loop(1, RING, lambda d: zall_b_copy(d).start())

    def sum_owners(g):
        low, high = GROUPS[g]
        arrived(far_r.at[0:others, low * QUOTA : high * QUOTA], fb_s.at[g], fb_r.at[g])
        for at in range(low, high):
            k = ORDER[at]
            pick = hot32(asked_z[:, k : k + 1] == lane32)
            rows = far_r[:, at * QUOTA : (at + 1) * QUOTA, :].reshape(planes * QUOTA, HALF)
            zfar_s[k] = mm(pick, rows, TN)[0:COARSE].astype(BF16)
            if k:
                zfar_copy(k).start()

    def zfar_copy(d):
        return remote(zfar_s.at[d], zfar_r.at[d], zf_s.at[0], zf_r.at[0], ring_peer(d), feat)

    def all_b_copy(d):
        return remote(
            plane_bs, plane_all.at[xy, chunk_a : chunk_a + chunk_b], pb_s.at[0], pb_r.at[0], plane_at(d) * RING + z, feat
        )

    sum_owners(2)
    arrived(zall_b.at[0:around], zy_s.at[0], zy_r.at[0])
    plane_bs[...] = zall_b[...].reshape(chunk_b, 128).astype(BF16)
    loop(1, planes, lambda d: all_b_copy(d).start())
    keep_plane_b = pltpu.make_async_copy(plane_bs, plane_all.at[xy, chunk_a : chunk_a + chunk_b], loc.at[8])
    keep_plane_b.start()

    sum_owners(1)
    sum_owners(0)
    zfar_r[0] = zfar_s[0]
    back_below.wait()
    back_up.wait()
    arrived(zfar_r.at[0:around], zf_s.at[0], zf_r.at[0])
    head = zfar_r[0].astype(F32)
    for k in range(1, RING):
        head = head + zfar_r[k].astype(F32)
    head = head + dtab[HALO : HALO + COARSE, :] + rim_r[0, 0:COARSE, :].astype(F32)
    rest = dtab[HALO + COARSE : 2 * HALO, :] + rim_r[0, COARSE:HALO, :].astype(F32)
    end = dtab[ROWS : ROWS + HALO, :] + rim_r[1].astype(F32)
    send_grad = jnp.concatenate([head, rest, dtab[2 * HALO : ROWS, :], end], axis=0).astype(BF16)
    terms = back[...] + mm(send_grad, send_w[...], NT)
    back_s[0] = terms[:, 0:HALF]
    back_s[1] = terms[:, HALF:]
    swap_back = remote(back_s.at[other], back_r, os_s.at[5], os_r.at[5], me, other)
    swap_back.start()
    swap_back.wait()
    nodes_v[...] = (cots[feat].astype(F32) + back_s[feat] + back_r[...]).astype(BF16)
    keep_nodes = pltpu.make_async_copy(nodes_v, grad_nodes, loc.at[0])
    keep_nodes.start()

    arrived(plane_all.at[0:others, 0:chunk_a], pa_s.at[0], pa_r.at[0])
    arrived(plane_all.at[0:others, chunk_a : chunk_a + chunk_b], pb_s.at[0], pb_r.at[0])
    keep_updated.wait()
    keep_nodes.wait()
    keep_plane.wait()
    keep_plane_b.wait()

    departed(lists.at[0 : others * QUOTA], ls_s.at[0], ls_r.at[0])
    departed(coarse.at[1:RING, 0:COARSE], zs_s.at[0], zs_r.at[0])
    for g, (low, high) in enumerate(GROUPS):
        departed(all_far(feat, low, high), ps_s.at[g], ps_r.at[g])
    departed(wire_a.at[0:others], wa_s.at[0], wa_r.at[0])
    departed(wire_b.at[0:others], wb_s.at[0], wb_r.at[0])
    for g, (low, high) in enumerate(GROUPS):
        departed(far_r.at[0:others, low * QUOTA : high * QUOTA], fb_s.at[g], fb_r.at[g])
    departed(plane_all.at[0:others, chunk_a : chunk_a + chunk_b], pb_s.at[0], pb_r.at[0])
    departed(zsum_bs.at[0:around], zx_s.at[0], zx_r.at[0])
    departed(zall_b.at[0:around], zy_s.at[0], zy_r.at[0])
    departed(plane_all.at[0:others, 0:chunk_a], pa_s.at[0], pa_r.at[0])
    departed(zsum_s.at[0:around], zw_s.at[0], zw_r.at[0])
    departed(zall.at[0:around], za_s.at[0], za_r.at[0])
    departed(zfar_s.at[0:around], zf_s.at[0], zf_r.at[0])


def layer(n_patch, *args):
    planes = n_patch // RING
    table_rows = NEAR + n_patch * QUOTA
    tiles = pl.cdiv(table_rows, TILE)
    padded = tiles * TILE
    n_items = pl.cdiv(BLOCKS + tiles - 1, UNROLL) * UNROLL
    chunk_a, chunk_b = 2048 // planes, 1024 // planes
    part = chunk_a // RING
    vmem = pl.BlockSpec(memory_space=pltpu.VMEM)
    hbm = pl.BlockSpec(memory_space=pltpu.HBM)
    dma = pltpu.SemaphoreType.DMA

    def both(*shape):
        return [dma(shape), dma(shape)]

    return pl.pallas_call(
        functools.partial(layer_kernel, n_patch),
        out_shape=(
            jax.ShapeDtypeStruct((ROWS, HALF), BF16),
            jax.ShapeDtypeStruct((ROWS, HALF), BF16),
            jax.ShapeDtypeStruct((planes, chunk_a + chunk_b, 128), BF16),
            jax.ShapeDtypeStruct((1, HALF), F32),
        ),
        in_specs=[vmem] * 4 + [hbm] * 5,
        out_specs=(hbm,) * 3 + (vmem,),
        scratch_shapes=[
            pltpu.VMEM((2, table_rows, HALF), BF16),
            pltpu.VMEM((2, ROWS, HALF), BF16),
            pltpu.VMEM((2 * HALF, HALF), BF16),
            pltpu.VMEM((2 * HALF, HALF), BF16),
            pltpu.VMEM((HALF, 2 * HALF), BF16),
            pltpu.VMEM((planes * QUOTA, 128), I32),
            pltpu.VMEM((planes * QUOTA, 128), I32),
            pltpu.VMEM((RING, HALO, HALF), BF16),
            pltpu.VMEM((planes, PER, HALF), BF16),
            pltpu.VMEM((planes * QUOTA, 128), I32),
            pltpu.VMEM((PAIRS, 128), I32),
            pltpu.VMEM((128, 128), I32),
            pltpu.VMEM((8, 128), I32),
            pltpu.SMEM((8, 128), I32),
            pltpu.VMEM((BLOCKS, BLOCK, 128), I16),
            pltpu.VMEM((BLOCKS, BLOCK, 128), I16),
            pltpu.VMEM((PAIRS, 128), I32),
            pltpu.VMEM((BLOCKS, 8, 128), I32),
            pltpu.VMEM((tiles + 1, TILE, HALF), BF16),
            pltpu.VMEM((ROWS, 2 * HALF), BF16),
            pltpu.VMEM((ROWS, HALF), F32),
            pltpu.VMEM((BLOCKS, BLOCK, HALF), F32),
            pltpu.VMEM((BLOCKS, BLOCK, HALF), BF16),
            pltpu.VMEM((n_items, BLOCK, HALF), F32),
            pltpu.VMEM((SPAN, 2 * HALF), BF16),
            pltpu.VMEM((SPAN, 2 * HALF), BF16),
            pltpu.VMEM((ROWS, 2 * HALF), F32),
            pltpu.VMEM((padded, HALF), F32),
            pltpu.VMEM((n_patch * QUOTA, HALF), BF16),
            pltpu.VMEM((2, HALO, HALF), BF16),
            pltpu.VMEM((2, ROWS, HALF), F32),
            pltpu.VMEM((ROWS, HALF), F32),
            pltpu.VMEM((ROWS, 2 * HALF), F32),
            pltpu.VMEM((2, ROWS, HALF), F32),
            pltpu.VMEM((ROWS, HALF), F32),
            pltpu.VMEM((planes, chunk_a + 16, 128), BF16),
            pltpu.VMEM((planes, chunk_b, 128), BF16),
            pltpu.VMEM((planes, chunk_a + 16, 128), BF16),
            pltpu.VMEM((planes, chunk_b, 128), BF16),
            pltpu.VMEM((planes, PER, HALF), BF16),
            pltpu.VMEM((2, HALO, HALF), BF16),
            pltpu.VMEM((RING, COARSE, HALF), BF16),
            pltpu.VMEM((RING, COARSE, HALF), BF16),
            pltpu.VMEM((RING, part + 8, 128), F32),
            pltpu.VMEM((RING, part + 8, 128), F32),
            pltpu.VMEM((RING, part, 128), F32),
            pltpu.VMEM((chunk_a, 128), BF16),
            pltpu.VMEM((RING, chunk_b // RING, 128), F32),
            pltpu.VMEM((RING, chunk_b // RING, 128), F32),
            pltpu.VMEM((RING, chunk_b // RING, 128), F32),
            pltpu.VMEM((chunk_b, 128), BF16),
            pltpu.VMEM((ROWS, HALF), BF16),
            pltpu.VMEM((ROWS, HALF), BF16),
            dma((9,)),
            *both(2), *both(1), *both(3), *both(3), *both(2), *both(6), *both(1), *both(1), *both(3), *both(2), *both(1), *both(1), *both(1), *both(1), *both(1), *both(1), *both(1),
        ],
        compiler_params=pltpu.CompilerParams(
            collective_id=0, has_side_effects=True, vmem_limit_bytes=60 * 2**20
        ),
        name="layer",
    )(*args)


def finish_kernel(
    chunk_a, updated, grad_nodes, weights, bias,
    updated_o, grad_nodes_o, g_send, g_recv, g_out, g_bias,
    weights_v, sems,
):
    copies = [
        pltpu.make_async_copy(weights, weights_v, sems.at[0]),
        pltpu.make_async_copy(updated, updated_o, sems.at[1]),
        pltpu.make_async_copy(grad_nodes, grad_nodes_o, sems.at[2]),
    ]
    for copy in copies:
        copy.start()
    g_bias[...] = bias[...]
    copies[0].wait()
    a = weights_v[:, 0:chunk_a, :].reshape(2048, 128).astype(F32)
    for m in range(2):
        g_recv[:, 128 * m : 128 * (m + 1)] = a[512 * m : 512 * (m + 1)]
    for m in range(4):
        g_out[:, 128 * m : 128 * (m + 1)] = a[1024 + 256 * m : 1024 + 256 * (m + 1)]
    b = weights_v[:, chunk_a:, :].reshape(1024, 128).astype(F32)
    for m in range(2):
        g_send[:, 128 * m : 128 * (m + 1)] = b[512 * m : 512 * (m + 1)]
    copies[1].wait()
    copies[2].wait()


def finish(*args):
    vmem = pl.BlockSpec(memory_space=pltpu.VMEM)
    hbm = pl.BlockSpec(memory_space=pltpu.HBM)
    return pl.pallas_call(
        functools.partial(finish_kernel, 2048 // args[2].shape[0]),
        out_shape=(
            jax.ShapeDtypeStruct((ROWS, HALF), BF16),
            jax.ShapeDtypeStruct((ROWS, HALF), BF16),
            jax.ShapeDtypeStruct((2 * HALF, HALF), F32),
            jax.ShapeDtypeStruct((2 * HALF, HALF), F32),
            jax.ShapeDtypeStruct((HALF, 2 * HALF), F32),
            jax.ShapeDtypeStruct((1, HALF), F32),
        ),
        in_specs=[hbm] * 3 + [vmem],
        out_specs=(vmem,) * 6,
        scratch_shapes=[
            pltpu.VMEM(args[2].shape, BF16),
            pltpu.SemaphoreType.DMA((3,)),
        ],
        compiler_params=pltpu.CompilerParams(vmem_limit_bytes=62 * 2**20),
        name="finish",
    )(*args)


def shards(n_patch, feats, cot, send_w, recv_w, out_w, bias, sender, receiver, wanted):
    parts = layer(
        n_patch, sender.reshape(PAIRS, 128), receiver.reshape(PAIRS, 128), wanted.reshape(n_patch, QUOTA).T, bias.reshape(1, HALF),
        feats, cot, send_w, recv_w, out_w,
    )
    updated, grad_nodes, g_send, g_recv, g_out, g_bias = finish(*parts)
    return (updated, grad_nodes, g_send, g_recv, g_out, g_bias.reshape(HALF))


def solution(mesh):
    n_patch = mesh.shape["patch"]
    in_specs = (
        P("patch", "feat"),
        P("patch", "feat"),
        P(None, "feat"),
        P(None, "feat"),
        P("feat", None),
        P("feat"),
        P("patch"),
        P("patch"),
        P("patch", None, None),
    )
    out_specs = (
        P("patch", "feat"),
        P("patch", "feat"),
        P(None, "feat"),
        P(None, "feat"),
        P("feat", None),
        P("feat"),
    )
    return jax.shard_map(
        functools.partial(shards, n_patch), mesh=mesh, in_specs=in_specs, out_specs=out_specs, check_vma=False
    )
```

```python
import functools

import jax
import jax.numpy as jnp
from jax import lax
from jax.experimental import pallas as pl
from jax.experimental.pallas import tpu as pltpu
from jax.sharding import PartitionSpec as P

HALO = 128
COARSE = 80
QUOTA = 16
ROWS = 640
HALF = 256
EDGES = 8192
NEAR = ROWS + 2 * HALO
BLOCK = 256
BLOCKS = EDGES // BLOCK
TILE = 256
SPAN = 1024
UNROLL = 11
PAIRS = EDGES // 128
RING = 8
PER = RING * QUOTA
ORDER = (0, 1, 7, 2, 6, 3, 5, 4)
GROUPS = ((0, 1), (1, 3), (3, 5), (5, 8))
HALVES = ((0, 5), (5, 8))
MESH = pl.DeviceIdType.MESH
F32 = jnp.float32
BF16 = jnp.bfloat16
I32 = jnp.int32
I16 = jnp.int16
NN = (((1,), (0,)), ((), ()))
TN = (((0,), (0,)), ((), ()))
NT = (((1,), (1,)), ((), ()))


def mm(a, b, dims=NN):
    return lax.dot_general(a, b, dims, preferred_element_type=F32)


def loop(low, high, body):
    def step(i, carry):
        body(i)
        return carry

    lax.fori_loop(low, high, step, 0)


def hot(mask):
    return jnp.where(mask, BF16(1.0), BF16(0.0))


def hot32(mask):
    return jnp.where(mask, 1.0, 0.0).astype(BF16)


def down(row, rows):
    packed = jnp.broadcast_to(row, (16, 128)).astype(I16)
    return jnp.concatenate([packed] * (rows // 16), axis=0)


def rows_of(b, size=BLOCK):
    return pl.ds(pl.multiple_of(b * size, size), size)


def remote(src, dst, send, recv, patch, core):
    return pltpu.make_async_remote_copy(
        src_ref=src, dst_ref=dst, send_sem=send, recv_sem=recv,
        device_id=(patch, core), device_id_type=MESH,
    )


def sort_steps(first, last):
    return [(k, j) for k in range(first, last + 1) for j in range(k - 1, -1, -1)]


def bitonic(xs, steps):
    lane = lax.broadcasted_iota(I32, (8, 128), 1)
    sub = lax.broadcasted_iota(I32, (8, 128), 0)

    def bit(j, v):
        if j >= 13:
            return True
        if j < 3:
            return (v >> j) & 1 == 0
        if j < 6:
            return jnp.bitwise_and(sub, 1 << (j - 3)) == 0
        return jnp.bitwise_and(lane, 1 << (j - 6)) == 0

    def pick(cond, a, b):
        if isinstance(cond, bool):
            return a if cond else b
        return jnp.where(cond, a, b)

    for k, j in steps:
        out = list(xs)
        if j < 3:
            for v in range(8):
                if v & (1 << j):
                    continue
                w = v | (1 << j)
                small, large = jnp.minimum(xs[v], xs[w]), jnp.maximum(xs[v], xs[w])
                rising = bit(k, v)
                out[v], out[w] = pick(rising, small, large), pick(rising, large, small)
        else:
            axis, size, far = (0, 8, 1 << (j - 3)) if j < 6 else (1, 128, 1 << (j - 6))
            low = bit(j, 0)
            for v in range(8):
                x = xs[v]
                mate = jnp.where(low, pltpu.roll(x, size - far, axis), pltpu.roll(x, far, axis))
                rising = bit(k, v)
                if isinstance(rising, bool):
                    least = low if rising else jnp.logical_not(low)
                else:
                    least = low == rising
                out[v] = jnp.where(least, jnp.minimum(x, mate), jnp.maximum(x, mate))
        xs = out
    return xs


def layer_kernel(
    n_patch,
    sender, receiver, wanted, bias, feats, cot, send_w_in, recv_w_in, out_w_in,
    updated, grad_nodes, plane_all, bias_out,
    table, cots, send_w, recv_w, out_w, asked, asked_z, coarse, packed,
    lists, picks, keys, turned, plan_v, plan, cols_s, cols_r, rows_k, pairs_k,
    send_s, pair_s, gsum, pre_s, gat_s, items, act_a, act_b, acc, dtab,
    far_s, rim_s, mix, mix_r, back, back_s, back_r,
    wire_a, wire_b, wire_ar, wire_br, far_r, rim_r,
    zfar_s, zfar_r, zsum_s, zsum_r, zall, plane_s, zsum_bs, zsum_br, plane_bs, updated_v, nodes_v,
    loc, zs_s, zs_r, ls_s, ls_r, ps_s, ps_r, pass_s, pass_r, hs_s, hs_r, os_s, os_r,
    wa_s, wa_r, wb_s, wb_r, fb_s, fb_r, hb_s, hb_r, zf_s, zf_r, zw_s, zw_r, za_s, za_r, pa_s, pa_r, pb_s, pb_r, zx_s, zx_r,
):
    planes = n_patch // RING
    table_rows = NEAR + n_patch * QUOTA
    tiles = pl.cdiv(table_rows, TILE)
    padded = tiles * TILE
    n_items = pl.cdiv(BLOCKS + tiles - 1, UNROLL) * UNROLL
    own = slice(HALO, HALO + ROWS)
    me = lax.axis_index("patch")
    feat = lax.axis_index("feat")
    other = 1 - feat
    xy, z = lax.div(me, RING), lax.rem(me, RING)
    up = lax.rem(me + 1, n_patch)
    below = lax.rem(me + n_patch - 1, n_patch)

    def ring_peer(d):
        return xy * RING + lax.rem(z + d, RING)

    def plane_at(d):
        return lax.rem(xy + d, planes)

    def plane_from(d):
        return lax.rem(xy + planes - d, planes)

    def arrived(at, send, recv):
        remote(at, at, send, recv, me, other).wait_recv()

    def departed(at, send, recv):
        remote(at, at, send, recv, me, other).wait_send()

    others, around = planes - 1, RING - 1

    own_rows = table.at[feat, HALO : HALO + ROWS]
    local = [
        pltpu.make_async_copy(feats.at[0:COARSE], coarse.at[0, 0:COARSE], loc.at[0]),
        pltpu.make_async_copy(feats, own_rows, loc.at[1]),
        pltpu.make_async_copy(cot, cots.at[feat], loc.at[2]),
        pltpu.make_async_copy(send_w_in, send_w, loc.at[3]),
        pltpu.make_async_copy(recv_w_in, recv_w, loc.at[4]),
        pltpu.make_async_copy(out_w_in, out_w, loc.at[5]),
    ]
    for copy in local:
        copy.start()

    barrier = pltpu.get_barrier_semaphore()

    def greet(patch, core):
        pl.semaphore_signal(barrier, inc=1, device_id=(patch, core), device_id_type=MESH)

    loop(1, RING, lambda d: greet(ring_peer(d), feat))
    loop(1, planes, lambda d: greet(plane_at(d) * RING + z, feat))
    greet(up, feat)
    greet(below, feat)
    greet(me, other)

    grid = wanted[...]
    lane_q = lax.broadcasted_iota(I32, (QUOTA, 128), 1)
    for p in range(planes):
        first = pltpu.roll(grid, (128 - RING * p) % 128, 1) if p else grid
        lists[p * QUOTA : (p + 1) * QUOTA, :] = jnp.where(lane_q < RING, first, pltpu.roll(first, RING, 1))
    pl.semaphore_wait(barrier, planes - 1 + RING - 1 + 3)

    def coarse_copy(d):
        return remote(feats.at[0:COARSE], coarse.at[RING - d, 0:COARSE], zs_s.at[0], zs_r.at[min(d, RING - d, 3) - 1], ring_peer(d), feat)

    def list_copy(d):
        to = plane_at(d)
        return remote(lists.at[rows_of(to, QUOTA)], asked.at[rows_of(xy, QUOTA)], ls_s.at[0], ls_r.at[0], to * RING + z, feat)

    def far_rows(p, low=0, high=RING):
        return table.at[feat, pl.ds(pl.multiple_of(NEAR + p * PER + low * QUOTA, QUOTA), (high - low) * QUOTA)]

    def plane_copy(g, d):
        low, high = GROUPS[g]
        to = plane_at(d)
        return remote(
            packed.at[to, low * QUOTA : high * QUOTA], far_rows(xy, low, high), ps_s.at[g], ps_r.at[g], to * RING + z, feat
        )

    def swap(ref, slot):
        return remote(ref, ref, os_s.at[slot], os_r.at[slot], me, other)

    loop(1, planes, lambda d: list_copy(d).start())
    for d in ORDER[1:]:
        coarse_copy(d).start()
    low_rim = table.at[feat, 0:HALO]
    high_rim = table.at[feat, HALO + ROWS : NEAR]
    to_up = remote(feats.at[ROWS - HALO : ROWS], low_rim, hs_s.at[0], hs_r.at[0], up, feat)
    to_below = remote(feats.at[0:HALO], high_rim, hs_s.at[1], hs_r.at[1], below, feat)
    to_up.start()
    to_below.start()
    swap_own = remote(feats, own_rows, os_s.at[0], os_r.at[0], me, other)
    swap_cot = remote(cot, cots.at[feat], os_s.at[1], os_r.at[1], me, other)
    swap_own.start()
    swap_cot.start()

    lane32 = lax.broadcasted_iota(I32, (planes * QUOTA, HALO), 1)
    for k in range(RING):
        coarse[k, COARSE:HALO] = jnp.zeros((HALO - COARSE, HALF), BF16)

    def pack(g):
        for at in range(*GROUPS[g]):
            k = ORDER[at]
            pick = hot32(asked_z[:, k : k + 1] == lane32)
            rows = mm(pick, coarse[k]).astype(BF16)
            packed[:, at * QUOTA : (at + 1) * QUOTA, :] = rows.reshape(planes, QUOTA, HALF)
        loop(1, planes, lambda d: plane_copy(g, d).start())

    s = sender[...]
    j = s - NEAR
    away = jnp.bitwise_and(jnp.right_shift(j, 4) - z, RING - 1)
    spot = jnp.where(away <= 4, jnp.maximum(2 * away - 1, 0), 2 * RING - 2 * away)
    row = NEAR + j - jnp.bitwise_and(j, PER - 1) + spot * QUOTA + jnp.bitwise_and(j, QUOTA - 1)
    word = jnp.where(s < NEAR, s, row) * 1024 + receiver[...]
    xs = [word[8 * v : 8 * v + 8] for v in range(8)]

    xs = bitonic(xs, sort_steps(1, 13))
    for v in range(8):
        keys[8 * v : 8 * v + 8, :] = xs[v]
    asked[rows_of(xy, QUOTA), :] = lists[rows_of(xy, QUOTA), :]
    arrived(asked.at[0 : others * QUOTA], ls_s.at[0], ls_r.at[0])
    asked_z[...] = pltpu.roll(asked[...], lax.rem(128 - z, 128), 1)
    local[0].wait()
    pack(0)
    arrived(coarse.at[1:3, 0:COARSE], zs_s.at[0], zs_r.at[0])
    pack(1)
    arrived(coarse.at[1:3, 0:COARSE], zs_s.at[0], zs_r.at[1])
    pack(2)
    flat = keys[...]
    turned[...] = jnp.transpose(jnp.concatenate([flat, flat], axis=0))
    lane64 = lax.broadcasted_iota(I32, (PAIRS, 128), 1)
    rows_k[...] = jnp.where(
        lane64 < 64, turned[pl.ds(0, PAIRS, stride=2), :], turned[pl.ds(1, PAIRS, stride=2), :]
    )
    for r in range(128):
        spread = jnp.broadcast_to(flat[:, r : r + 1], (64, 128))
        rows = slice(64 * (r % 4), 64 * (r % 4) + 64)
        cols_s[r // 4, rows, :] = jnp.right_shift(spread, 10).astype(I16)
        cols_r[r // 4, rows, :] = jnp.bitwise_and(spread, 1023).astype(I16)
    for b in range(BLOCKS):
        pairs_k[b] = jnp.concatenate([rows_k[2 * b : 2 * b + 2, :], jnp.zeros((6, 128), I32)], axis=0)

    tall = lax.broadcasted_iota(I32, (128, 128), 0)
    wide = lax.broadcasted_iota(I32, (128, 128), 1)
    heads = jnp.logical_and(jnp.bitwise_and(tall, 3) == 0, tall > 0)
    first_tile = jnp.right_shift(jnp.broadcast_to(turned[:, 0:1], (128, 128)), 18)
    first_item = first_tile + jnp.right_shift(tall, 2)
    block_of = jnp.sum(jnp.where(jnp.logical_and(heads, first_item <= wide), 1, 0), axis=0, keepdims=True)
    last_of = jnp.sum(jnp.where(jnp.logical_and(heads, first_tile <= wide), 1, 0), axis=0, keepdims=True) + wide[0:1]
    first_of = jnp.right_shift(flat[0:1], 18) + jnp.right_shift(wide[0:1], 2)
    plan_v[...] = jnp.concatenate([block_of, last_of, first_of, jnp.zeros((5, 128), I32)], axis=0)
    to_scalars = pltpu.make_async_copy(plan_v, plan, loc.at[8])
    to_scalars.start()
    asked_t = jnp.transpose(asked_z[...])
    tall_c = lax.broadcasted_iota(I32, (COARSE, planes * QUOTA), 0)
    for k in range(RING):
        picks[k] = hot32(asked_t[k : k + 1, :] == tall_c)

    arrived(coarse.at[3:6, 0:COARSE], zs_s.at[0], zs_r.at[2])
    pack(3)
    own_far = pltpu.make_async_copy(packed.at[xy], far_rows(xy), loc.at[7])
    own_far.start()
    swap_far = remote(packed.at[xy], far_rows(xy), pass_s.at[2], pass_r.at[2], me, other)
    swap_far.start()
    to_scalars.wait()

    for copy in local[1:]:
        copy.wait()
    swap_own.wait()
    swap_cot.wait()
    pair_s[:, 0:HALF] = (
        mm(table[0, own, :], recv_w[0:HALF, :]) + mm(table[1, own, :], recv_w[HALF:, :]) + bias[...]
    ).astype(BF16)
    grad_sum = mm(cots[0], out_w[:, 0:HALF], NT) + mm(cots[1], out_w[:, HALF:], NT)
    gsum[...] = grad_sum
    pair_s[:, HALF:] = grad_sum.astype(BF16)
    acc[...] = jnp.zeros_like(acc)
    lane = lax.broadcasted_iota(I32, (BLOCK, 128), 1).astype(I16)
    sub = lax.broadcasted_iota(I32, (ROWS, 128), 0).astype(I16)
    sub_t = lax.broadcasted_iota(I32, (TILE, 128), 0).astype(I16)

    def receive(i):
        for u in range(4):
            b = 4 * i + u
            col = cols_r[b]
            pick = jnp.concatenate([hot(col == lane + I16(128 * m)) for m in range(ROWS // 128)], axis=1)
            both = mm(pick, pair_s[...])
            pre_s[b] = both[:, 0:HALF]
            gat_s[b] = both[:, HALF:].astype(BF16)

    loop(0, BLOCKS // 8, receive)

    def pass_on(p, half):
        low, high = HALVES[half]
        return remote(far_rows(p, low, high), far_rows(p, low, high), pass_s.at[half], pass_r.at[half], me, other)

    def all_far(core, low, high):
        return table.at[core, NEAR : NEAR + others * (high - low) * QUOTA]

    to_up.wait()
    swap(low_rim, 2).start()
    to_below.wait()
    swap(high_rim, 3).start()
    for g in range(3):
        arrived(all_far(feat, *GROUPS[g]), ps_s.at[g], ps_r.at[g])
    loop(1, planes, lambda d: pass_on(plane_from(d), 0).start())
    loop(BLOCKS // 8, BLOCKS // 4, receive)
    arrived(all_far(feat, *GROUPS[3]), ps_s.at[3], ps_r.at[3])
    loop(1, planes, lambda d: pass_on(plane_from(d), 1).start())

    def project(start, size):
        part = slice(start, start + size)
        value = (mm(table[0, part, :], send_w[0:HALF, :]) + mm(table[1, part, :], send_w[HALF:, :])).astype(BF16)
        at = 0
        while at < size:
            t, r = divmod(start + at, TILE)
            count = min(TILE - r, size - at)
            send_s[t, r : r + count, :] = value[at : at + count]
            at += count

    swap(low_rim, 2).wait()
    swap(high_rim, 3).wait()
    project(0, NEAR)
    if padded > table_rows:
        send_s[tiles - 1, table_rows - padded + TILE :, :] = jnp.zeros((padded - table_rows, HALF), BF16)
    send_s[tiles] = jnp.zeros((TILE, HALF), BF16)
    own_far.wait()
    swap_far.wait()
    for half in range(2):
        departed(all_far(feat, *HALVES[half]), pass_s.at[half], pass_r.at[half])
        arrived(all_far(other, *HALVES[half]), pass_s.at[half], pass_r.at[half])
    for start in range(NEAR, table_rows, 1024):
        project(start, min(1024, table_rows - start))

    def gather(i):
        for u in range(UNROLL):
            at = i * UNROLL + u
            b = plan[0, at]
            before = plan[0, jnp.maximum(at - 1, 0)]
            t = at - b
            col = cols_s[b] - jnp.full((BLOCK, 128), t * TILE, I32).astype(I16)
            pick = jnp.concatenate([hot(col == lane), hot(col == lane + I16(128))], axis=1)
            part = mm(pick, send_s[t])
            keep = 1.0 - (b - before).astype(F32)
            items[at] = part + keep * items[jnp.maximum(at - 1, 0)]

    items[0] = jnp.zeros((BLOCK, HALF), F32)
    loop(0, n_items // UNROLL, gather)

    def messages(i, act):
        for u in range(SPAN // BLOCK):
            b = i * (SPAN // BLOCK) + u
            last = jnp.where(b == BLOCKS - 1, BLOCKS + tiles - 1, plan[2, jnp.minimum(4 * b + 4, 127)]) - 1
            pre = pre_s[b] + items[last]
            sig = 0.5 * jnp.tanh(0.5 * pre) + 0.5
            hidden = pre * sig
            slope = sig + hidden * (1.0 - sig)
            act[u * BLOCK : (u + 1) * BLOCK, 0:HALF] = hidden.astype(BF16)
            act[u * BLOCK : (u + 1) * BLOCK, HALF:] = slope.astype(BF16)
            gat_s[b] = (gat_s[b].astype(F32) * slope).astype(BF16)

    def collect(i, act):
        words = jnp.bitwise_and(rows_k[rows_of(i, SPAN // 128), :], 1023)
        spread = jnp.concatenate([hot(sub == down(words[m : m + 1], ROWS)) for m in range(SPAN // 128)], axis=1)
        acc[...] += mm(spread, act[...])

    act_b[...] = jnp.zeros_like(act_b)

    def two_spans(i):
        messages(2 * i, act_a)
        collect(jnp.maximum(2 * i - 1, 0), act_b)
        messages(2 * i + 1, act_b)
        collect(2 * i, act_a)

    loop(0, EDGES // SPAN // 2, two_spans)
    collect(EDGES // SPAN - 1, act_b)

    edge_sum = acc[:, 0:HALF].astype(BF16)
    recv_grad = gsum[...] * acc[:, HALF:]
    bias_part = jnp.sum(recv_grad, axis=0, keepdims=True)
    recv_grad_b = recv_grad.astype(BF16)

    chunk_a, chunk_b = 2048 // planes, 1024 // planes

    def put(wire, chunk, start, value):
        value = value.astype(BF16)
        for m in range(value.shape[1] // 128):
            at = 0
            while at < value.shape[0]:
                c, r = divmod(start + m * value.shape[0] + at, chunk)
                count = min(chunk - r, value.shape[0] - at)
                wire[c, r : r + count, :] = value[at : at + count, m * 128 : (m + 1) * 128]
                at += count

    put(
        wire_a, chunk_a, 0,
        jnp.concatenate([mm(table[0, own, :], recv_grad_b, TN), mm(table[1, own, :], recv_grad_b, TN)], axis=0),
    )
    put(wire_a, chunk_a, 1024, jnp.concatenate([mm(edge_sum, cots[0], TN), mm(edge_sum, cots[1], TN)], axis=1))
    sub16 = lax.broadcasted_iota(I32, (16, 128), 0)
    tail = jnp.where(sub16 == 0, bias_part[:, 0:128], jnp.where(sub16 == 1, bias_part[:, 128:], 0.0)).astype(BF16)
    for c in range(planes):
        wire_a[c, chunk_a : chunk_a + 16, :] = tail

    def wire_copy(src, dst, send, recv, d):
        to = plane_at(d)
        return remote(src.at[to], dst.at[xy], send.at[0], recv.at[0], to * RING + z, feat)

    loop(1, planes, lambda d: wire_copy(wire_a, wire_ar, wa_s, wa_r, d).start())
    wire_ar[xy] = wire_a[xy]
    mixed = mm(edge_sum, out_w[...])
    mix[0] = mixed[:, 0:HALF]
    mix[1] = mixed[:, HALF:]
    swap_mix = remote(mix.at[other], mix_r, os_s.at[4], os_r.at[4], me, other)
    swap_mix.start()

    def scatter(i):
        for u in range(UNROLL):
            at = i * UNROLL + u
            b = plan[0, at]
            before = plan[0, jnp.maximum(at - 1, 0)]
            t = at - b
            words = jnp.right_shift(pairs_k[b], 10) - t * TILE
            spread = jnp.concatenate([hot(sub_t == down(words[0:1], TILE)), hot(sub_t == down(words[1:2], TILE))], axis=1)
            part = mm(spread, gat_s[b])
            keep = (b - before).astype(F32)
            items[at] = part + keep * items[jnp.maximum(at - 1, 0)]

    items[0] = jnp.zeros((BLOCK, HALF), F32)
    loop(0, n_items // UNROLL, scatter)
    for t in range(tiles):
        dtab[t * TILE : (t + 1) * TILE, :] = items[plan[1, t]]

    dtab_b = dtab[0:table_rows, :].astype(BF16)
    put(wire_b, chunk_b, 0, jnp.concatenate([mm(table[0], dtab_b, TN), mm(table[1], dtab_b, TN)], axis=0))
    loop(1, planes, lambda d: wire_copy(wire_b, wire_br, wb_s, wb_r, d).start())
    wire_br[xy] = wire_b[xy]
    rim_s[0] = dtab_b[0:HALO]
    rim_s[1] = dtab_b[HALO + ROWS : NEAR]
    far_s[...] = dtab_b[NEAR:table_rows]
    back_below = remote(rim_s.at[0], rim_r.at[1], hb_s.at[0], hb_r.at[0], below, feat)
    back_up = remote(rim_s.at[1], rim_r.at[0], hb_s.at[1], hb_r.at[1], up, feat)
    back_below.start()
    back_up.start()

    def far_copy(g, d):
        low, high = GROUPS[g]
        to = plane_at(d)
        src = far_s.at[pl.ds(pl.multiple_of(to * PER + low * QUOTA, QUOTA), (high - low) * QUOTA)]
        return remote(src, far_r.at[xy, low * QUOTA : high * QUOTA], fb_s.at[g], fb_r.at[g], to * RING + z, feat)

    for g in (3, 2, 1, 0):
        loop(1, planes, lambda d: far_copy(g, d).start())
    far_r[xy] = far_s[rows_of(xy, PER), :]
    back[...] = mm(recv_grad_b, recv_w[...], NT)
    swap_mix.wait()
    updated_v[...] = (table[feat, own, :].astype(F32) + mix[feat] + mix_r[...]).astype(BF16)
    keep_updated = pltpu.make_async_copy(updated_v, updated, loc.at[6])
    keep_updated.start()

    part = chunk_a // RING
    arrived(wire_ar.at[0:others], wa_s.at[0], wa_r.at[0])
    total = wire_ar[0].astype(F32)
    for p in range(1, planes):
        total = total + wire_ar[p].astype(F32)
    for k in range(RING):
        zsum_s[k, 0:part, :] = total[k * part : (k + 1) * part, :]
        zsum_s[k, part : part + 8, :] = total[chunk_a : chunk_a + 8, :]

    def zsum_copy(d):
        to = lax.rem(z + d, RING)
        return remote(zsum_s.at[to], zsum_r.at[z], zw_s.at[0], zw_r.at[0], ring_peer(d), feat)

    loop(1, RING, lambda d: zsum_copy(d).start())
    zsum_r[z] = zsum_s[z]

    arrived(zsum_r.at[0:around], zw_s.at[0], zw_r.at[0])
    whole = zsum_r[0]
    for k in range(1, RING):
        whole = whole + zsum_r[k]
    bias_out[...] = jnp.concatenate([whole[part : part + 1], whole[part + 1 : part + 2]], axis=1)
    zall[z] = whole[0:part]

    def zall_copy(d):
        return remote(zall.at[z], zall.at[z], za_s.at[0], za_r.at[0], ring_peer(d), feat)

    loop(1, RING, lambda d: zall_copy(d).start())

    arrived(wire_br.at[0:others], wb_s.at[0], wb_r.at[0])
    total = wire_br[0].astype(F32)
    for p in range(1, planes):
        total = total + wire_br[p].astype(F32)
    zsum_bs[...] = total.astype(BF16)

    def zsum_b_copy(d):
        return remote(zsum_bs, zsum_br.at[z], zx_s.at[0], zx_r.at[0], ring_peer(d), feat)

    loop(1, RING, lambda d: zsum_b_copy(d).start())
    zsum_br[z] = zsum_bs[...]

    arrived(zall.at[0:around], za_s.at[0], za_r.at[0])
    plane_s[...] = zall[...].reshape(chunk_a, 128).astype(BF16)

    def all_copy(d):
        return remote(
            plane_s, plane_all.at[xy, 0:chunk_a], pa_s.at[0], pa_r.at[0], plane_at(d) * RING + z, feat
        )

    loop(1, planes, lambda d: all_copy(d).start())
    keep_plane = pltpu.make_async_copy(plane_s, plane_all.at[xy, 0:chunk_a], loc.at[7])
    keep_plane.start()

    arrived(zsum_br.at[0:around], zx_s.at[0], zx_r.at[0])
    whole = zsum_br[0].astype(F32)
    for k in range(1, RING):
        whole = whole + zsum_br[k].astype(F32)
    plane_bs[...] = whole.astype(BF16)

    def all_b_copy(d):
        return remote(
            plane_bs, plane_all.at[xy, chunk_a : chunk_a + chunk_b], pb_s.at[0], pb_r.at[0], plane_at(d) * RING + z, feat
        )

    loop(1, planes, lambda d: all_b_copy(d).start())
    keep_plane_b = pltpu.make_async_copy(plane_bs, plane_all.at[xy, chunk_a : chunk_a + chunk_b], loc.at[8])
    keep_plane_b.start()

    back_below.wait()
    back_up.wait()
    rest = dtab[HALO + COARSE : 2 * HALO, :] + rim_r[0, COARSE:HALO, :].astype(F32)
    end = dtab[ROWS : ROWS + HALO, :] + rim_r[1].astype(F32)
    send_grad = jnp.concatenate([rest, dtab[2 * HALO : ROWS, :], end], axis=0).astype(BF16)
    terms = back[COARSE:, :] + mm(send_grad, send_w[...], NT)
    back_s[0, COARSE:] = terms[:, 0:HALF]
    back_s[1, COARSE:] = terms[:, HALF:]
    swap_back = remote(back_s.at[other, COARSE:ROWS], back_r.at[COARSE:ROWS], os_s.at[5], os_r.at[5], me, other)
    swap_back.start()

    def sum_owners(g):
        low, high = GROUPS[g]
        arrived(far_r.at[0:others, low * QUOTA : high * QUOTA], fb_s.at[g], fb_r.at[g])
        for at in range(low, high):
            k = ORDER[at]
            rows = far_r[:, at * QUOTA : (at + 1) * QUOTA, :].reshape(planes * QUOTA, HALF)
            zfar_s[k] = mm(picks[k], rows).astype(BF16)
            if k:
                zfar_copy(k).start()

    def zfar_copy(d):
        return remote(zfar_s.at[d], zfar_r.at[d], zf_s.at[0], zf_r.at[0], ring_peer(d), feat)

    sum_owners(3)
    sum_owners(2)
    sum_owners(1)
    sum_owners(0)
    zfar_r[0] = zfar_s[0]
    arrived(zfar_r.at[0:around], zf_s.at[0], zf_r.at[0])
    head = zfar_r[0].astype(F32)
    for k in range(1, RING):
        head = head + zfar_r[k].astype(F32)
    head = head + dtab[HALO : HALO + COARSE, :] + rim_r[0, 0:COARSE, :].astype(F32)
    terms = back[0:COARSE, :] + mm(head.astype(BF16), send_w[...], NT)
    back_s[0, 0:COARSE] = terms[:, 0:HALF]
    back_s[1, 0:COARSE] = terms[:, HALF:]
    swap_head = remote(back_s.at[other, 0:COARSE], back_r.at[0:COARSE], os_s.at[6], os_r.at[6], me, other)
    swap_head.start()
    swap_back.wait()
    nodes_v[COARSE:, :] = (cots[feat, COARSE:, :].astype(F32) + back_s[feat, COARSE:] + back_r[COARSE:, :]).astype(BF16)
    keep_rest = pltpu.make_async_copy(nodes_v.at[COARSE:ROWS], grad_nodes.at[COARSE:ROWS], loc.at[1])
    keep_rest.start()
    swap_head.wait()
    nodes_v[0:COARSE, :] = (cots[feat, 0:COARSE, :].astype(F32) + back_s[feat, 0:COARSE] + back_r[0:COARSE, :]).astype(BF16)
    keep_nodes = pltpu.make_async_copy(nodes_v.at[0:COARSE], grad_nodes.at[0:COARSE], loc.at[0])
    keep_nodes.start()

    arrived(plane_all.at[0:others, 0:chunk_a], pa_s.at[0], pa_r.at[0])
    arrived(plane_all.at[0:others, chunk_a : chunk_a + chunk_b], pb_s.at[0], pb_r.at[0])
    keep_updated.wait()
    keep_nodes.wait()
    keep_rest.wait()
    keep_plane.wait()
    keep_plane_b.wait()

    departed(lists.at[0 : others * QUOTA], ls_s.at[0], ls_r.at[0])
    departed(coarse.at[1:RING, 0:COARSE], zs_s.at[0], zs_r.at[0])
    for g, (low, high) in enumerate(GROUPS):
        departed(all_far(feat, low, high), ps_s.at[g], ps_r.at[g])
    departed(wire_a.at[0:others], wa_s.at[0], wa_r.at[0])
    departed(wire_b.at[0:others], wb_s.at[0], wb_r.at[0])
    for g, (low, high) in enumerate(GROUPS):
        departed(far_r.at[0:others, low * QUOTA : high * QUOTA], fb_s.at[g], fb_r.at[g])
    departed(plane_all.at[0:others, chunk_a : chunk_a + chunk_b], pb_s.at[0], pb_r.at[0])
    departed(zsum_br.at[0:around], zx_s.at[0], zx_r.at[0])
    departed(plane_all.at[0:others, 0:chunk_a], pa_s.at[0], pa_r.at[0])
    departed(zsum_s.at[0:around], zw_s.at[0], zw_r.at[0])
    departed(zall.at[0:around], za_s.at[0], za_r.at[0])
    departed(zfar_s.at[0:around], zf_s.at[0], zf_r.at[0])


def layer(n_patch, *args):
    planes = n_patch // RING
    table_rows = NEAR + n_patch * QUOTA
    tiles = pl.cdiv(table_rows, TILE)
    padded = tiles * TILE
    n_items = pl.cdiv(BLOCKS + tiles - 1, UNROLL) * UNROLL
    chunk_a, chunk_b = 2048 // planes, 1024 // planes
    part = chunk_a // RING
    vmem = pl.BlockSpec(memory_space=pltpu.VMEM)
    hbm = pl.BlockSpec(memory_space=pltpu.HBM)
    dma = pltpu.SemaphoreType.DMA

    def both(*shape):
        return [dma(shape), dma(shape)]

    return pl.pallas_call(
        functools.partial(layer_kernel, n_patch),
        out_shape=(
            jax.ShapeDtypeStruct((ROWS, HALF), BF16),
            jax.ShapeDtypeStruct((ROWS, HALF), BF16),
            jax.ShapeDtypeStruct((planes, chunk_a + chunk_b, 128), BF16),
            jax.ShapeDtypeStruct((1, HALF), F32),
        ),
        in_specs=[vmem] * 4 + [hbm] * 5,
        out_specs=(hbm,) * 3 + (vmem,),
        scratch_shapes=[
            pltpu.VMEM((2, table_rows, HALF), BF16),
            pltpu.VMEM((2, ROWS, HALF), BF16),
            pltpu.VMEM((2 * HALF, HALF), BF16),
            pltpu.VMEM((2 * HALF, HALF), BF16),
            pltpu.VMEM((HALF, 2 * HALF), BF16),
            pltpu.VMEM((planes * QUOTA, 128), I32),
            pltpu.VMEM((planes * QUOTA, 128), I32),
            pltpu.VMEM((RING, HALO, HALF), BF16),
            pltpu.VMEM((planes, PER, HALF), BF16),
            pltpu.VMEM((planes * QUOTA, 128), I32),
            pltpu.VMEM((RING, COARSE, planes * QUOTA), BF16),
            pltpu.VMEM((PAIRS, 128), I32),
            pltpu.VMEM((128, 128), I32),
            pltpu.VMEM((8, 128), I32),
            pltpu.SMEM((8, 128), I32),
            pltpu.VMEM((BLOCKS, BLOCK, 128), I16),
            pltpu.VMEM((BLOCKS, BLOCK, 128), I16),
            pltpu.VMEM((PAIRS, 128), I32),
            pltpu.VMEM((BLOCKS, 8, 128), I32),
            pltpu.VMEM((tiles + 1, TILE, HALF), BF16),
            pltpu.VMEM((ROWS, 2 * HALF), BF16),
            pltpu.VMEM((ROWS, HALF), F32),
            pltpu.VMEM((BLOCKS, BLOCK, HALF), F32),
            pltpu.VMEM((BLOCKS, BLOCK, HALF), BF16),
            pltpu.VMEM((n_items, BLOCK, HALF), F32),
            pltpu.VMEM((SPAN, 2 * HALF), BF16),
            pltpu.VMEM((SPAN, 2 * HALF), BF16),
            pltpu.VMEM((ROWS, 2 * HALF), F32),
            pltpu.VMEM((padded, HALF), F32),
            pltpu.VMEM((n_patch * QUOTA, HALF), BF16),
            pltpu.VMEM((2, HALO, HALF), BF16),
            pltpu.VMEM((2, ROWS, HALF), F32),
            pltpu.VMEM((ROWS, HALF), F32),
            pltpu.VMEM((ROWS, 2 * HALF), F32),
            pltpu.VMEM((2, ROWS, HALF), F32),
            pltpu.VMEM((ROWS, HALF), F32),
            pltpu.VMEM((planes, chunk_a + 16, 128), BF16),
            pltpu.VMEM((planes, chunk_b, 128), BF16),
            pltpu.VMEM((planes, chunk_a + 16, 128), BF16),
            pltpu.VMEM((planes, chunk_b, 128), BF16),
            pltpu.VMEM((planes, PER, HALF), BF16),
            pltpu.VMEM((2, HALO, HALF), BF16),
            pltpu.VMEM((RING, COARSE, HALF), BF16),
            pltpu.VMEM((RING, COARSE, HALF), BF16),
            pltpu.VMEM((RING, part + 8, 128), F32),
            pltpu.VMEM((RING, part + 8, 128), F32),
            pltpu.VMEM((RING, part, 128), F32),
            pltpu.VMEM((chunk_a, 128), BF16),
            pltpu.VMEM((chunk_b, 128), BF16),
            pltpu.VMEM((RING, chunk_b, 128), BF16),
            pltpu.VMEM((chunk_b, 128), BF16),
            pltpu.VMEM((ROWS, HALF), BF16),
            pltpu.VMEM((ROWS, HALF), BF16),
            dma((9,)),
            *both(3), *both(1), *both(4), *both(3), *both(2), *both(7), *both(1), *both(1), *both(4), *both(2), *both(1), *both(1), *both(1), *both(1), *both(1), *both(1),
        ],
        compiler_params=pltpu.CompilerParams(
            collective_id=0, has_side_effects=True, vmem_limit_bytes=60 * 2**20
        ),
        name="layer",
    )(*args)


def finish_kernel(
    chunk_a, updated, grad_nodes, weights, bias,
    updated_o, grad_nodes_o, g_send, g_recv, g_out, g_bias,
    a_v, b_v, updated_v, nodes_v, send_v, recv_v, out_v, sems,
):
    chunk = weights.shape[1]
    a_in = pltpu.make_async_copy(weights.at[:, 0:chunk_a], a_v, sems.at[0])
    b_in = pltpu.make_async_copy(weights.at[:, chunk_a:chunk], b_v, sems.at[1])
    updated_in = pltpu.make_async_copy(updated, updated_v, sems.at[2])
    nodes_in = pltpu.make_async_copy(grad_nodes, nodes_v, sems.at[3])
    for copy in (a_in, b_in, updated_in, nodes_in):
        copy.start()
    g_bias[...] = bias[...]
    outs = [
        pltpu.make_async_copy(recv_v, g_recv, sems.at[4]),
        pltpu.make_async_copy(out_v, g_out, sems.at[5]),
        pltpu.make_async_copy(send_v, g_send, sems.at[6]),
        pltpu.make_async_copy(updated_v, updated_o, sems.at[7]),
        pltpu.make_async_copy(nodes_v, grad_nodes_o, sems.at[8]),
    ]
    a_in.wait()
    a = a_v[...].reshape(2048, 128)
    for m in range(2):
        recv_v[:, 128 * m : 128 * (m + 1)] = a[512 * m : 512 * (m + 1)].astype(F32)
    outs[0].start()
    for m in range(4):
        out_v[:, 128 * m : 128 * (m + 1)] = a[1024 + 256 * m : 1024 + 256 * (m + 1)].astype(F32)
    outs[1].start()
    b_in.wait()
    b = b_v[...].reshape(1024, 128)
    for m in range(2):
        send_v[:, 128 * m : 128 * (m + 1)] = b[512 * m : 512 * (m + 1)].astype(F32)
    outs[2].start()
    updated_in.wait()
    outs[3].start()
    nodes_in.wait()
    outs[4].start()
    for copy in outs:
        copy.wait()


def finish(*args):
    vmem = pl.BlockSpec(memory_space=pltpu.VMEM)
    hbm = pl.BlockSpec(memory_space=pltpu.HBM)
    planes, chunk, _ = args[2].shape
    chunk_a = 2048 // planes
    return pl.pallas_call(
        functools.partial(finish_kernel, chunk_a),
        out_shape=(
            jax.ShapeDtypeStruct((ROWS, HALF), BF16),
            jax.ShapeDtypeStruct((ROWS, HALF), BF16),
            jax.ShapeDtypeStruct((2 * HALF, HALF), F32),
            jax.ShapeDtypeStruct((2 * HALF, HALF), F32),
            jax.ShapeDtypeStruct((HALF, 2 * HALF), F32),
            jax.ShapeDtypeStruct((1, HALF), F32),
        ),
        in_specs=[hbm] * 3 + [vmem],
        out_specs=(hbm,) * 5 + (vmem,),
        scratch_shapes=[
            pltpu.VMEM((planes, chunk_a, 128), BF16),
            pltpu.VMEM((planes, chunk - chunk_a, 128), BF16),
            pltpu.VMEM((ROWS, HALF), BF16),
            pltpu.VMEM((ROWS, HALF), BF16),
            pltpu.VMEM((2 * HALF, HALF), F32),
            pltpu.VMEM((2 * HALF, HALF), F32),
            pltpu.VMEM((HALF, 2 * HALF), F32),
            pltpu.SemaphoreType.DMA((9,)),
        ],
        compiler_params=pltpu.CompilerParams(vmem_limit_bytes=62 * 2**20),
        name="finish",
    )(*args)


def shards(n_patch, feats, cot, send_w, recv_w, out_w, bias, sender, receiver, wanted):
    parts = layer(
        n_patch, sender.reshape(PAIRS, 128), receiver.reshape(PAIRS, 128), wanted.reshape(n_patch, QUOTA).T, bias.reshape(1, HALF),
        feats, cot, send_w, recv_w, out_w,
    )
    updated, grad_nodes, g_send, g_recv, g_out, g_bias = finish(*parts)
    return (updated, grad_nodes, g_send, g_recv, g_out, g_bias.reshape(HALF))


def solution(mesh):
    n_patch = mesh.shape["patch"]
    in_specs = (
        P("patch", "feat"),
        P("patch", "feat"),
        P(None, "feat"),
        P(None, "feat"),
        P("feat", None),
        P("feat"),
        P("patch"),
        P("patch"),
        P("patch", None, None),
    )
    out_specs = (
        P("patch", "feat"),
        P("patch", "feat"),
        P(None, "feat"),
        P(None, "feat"),
        P("feat", None),
        P("feat"),
    )
    return jax.shard_map(
        functools.partial(shards, n_patch), mesh=mesh, in_specs=in_specs, out_specs=out_specs, check_vma=False
    )
```

```python
import functools

import jax
import jax.numpy as jnp
from jax import lax
from jax.experimental import pallas as pl
from jax.experimental.pallas import tpu as pltpu
from jax.sharding import PartitionSpec as P

HALO = 128
COARSE = 80
QUOTA = 16
ROWS = 640
HALF = 256
EDGES = 8192
NEAR = ROWS + 2 * HALO
BLOCK = 256
BLOCKS = EDGES // BLOCK
TILE = 256
SPAN = 1024
UNROLL = 11
PAIRS = EDGES // 128
RING = 8
PER = RING * QUOTA
ORDER = (0, 1, 7, 2, 6, 3, 5, 4)
GROUPS = ((0, 1), (1, 3), (3, 5), (5, 8))
HALVES = ((0, 5), (5, 8))
MESH = pl.DeviceIdType.MESH
F32 = jnp.float32
BF16 = jnp.bfloat16
I32 = jnp.int32
I16 = jnp.int16
NN = (((1,), (0,)), ((), ()))
TN = (((0,), (0,)), ((), ()))
NT = (((1,), (1,)), ((), ()))


def mm(a, b, dims=NN):
    return lax.dot_general(a, b, dims, preferred_element_type=F32)


def loop(low, high, body):
    def step(i, carry):
        body(i)
        return carry

    lax.fori_loop(low, high, step, 0)


def hot(mask):
    return jnp.where(mask, BF16(1.0), BF16(0.0))


def hot32(mask):
    return jnp.where(mask, 1.0, 0.0).astype(BF16)


def down(row, rows):
    packed = jnp.broadcast_to(row, (16, 128)).astype(I16)
    return jnp.concatenate([packed] * (rows // 16), axis=0)


def rows_of(b, size=BLOCK):
    return pl.ds(pl.multiple_of(b * size, size), size)


def remote(src, dst, send, recv, patch, core):
    return pltpu.make_async_remote_copy(
        src_ref=src, dst_ref=dst, send_sem=send, recv_sem=recv,
        device_id=(patch, core), device_id_type=MESH,
    )


def sort_steps(first, last):
    return [(k, j) for k in range(first, last + 1) for j in range(k - 1, -1, -1)]


def bitonic(xs, steps):
    lane = lax.broadcasted_iota(I32, (8, 128), 1)
    sub = lax.broadcasted_iota(I32, (8, 128), 0)

    def bit(j, v):
        if j >= 13:
            return True
        if j < 3:
            return (v >> j) & 1 == 0
        if j < 6:
            return jnp.bitwise_and(sub, 1 << (j - 3)) == 0
        return jnp.bitwise_and(lane, 1 << (j - 6)) == 0

    def pick(cond, a, b):
        if isinstance(cond, bool):
            return a if cond else b
        return jnp.where(cond, a, b)

    for k, j in steps:
        out = list(xs)
        if j < 3:
            for v in range(8):
                if v & (1 << j):
                    continue
                w = v | (1 << j)
                small, large = jnp.minimum(xs[v], xs[w]), jnp.maximum(xs[v], xs[w])
                rising = bit(k, v)
                out[v], out[w] = pick(rising, small, large), pick(rising, large, small)
        else:
            axis, size, far = (0, 8, 1 << (j - 3)) if j < 6 else (1, 128, 1 << (j - 6))
            low = bit(j, 0)
            for v in range(8):
                x = xs[v]
                mate = jnp.where(low, pltpu.roll(x, size - far, axis), pltpu.roll(x, far, axis))
                rising = bit(k, v)
                if isinstance(rising, bool):
                    least = low if rising else jnp.logical_not(low)
                else:
                    least = low == rising
                out[v] = jnp.where(least, jnp.minimum(x, mate), jnp.maximum(x, mate))
        xs = out
    return xs


def layer_kernel(
    n_patch,
    sender, receiver, wanted, bias, feats, cot, send_w_in, recv_w_in, out_w_in,
    updated, grad_nodes, plane_all, bias_out,
    table, cots, send_w, recv_w, out_w, asked, asked_z, coarse, packed,
    lists, picks, keys, turned, plan_v, plan, cols_s, cols_r, rows_k, pairs_k,
    send_s, pair_s, gsum, pre_s, gat_s, items, act_a, act_b, acc, dtab,
    far_s, rim_s, mix, mix_r, back, back_s, back_r,
    wire_a, wire_b, wire_ar, wire_br, far_r, rim_r,
    zfar_s, zfar_r, zsum_s, zsum_r, zall, plane_s, zsum_bs, zsum_br, plane_bs, updated_v, nodes_v,
    loc, zs_s, zs_r, ls_s, ls_r, ps_s, ps_r, pass_s, pass_r, hs_s, hs_r, os_s, os_r,
    wa_s, wa_r, wb_s, wb_r, fb_s, fb_r, hb_s, hb_r, zf_s, zf_r, zw_s, zw_r, za_s, za_r, pa_s, pa_r, pb_s, pb_r, zx_s, zx_r,
):
    planes = n_patch // RING
    table_rows = NEAR + n_patch * QUOTA
    tiles = pl.cdiv(table_rows, TILE)
    padded = tiles * TILE
    n_items = pl.cdiv(BLOCKS + tiles - 1, UNROLL) * UNROLL
    own = slice(HALO, HALO + ROWS)
    me = lax.axis_index("patch")
    feat = lax.axis_index("feat")
    other = 1 - feat
    xy, z = lax.div(me, RING), lax.rem(me, RING)
    up = lax.rem(me + 1, n_patch)
    below = lax.rem(me + n_patch - 1, n_patch)

    def ring_peer(d):
        return xy * RING + lax.rem(z + d, RING)

    def plane_at(d):
        return lax.rem(xy + d, planes)

    def plane_from(d):
        return lax.rem(xy + planes - d, planes)

    def arrived(at, send, recv):
        remote(at, at, send, recv, me, other).wait_recv()

    def departed(at, send, recv):
        remote(at, at, send, recv, me, other).wait_send()

    others, around = planes - 1, RING - 1

    own_rows = table.at[feat, HALO : HALO + ROWS]
    local = [
        pltpu.make_async_copy(feats.at[0:COARSE], coarse.at[0, 0:COARSE], loc.at[0]),
        pltpu.make_async_copy(feats, own_rows, loc.at[1]),
        pltpu.make_async_copy(cot, cots.at[feat], loc.at[2]),
        pltpu.make_async_copy(send_w_in, send_w, loc.at[3]),
        pltpu.make_async_copy(recv_w_in, recv_w, loc.at[4]),
        pltpu.make_async_copy(out_w_in, out_w, loc.at[5]),
    ]
    for copy in local:
        copy.start()

    barrier = pltpu.get_barrier_semaphore()

    def greet(patch, core):
        pl.semaphore_signal(barrier, inc=1, device_id=(patch, core), device_id_type=MESH)

    loop(1, RING, lambda d: greet(ring_peer(d), feat))
    loop(1, planes, lambda d: greet(plane_at(d) * RING + z, feat))
    greet(up, feat)
    greet(below, feat)
    greet(me, other)

    grid = wanted[...]
    lane_q = lax.broadcasted_iota(I32, (QUOTA, 128), 1)
    for p in range(planes):
        first = pltpu.roll(grid, (128 - RING * p) % 128, 1) if p else grid
        lists[p * QUOTA : (p + 1) * QUOTA, :] = jnp.where(lane_q < RING, first, pltpu.roll(first, RING, 1))
    pl.semaphore_wait(barrier, planes - 1 + RING - 1 + 3)

    def coarse_copy(d):
        return remote(feats.at[0:COARSE], coarse.at[RING - d, 0:COARSE], zs_s.at[0], zs_r.at[min(d, RING - d, 3) - 1], ring_peer(d), feat)

    def list_copy(d):
        to = plane_at(d)
        return remote(lists.at[rows_of(to, QUOTA)], asked.at[rows_of(xy, QUOTA)], ls_s.at[0], ls_r.at[0], to * RING + z, feat)

    def far_rows(p, low=0, high=RING):
        return table.at[feat, pl.ds(pl.multiple_of(NEAR + p * PER + low * QUOTA, QUOTA), (high - low) * QUOTA)]

    def plane_copy(g, d):
        low, high = GROUPS[g]
        to = plane_at(d)
        return remote(
            packed.at[to, low * QUOTA : high * QUOTA], far_rows(xy, low, high), ps_s.at[g], ps_r.at[g], to * RING + z, feat
        )

    def swap(ref, slot):
        return remote(ref, ref, os_s.at[slot], os_r.at[slot], me, other)

    loop(1, planes, lambda d: list_copy(d).start())
    for d in ORDER[1:]:
        coarse_copy(d).start()
    low_rim = table.at[feat, 0:HALO]
    high_rim = table.at[feat, HALO + ROWS : NEAR]
    to_up = remote(feats.at[ROWS - HALO : ROWS], low_rim, hs_s.at[0], hs_r.at[0], up, feat)
    to_below = remote(feats.at[0:HALO], high_rim, hs_s.at[1], hs_r.at[1], below, feat)
    to_up.start()
    to_below.start()
    swap_own = remote(feats, own_rows, os_s.at[0], os_r.at[0], me, other)
    swap_cot = remote(cot, cots.at[feat], os_s.at[1], os_r.at[1], me, other)
    swap_own.start()
    swap_cot.start()

    lane32 = lax.broadcasted_iota(I32, (planes * QUOTA, HALO), 1)
    for k in range(RING):
        coarse[k, COARSE:HALO] = jnp.zeros((HALO - COARSE, HALF), BF16)

    def pack(g):
        for at in range(*GROUPS[g]):
            k = ORDER[at]
            pick = hot32(asked_z[:, k : k + 1] == lane32)
            rows = mm(pick, coarse[k]).astype(BF16)
            packed[:, at * QUOTA : (at + 1) * QUOTA, :] = rows.reshape(planes, QUOTA, HALF)
        loop(1, planes, lambda d: plane_copy(g, d).start())

    s = sender[...]
    j = s - NEAR
    away = jnp.bitwise_and(jnp.right_shift(j, 4) - z, RING - 1)
    spot = jnp.where(away <= 4, jnp.maximum(2 * away - 1, 0), 2 * RING - 2 * away)
    row = NEAR + j - jnp.bitwise_and(j, PER - 1) + spot * QUOTA + jnp.bitwise_and(j, QUOTA - 1)
    word = jnp.where(s < NEAR, s, row) * 1024 + receiver[...]
    xs = [word[8 * v : 8 * v + 8] for v in range(8)]

    xs = bitonic(xs, sort_steps(1, 13))
    for v in range(8):
        keys[8 * v : 8 * v + 8, :] = xs[v]
    asked[rows_of(xy, QUOTA), :] = lists[rows_of(xy, QUOTA), :]
    arrived(asked.at[0 : others * QUOTA], ls_s.at[0], ls_r.at[0])
    asked_z[...] = pltpu.roll(asked[...], lax.rem(128 - z, 128), 1)
    local[0].wait()
    pack(0)
    arrived(coarse.at[1:3, 0:COARSE], zs_s.at[0], zs_r.at[0])
    pack(1)
    arrived(coarse.at[1:3, 0:COARSE], zs_s.at[0], zs_r.at[1])
    pack(2)
    flat = keys[...]
    turned[...] = jnp.transpose(jnp.concatenate([flat, flat], axis=0))
    lane64 = lax.broadcasted_iota(I32, (PAIRS, 128), 1)
    rows_k[...] = jnp.where(
        lane64 < 64, turned[pl.ds(0, PAIRS, stride=2), :], turned[pl.ds(1, PAIRS, stride=2), :]
    )
    for r in range(128):
        spread = jnp.broadcast_to(flat[:, r : r + 1], (64, 128))
        rows = slice(64 * (r % 4), 64 * (r % 4) + 64)
        cols_s[r // 4, rows, :] = jnp.right_shift(spread, 10).astype(I16)
        cols_r[r // 4, rows, :] = jnp.bitwise_and(spread, 1023).astype(I16)
    for b in range(BLOCKS):
        pairs_k[b] = jnp.concatenate([rows_k[2 * b : 2 * b + 2, :], jnp.zeros((6, 128), I32)], axis=0)

    tall = lax.broadcasted_iota(I32, (128, 128), 0)
    wide = lax.broadcasted_iota(I32, (128, 128), 1)
    heads = jnp.logical_and(jnp.bitwise_and(tall, 3) == 0, tall > 0)
    first_tile = jnp.right_shift(jnp.broadcast_to(turned[:, 0:1], (128, 128)), 18)
    first_item = first_tile + jnp.right_shift(tall, 2)
    block_of = jnp.sum(jnp.where(jnp.logical_and(heads, first_item <= wide), 1, 0), axis=0, keepdims=True)
    last_of = jnp.sum(jnp.where(jnp.logical_and(heads, first_tile <= wide), 1, 0), axis=0, keepdims=True) + wide[0:1]
    first_of = jnp.right_shift(flat[0:1], 18) + jnp.right_shift(wide[0:1], 2)
    plan_v[...] = jnp.concatenate([block_of, last_of, first_of, jnp.zeros((5, 128), I32)], axis=0)
    to_scalars = pltpu.make_async_copy(plan_v, plan, loc.at[8])
    to_scalars.start()
    asked_t = jnp.transpose(asked_z[...])
    tall_c = lax.broadcasted_iota(I32, (COARSE, planes * QUOTA), 0)
    for k in range(RING):
        picks[k] = hot32(asked_t[k : k + 1, :] == tall_c)

    arrived(coarse.at[3:6, 0:COARSE], zs_s.at[0], zs_r.at[2])
    pack(3)
    own_far = pltpu.make_async_copy(packed.at[xy], far_rows(xy), loc.at[7])
    own_far.start()
    swap_far = remote(packed.at[xy], far_rows(xy), pass_s.at[2], pass_r.at[2], me, other)
    swap_far.start()
    to_scalars.wait()

    for copy in local[1:]:
        copy.wait()
    swap_own.wait()
    swap_cot.wait()
    pair_s[:, 0:HALF] = (
        mm(table[0, own, :], recv_w[0:HALF, :]) + mm(table[1, own, :], recv_w[HALF:, :]) + bias[...]
    ).astype(BF16)
    grad_sum = mm(cots[0], out_w[:, 0:HALF], NT) + mm(cots[1], out_w[:, HALF:], NT)
    gsum[...] = grad_sum
    pair_s[:, HALF:] = grad_sum.astype(BF16)
    acc[...] = jnp.zeros_like(acc)
    lane = lax.broadcasted_iota(I32, (BLOCK, 128), 1).astype(I16)
    sub = lax.broadcasted_iota(I32, (ROWS, 128), 0).astype(I16)
    sub_t = lax.broadcasted_iota(I32, (TILE, 128), 0).astype(I16)

    def receive(i):
        for u in range(4):
            b = 4 * i + u
            col = cols_r[b]
            pick = jnp.concatenate([hot(col == lane + I16(128 * m)) for m in range(ROWS // 128)], axis=1)
            both = mm(pick, pair_s[...])
            pre_s[b] = both[:, 0:HALF]
            gat_s[b] = both[:, HALF:].astype(BF16)

    loop(0, BLOCKS // 8, receive)

    def pass_on(p, half):
        low, high = HALVES[half]
        return remote(far_rows(p, low, high), far_rows(p, low, high), pass_s.at[half], pass_r.at[half], me, other)

    def all_far(core, low, high):
        return table.at[core, NEAR : NEAR + others * (high - low) * QUOTA]

    to_up.wait()
    swap(low_rim, 2).start()
    to_below.wait()
    swap(high_rim, 3).start()
    for g in range(3):
        arrived(all_far(feat, *GROUPS[g]), ps_s.at[g], ps_r.at[g])
    loop(1, planes, lambda d: pass_on(plane_from(d), 0).start())
    loop(BLOCKS // 8, BLOCKS // 4, receive)
    arrived(all_far(feat, *GROUPS[3]), ps_s.at[3], ps_r.at[3])
    loop(1, planes, lambda d: pass_on(plane_from(d), 1).start())

    def project(start, size):
        part = slice(start, start + size)
        value = (mm(table[0, part, :], send_w[0:HALF, :]) + mm(table[1, part, :], send_w[HALF:, :])).astype(BF16)
        at = 0
        while at < size:
            t, r = divmod(start + at, TILE)
            count = min(TILE - r, size - at)
            send_s[t, r : r + count, :] = value[at : at + count]
            at += count

    swap(low_rim, 2).wait()
    swap(high_rim, 3).wait()
    project(0, NEAR)
    if padded > table_rows:
        send_s[tiles - 1, table_rows - padded + TILE :, :] = jnp.zeros((padded - table_rows, HALF), BF16)
    send_s[tiles] = jnp.zeros((TILE, HALF), BF16)
    own_far.wait()
    swap_far.wait()
    for half in range(2):
        departed(all_far(feat, *HALVES[half]), pass_s.at[half], pass_r.at[half])
        arrived(all_far(other, *HALVES[half]), pass_s.at[half], pass_r.at[half])
    for start in range(NEAR, table_rows, 1024):
        project(start, min(1024, table_rows - start))

    def gather(i):
        for u in range(UNROLL):
            at = i * UNROLL + u
            b = plan[0, at]
            before = plan[0, jnp.maximum(at - 1, 0)]
            t = at - b
            col = cols_s[b] - jnp.full((BLOCK, 128), t * TILE, I32).astype(I16)
            pick = jnp.concatenate([hot(col == lane), hot(col == lane + I16(128))], axis=1)
            part = mm(pick, send_s[t])
            keep = 1.0 - (b - before).astype(F32)
            items[at] = part + keep * items[jnp.maximum(at - 1, 0)]

    items[0] = jnp.zeros((BLOCK, HALF), F32)
    loop(0, n_items // UNROLL, gather)

    def messages(i, act):
        for u in range(SPAN // BLOCK):
            b = i * (SPAN // BLOCK) + u
            last = jnp.where(b == BLOCKS - 1, BLOCKS + tiles - 1, plan[2, jnp.minimum(4 * b + 4, 127)]) - 1
            pre = pre_s[b] + items[last]
            sig = 0.5 * jnp.tanh(0.5 * pre) + 0.5
            hidden = pre * sig
            slope = sig + hidden * (1.0 - sig)
            act[u * BLOCK : (u + 1) * BLOCK, 0:HALF] = hidden.astype(BF16)
            act[u * BLOCK : (u + 1) * BLOCK, HALF:] = slope.astype(BF16)
            gat_s[b] = (gat_s[b].astype(F32) * slope).astype(BF16)

    def collect(i, act):
        words = jnp.bitwise_and(rows_k[rows_of(i, SPAN // 128), :], 1023)
        spread = jnp.concatenate([hot(sub == down(words[m : m + 1], ROWS)) for m in range(SPAN // 128)], axis=1)
        acc[...] += mm(spread, act[...])

    act_b[...] = jnp.zeros_like(act_b)

    def two_spans(i):
        messages(2 * i, act_a)
        collect(jnp.maximum(2 * i - 1, 0), act_b)
        messages(2 * i + 1, act_b)
        collect(2 * i, act_a)

    loop(0, EDGES // SPAN // 2, two_spans)
    collect(EDGES // SPAN - 1, act_b)

    edge_sum = acc[:, 0:HALF].astype(BF16)
    recv_grad = gsum[...] * acc[:, HALF:]
    bias_part = jnp.sum(recv_grad, axis=0, keepdims=True)
    recv_grad_b = recv_grad.astype(BF16)

    chunk_a, chunk_b = 2048 // planes, 1024 // planes

    def put(wire, chunk, start, value):
        value = value.astype(BF16)
        for m in range(value.shape[1] // 128):
            at = 0
            while at < value.shape[0]:
                c, r = divmod(start + m * value.shape[0] + at, chunk)
                count = min(chunk - r, value.shape[0] - at)
                wire[c, r : r + count, :] = value[at : at + count, m * 128 : (m + 1) * 128]
                at += count

    put(
        wire_a, chunk_a, 0,
        jnp.concatenate([mm(table[0, own, :], recv_grad_b, TN), mm(table[1, own, :], recv_grad_b, TN)], axis=0),
    )
    put(wire_a, chunk_a, 1024, jnp.concatenate([mm(edge_sum, cots[0], TN), mm(edge_sum, cots[1], TN)], axis=1))
    sub16 = lax.broadcasted_iota(I32, (16, 128), 0)
    tail = jnp.where(sub16 == 0, bias_part[:, 0:128], jnp.where(sub16 == 1, bias_part[:, 128:], 0.0)).astype(BF16)
    for c in range(planes):
        wire_a[c, chunk_a : chunk_a + 16, :] = tail

    def wire_copy(src, dst, send, recv, d):
        to = plane_at(d)
        return remote(src.at[to], dst.at[xy], send.at[0], recv.at[0], to * RING + z, feat)

    loop(1, planes, lambda d: wire_copy(wire_a, wire_ar, wa_s, wa_r, d).start())
    wire_ar[xy] = wire_a[xy]

    def scatter(i):
        for u in range(UNROLL):
            at = i * UNROLL + u
            b = plan[0, at]
            before = plan[0, jnp.maximum(at - 1, 0)]
            t = at - b
            words = jnp.right_shift(pairs_k[b], 10) - t * TILE
            spread = jnp.concatenate([hot(sub_t == down(words[0:1], TILE)), hot(sub_t == down(words[1:2], TILE))], axis=1)
            part = mm(spread, gat_s[b])
            keep = (b - before).astype(F32)
            items[at] = part + keep * items[jnp.maximum(at - 1, 0)]

    items[0] = jnp.zeros((BLOCK, HALF), F32)
    loop(0, n_items // UNROLL, scatter)
    for t in range(tiles):
        dtab[t * TILE : (t + 1) * TILE, :] = items[plan[1, t]]

    dtab_b = dtab[0:table_rows, :].astype(BF16)
    put(wire_b, chunk_b, 0, jnp.concatenate([mm(table[0], dtab_b, TN), mm(table[1], dtab_b, TN)], axis=0))
    loop(1, planes, lambda d: wire_copy(wire_b, wire_br, wb_s, wb_r, d).start())
    wire_br[xy] = wire_b[xy]
    rim_s[0] = dtab_b[0:HALO]
    rim_s[1] = dtab_b[HALO + ROWS : NEAR]
    far_s[...] = dtab_b[NEAR:table_rows]
    back_below = remote(rim_s.at[0], rim_r.at[1], hb_s.at[0], hb_r.at[0], below, feat)
    back_up = remote(rim_s.at[1], rim_r.at[0], hb_s.at[1], hb_r.at[1], up, feat)
    back_below.start()
    back_up.start()

    def far_copy(g, d):
        low, high = GROUPS[g]
        to = plane_at(d)
        src = far_s.at[pl.ds(pl.multiple_of(to * PER + low * QUOTA, QUOTA), (high - low) * QUOTA)]
        return remote(src, far_r.at[xy, low * QUOTA : high * QUOTA], fb_s.at[g], fb_r.at[g], to * RING + z, feat)

    loop(1, planes, lambda d: far_copy(3, d).start())
    far_r[xy] = far_s[rows_of(xy, PER), :]
    mixed = mm(edge_sum, out_w[...])
    mix[0] = mixed[:, 0:HALF]
    mix[1] = mixed[:, HALF:]
    swap_mix = remote(mix.at[other], mix_r, os_s.at[4], os_r.at[4], me, other)
    swap_mix.start()
    back[...] = mm(recv_grad_b, recv_w[...], NT)
    swap_mix.wait()
    updated_v[...] = (table[feat, own, :].astype(F32) + mix[feat] + mix_r[...]).astype(BF16)
    keep_updated = pltpu.make_async_copy(updated_v, updated, loc.at[6])
    keep_updated.start()

    part = chunk_a // RING
    arrived(wire_ar.at[0:others], wa_s.at[0], wa_r.at[0])
    total = wire_ar[0].astype(F32)
    for p in range(1, planes):
        total = total + wire_ar[p].astype(F32)
    for k in range(RING):
        zsum_s[k, 0:part, :] = total[k * part : (k + 1) * part, :]
        zsum_s[k, part : part + 8, :] = total[chunk_a : chunk_a + 8, :]

    def zsum_copy(d):
        to = lax.rem(z + d, RING)
        return remote(zsum_s.at[to], zsum_r.at[z], zw_s.at[0], zw_r.at[0], ring_peer(d), feat)

    loop(1, RING, lambda d: zsum_copy(d).start())
    zsum_r[z] = zsum_s[z]

    arrived(zsum_r.at[0:around], zw_s.at[0], zw_r.at[0])
    whole = zsum_r[0]
    for k in range(1, RING):
        whole = whole + zsum_r[k]
    bias_out[...] = jnp.concatenate([whole[part : part + 1], whole[part + 1 : part + 2]], axis=1)
    zall[z] = whole[0:part]

    def zall_copy(d):
        return remote(zall.at[z], zall.at[z], za_s.at[0], za_r.at[0], ring_peer(d), feat)

    loop(1, RING, lambda d: zall_copy(d).start())

    arrived(wire_br.at[0:others], wb_s.at[0], wb_r.at[0])
    total = wire_br[0].astype(F32)
    for p in range(1, planes):
        total = total + wire_br[p].astype(F32)
    zsum_bs[...] = total.astype(BF16)

    def zsum_b_copy(d):
        return remote(zsum_bs, zsum_br.at[z], zx_s.at[0], zx_r.at[0], ring_peer(d), feat)

    loop(1, RING, lambda d: zsum_b_copy(d).start())
    zsum_br[z] = zsum_bs[...]
    for g in (2, 1, 0):
        loop(1, planes, lambda d: far_copy(g, d).start())

    arrived(zall.at[0:around], za_s.at[0], za_r.at[0])
    plane_s[...] = zall[...].reshape(chunk_a, 128).astype(BF16)

    def all_copy(d):
        return remote(
            plane_s, plane_all.at[xy, 0:chunk_a], pa_s.at[0], pa_r.at[0], plane_at(d) * RING + z, feat
        )

    loop(1, planes, lambda d: all_copy(d).start())
    keep_plane = pltpu.make_async_copy(plane_s, plane_all.at[xy, 0:chunk_a], loc.at[7])
    keep_plane.start()

    arrived(zsum_br.at[0:around], zx_s.at[0], zx_r.at[0])
    whole = zsum_br[0].astype(F32)
    for k in range(1, RING):
        whole = whole + zsum_br[k].astype(F32)
    plane_bs[...] = whole.astype(BF16)

    def all_b_copy(d):
        return remote(
            plane_bs, plane_all.at[xy, chunk_a : chunk_a + chunk_b], pb_s.at[0], pb_r.at[0], plane_at(d) * RING + z, feat
        )

    loop(1, planes, lambda d: all_b_copy(d).start())
    keep_plane_b = pltpu.make_async_copy(plane_bs, plane_all.at[xy, chunk_a : chunk_a + chunk_b], loc.at[8])
    keep_plane_b.start()

    back_below.wait()
    back_up.wait()
    rest = dtab[HALO + COARSE : 2 * HALO, :] + rim_r[0, COARSE:HALO, :].astype(F32)
    end = dtab[ROWS : ROWS + HALO, :] + rim_r[1].astype(F32)
    send_grad = jnp.concatenate([rest, dtab[2 * HALO : ROWS, :], end], axis=0).astype(BF16)
    terms = back[COARSE:, :] + mm(send_grad, send_w[...], NT)
    back_s[0, COARSE:] = terms[:, 0:HALF]
    back_s[1, COARSE:] = terms[:, HALF:]
    swap_back = remote(back_s.at[other, COARSE:ROWS], back_r.at[COARSE:ROWS], os_s.at[5], os_r.at[5], me, other)
    swap_back.start()

    def sum_owners(g):
        low, high = GROUPS[g]
        arrived(far_r.at[0:others, low * QUOTA : high * QUOTA], fb_s.at[g], fb_r.at[g])
        for at in range(low, high):
            k = ORDER[at]
            rows = far_r[:, at * QUOTA : (at + 1) * QUOTA, :].reshape(planes * QUOTA, HALF)
            zfar_s[k] = mm(picks[k], rows).astype(BF16)
            if k:
                zfar_copy(k).start()

    def zfar_copy(d):
        return remote(zfar_s.at[d], zfar_r.at[d], zf_s.at[0], zf_r.at[0], ring_peer(d), feat)

    sum_owners(3)
    sum_owners(2)
    sum_owners(1)
    sum_owners(0)
    zfar_r[0] = zfar_s[0]
    arrived(zfar_r.at[0:around], zf_s.at[0], zf_r.at[0])
    head = zfar_r[0].astype(F32)
    for k in range(1, RING):
        head = head + zfar_r[k].astype(F32)
    head = head + dtab[HALO : HALO + COARSE, :] + rim_r[0, 0:COARSE, :].astype(F32)
    terms = back[0:COARSE, :] + mm(head.astype(BF16), send_w[...], NT)
    back_s[0, 0:COARSE] = terms[:, 0:HALF]
    back_s[1, 0:COARSE] = terms[:, HALF:]
    swap_head = remote(back_s.at[other, 0:COARSE], back_r.at[0:COARSE], os_s.at[6], os_r.at[6], me, other)
    swap_head.start()
    swap_back.wait()
    nodes_v[COARSE:, :] = (cots[feat, COARSE:, :].astype(F32) + back_s[feat, COARSE:] + back_r[COARSE:, :]).astype(BF16)
    keep_rest = pltpu.make_async_copy(nodes_v.at[COARSE:ROWS], grad_nodes.at[COARSE:ROWS], loc.at[1])
    keep_rest.start()
    swap_head.wait()
    nodes_v[0:COARSE, :] = (cots[feat, 0:COARSE, :].astype(F32) + back_s[feat, 0:COARSE] + back_r[0:COARSE, :]).astype(BF16)
    keep_nodes = pltpu.make_async_copy(nodes_v.at[0:COARSE], grad_nodes.at[0:COARSE], loc.at[0])
    keep_nodes.start()

    arrived(plane_all.at[0:others, 0:chunk_a], pa_s.at[0], pa_r.at[0])
    arrived(plane_all.at[0:others, chunk_a : chunk_a + chunk_b], pb_s.at[0], pb_r.at[0])
    keep_updated.wait()
    keep_nodes.wait()
    keep_rest.wait()
    keep_plane.wait()
    keep_plane_b.wait()

    departed(lists.at[0 : others * QUOTA], ls_s.at[0], ls_r.at[0])
    departed(coarse.at[1:RING, 0:COARSE], zs_s.at[0], zs_r.at[0])
    for g, (low, high) in enumerate(GROUPS):
        departed(all_far(feat, low, high), ps_s.at[g], ps_r.at[g])
    departed(wire_a.at[0:others], wa_s.at[0], wa_r.at[0])
    departed(wire_b.at[0:others], wb_s.at[0], wb_r.at[0])
    for g, (low, high) in enumerate(GROUPS):
        departed(far_r.at[0:others, low * QUOTA : high * QUOTA], fb_s.at[g], fb_r.at[g])
    departed(plane_all.at[0:others, chunk_a : chunk_a + chunk_b], pb_s.at[0], pb_r.at[0])
    departed(zsum_br.at[0:around], zx_s.at[0], zx_r.at[0])
    departed(plane_all.at[0:others, 0:chunk_a], pa_s.at[0], pa_r.at[0])
    departed(zsum_s.at[0:around], zw_s.at[0], zw_r.at[0])
    departed(zall.at[0:around], za_s.at[0], za_r.at[0])
    departed(zfar_s.at[0:around], zf_s.at[0], zf_r.at[0])


def layer(n_patch, *args):
    planes = n_patch // RING
    table_rows = NEAR + n_patch * QUOTA
    tiles = pl.cdiv(table_rows, TILE)
    padded = tiles * TILE
    n_items = pl.cdiv(BLOCKS + tiles - 1, UNROLL) * UNROLL
    chunk_a, chunk_b = 2048 // planes, 1024 // planes
    part = chunk_a // RING
    vmem = pl.BlockSpec(memory_space=pltpu.VMEM)
    hbm = pl.BlockSpec(memory_space=pltpu.HBM)
    dma = pltpu.SemaphoreType.DMA

    def both(*shape):
        return [dma(shape), dma(shape)]

    return pl.pallas_call(
        functools.partial(layer_kernel, n_patch),
        out_shape=(
            jax.ShapeDtypeStruct((ROWS, HALF), BF16),
            jax.ShapeDtypeStruct((ROWS, HALF), BF16),
            jax.ShapeDtypeStruct((planes, chunk_a + chunk_b, 128), BF16),
            jax.ShapeDtypeStruct((1, HALF), F32),
        ),
        in_specs=[vmem] * 4 + [hbm] * 5,
        out_specs=(hbm,) * 3 + (vmem,),
        scratch_shapes=[
            pltpu.VMEM((2, table_rows, HALF), BF16),
            pltpu.VMEM((2, ROWS, HALF), BF16),
            pltpu.VMEM((2 * HALF, HALF), BF16),
            pltpu.VMEM((2 * HALF, HALF), BF16),
            pltpu.VMEM((HALF, 2 * HALF), BF16),
            pltpu.VMEM((planes * QUOTA, 128), I32),
            pltpu.VMEM((planes * QUOTA, 128), I32),
            pltpu.VMEM((RING, HALO, HALF), BF16),
            pltpu.VMEM((planes, PER, HALF), BF16),
            pltpu.VMEM((planes * QUOTA, 128), I32),
            pltpu.VMEM((RING, COARSE, planes * QUOTA), BF16),
            pltpu.VMEM((PAIRS, 128), I32),
            pltpu.VMEM((128, 128), I32),
            pltpu.VMEM((8, 128), I32),
            pltpu.SMEM((8, 128), I32),
            pltpu.VMEM((BLOCKS, BLOCK, 128), I16),
            pltpu.VMEM((BLOCKS, BLOCK, 128), I16),
            pltpu.VMEM((PAIRS, 128), I32),
            pltpu.VMEM((BLOCKS, 8, 128), I32),
            pltpu.VMEM((tiles + 1, TILE, HALF), BF16),
            pltpu.VMEM((ROWS, 2 * HALF), BF16),
            pltpu.VMEM((ROWS, HALF), F32),
            pltpu.VMEM((BLOCKS, BLOCK, HALF), F32),
            pltpu.VMEM((BLOCKS, BLOCK, HALF), BF16),
            pltpu.VMEM((n_items, BLOCK, HALF), F32),
            pltpu.VMEM((SPAN, 2 * HALF), BF16),
            pltpu.VMEM((SPAN, 2 * HALF), BF16),
            pltpu.VMEM((ROWS, 2 * HALF), F32),
            pltpu.VMEM((padded, HALF), F32),
            pltpu.VMEM((n_patch * QUOTA, HALF), BF16),
            pltpu.VMEM((2, HALO, HALF), BF16),
            pltpu.VMEM((2, ROWS, HALF), F32),
            pltpu.VMEM((ROWS, HALF), F32),
            pltpu.VMEM((ROWS, 2 * HALF), F32),
            pltpu.VMEM((2, ROWS, HALF), F32),
            pltpu.VMEM((ROWS, HALF), F32),
            pltpu.VMEM((planes, chunk_a + 16, 128), BF16),
            pltpu.VMEM((planes, chunk_b, 128), BF16),
            pltpu.VMEM((planes, chunk_a + 16, 128), BF16),
            pltpu.VMEM((planes, chunk_b, 128), BF16),
            pltpu.VMEM((planes, PER, HALF), BF16),
            pltpu.VMEM((2, HALO, HALF), BF16),
            pltpu.VMEM((RING, COARSE, HALF), BF16),
            pltpu.VMEM((RING, COARSE, HALF), BF16),
            pltpu.VMEM((RING, part + 8, 128), F32),
            pltpu.VMEM((RING, part + 8, 128), F32),
            pltpu.VMEM((RING, part, 128), F32),
            pltpu.VMEM((chunk_a, 128), BF16),
            pltpu.VMEM((chunk_b, 128), BF16),
            pltpu.VMEM((RING, chunk_b, 128), BF16),
            pltpu.VMEM((chunk_b, 128), BF16),
            pltpu.VMEM((ROWS, HALF), BF16),
            pltpu.VMEM((ROWS, HALF), BF16),
            dma((9,)),
            *both(3), *both(1), *both(4), *both(3), *both(2), *both(7), *both(1), *both(1), *both(4), *both(2), *both(1), *both(1), *both(1), *both(1), *both(1), *both(1),
        ],
        compiler_params=pltpu.CompilerParams(
            collective_id=0, has_side_effects=True, vmem_limit_bytes=60 * 2**20
        ),
        name="layer",
    )(*args)


def finish_kernel(
    chunk_a, updated, grad_nodes, weights, bias,
    updated_o, grad_nodes_o, g_send, g_recv, g_out, g_bias,
    weights_v, sems,
):
    copies = [
        pltpu.make_async_copy(weights, weights_v, sems.at[0]),
        pltpu.make_async_copy(updated, updated_o, sems.at[1]),
        pltpu.make_async_copy(grad_nodes, grad_nodes_o, sems.at[2]),
    ]
    for copy in copies:
        copy.start()
    g_bias[...] = bias[...]
    copies[0].wait()
    a = weights_v[:, 0:chunk_a, :].reshape(2048, 128).astype(F32)
    for m in range(2):
        g_recv[:, 128 * m : 128 * (m + 1)] = a[512 * m : 512 * (m + 1)]
    for m in range(4):
        g_out[:, 128 * m : 128 * (m + 1)] = a[1024 + 256 * m : 1024 + 256 * (m + 1)]
    b = weights_v[:, chunk_a:, :].reshape(1024, 128).astype(F32)
    for m in range(2):
        g_send[:, 128 * m : 128 * (m + 1)] = b[512 * m : 512 * (m + 1)]
    copies[1].wait()
    copies[2].wait()


def finish(*args):
    vmem = pl.BlockSpec(memory_space=pltpu.VMEM)
    hbm = pl.BlockSpec(memory_space=pltpu.HBM)
    return pl.pallas_call(
        functools.partial(finish_kernel, 2048 // args[2].shape[0]),
        out_shape=(
            jax.ShapeDtypeStruct((ROWS, HALF), BF16),
            jax.ShapeDtypeStruct((ROWS, HALF), BF16),
            jax.ShapeDtypeStruct((2 * HALF, HALF), F32),
            jax.ShapeDtypeStruct((2 * HALF, HALF), F32),
            jax.ShapeDtypeStruct((HALF, 2 * HALF), F32),
            jax.ShapeDtypeStruct((1, HALF), F32),
        ),
        in_specs=[hbm] * 3 + [vmem],
        out_specs=(vmem,) * 6,
        scratch_shapes=[
            pltpu.VMEM(args[2].shape, BF16),
            pltpu.SemaphoreType.DMA((3,)),
        ],
        compiler_params=pltpu.CompilerParams(vmem_limit_bytes=62 * 2**20),
        name="finish",
    )(*args)


def shards(n_patch, feats, cot, send_w, recv_w, out_w, bias, sender, receiver, wanted):
    parts = layer(
        n_patch, sender.reshape(PAIRS, 128), receiver.reshape(PAIRS, 128), wanted.reshape(n_patch, QUOTA).T, bias.reshape(1, HALF),
        feats, cot, send_w, recv_w, out_w,
    )
    updated, grad_nodes, g_send, g_recv, g_out, g_bias = finish(*parts)
    return (updated, grad_nodes, g_send, g_recv, g_out, g_bias.reshape(HALF))


def solution(mesh):
    n_patch = mesh.shape["patch"]
    in_specs = (
        P("patch", "feat"),
        P("patch", "feat"),
        P(None, "feat"),
        P(None, "feat"),
        P("feat", None),
        P("feat"),
        P("patch"),
        P("patch"),
        P("patch", None, None),
    )
    out_specs = (
        P("patch", "feat"),
        P("patch", "feat"),
        P(None, "feat"),
        P(None, "feat"),
        P("feat", None),
        P("feat"),
    )
    return jax.shard_map(
        functools.partial(shards, n_patch), mesh=mesh, in_specs=in_specs, out_specs=out_specs, check_vma=False
    )
```
